128 devices in a mesh: side: 2 (over core), dom: 64 (over z, y, x).
Axes of the slice: x: 4, y: 4, z: 4, core: 2. Of those that a mesh axis runs over, the one named last changes fastest.
Arguments:
- features: bfloat16 [2, 16384, 1024], P('side', 'dom'), may hold values from -6 to 6
- live_rows: int32 [2, 64], P('side', 'dom'), may hold values from 128 to 256, as said below
- listed: int32 [2, 64, 8, 2], P('side', 'dom'), may hold values from 0 to 1, as said below
- counts: int32 [2, 16384, 2048], P('side', 'dom'), may hold values from 0 to 3, as said below
- cotangent: bfloat16 [2, 16384, 1024], P('side', 'dom'), may hold values from -6 to 6
- q_weight: bfloat16 [1024, 2048], replicated, may hold values from -0.1875 to 0.1875
- q_bias: float32 [2048], replicated, may hold values from -3 to 3
- self_weight: bfloat16 [1024, 1024], replicated, may hold values from -0.109375 to 0.109375
- nb_weight: bfloat16 [2048, 1024], replicated, may hold values from -0.109375 to 0.109375
- out_bias: float32 [1024], replicated, may hold values from -3 to 3
Outputs:
- embedded: bfloat16 [2, 16384, 1024], P('side', 'dom')
- grad_features: bfloat16 [2, 16384, 1024], P('side', 'dom')
The draws below stay inside these ranges and needn't reach their ends.
Inputs may be any that keep to these rules, and one draw needn't show every extreme that they name: `live_rows`: live rows come first on each device; user devices (group 0) hold one half to three quarters of 256 live rows, item devices three quarters to all. listed[s, j, o, b] is 1 when device (s, j) reads block b of device (1 - s, j - o), positions taken modulo the devices of a group; every block is read by 2 to 4 of the 8 devices that may read it; a device reads at most 1 block of one source, and in every draw some device reads exactly 1 block of some source. `counts`: mostly zero.
All inputs are finite; a program needn't handle non-finite values.
Results may differ from the reference program's by a relative error of at most 0.028.
The reference program's roundings to bfloat16 on the way count: a program that leaves them out, or rounds other values in their place, can miss the bound.
Values may be sent and summed in bfloat16 or wider, within the bound.
No kernel may reach another device: no remote copies, remote signals or barrier semaphores. Data moves between devices by JAX's collectives and lax.ppermute only.
A program may use at most 128 MiB of HBM per device.

```python
import jax
import jax.numpy as jnp
from jax import lax

D = 1024
HIDDEN_SIZE = 2048
ROWS = 256
BLOCK = 128
READ_SPAN = 8
NODES = 16384
N_DOM = 64


def draw_live_rows(key, part):
    first, second = jax.random.split(jax.random.fold_in(key, 11))
    users = jax.random.randint(first, (N_DOM,), ROWS // 2, 3 * ROWS // 4 + 1, dtype=jnp.int32)
    items = jax.random.randint(second, (N_DOM,), 3 * ROWS // 4, ROWS + 1, dtype=jnp.int32)
    users = users.at[0].set(ROWS // 2)
    items = items.at[0].set(ROWS)
    return jnp.stack([users, items])


def draw_listed(key, part):
    block_count = ROWS // BLOCK
    most = (block_count + 1) // 2
    quarter = READ_SPAN // 2
    keys = jax.random.split(jax.random.fold_in(key, 23), 4)
    block_scores = jax.random.randint(keys[0], (2, N_DOM, block_count), 0, 1 << 20, dtype=jnp.int32)
    block_scores = block_scores * block_count + jnp.arange(block_count, dtype=jnp.int32)
    block_rank = jnp.argsort(jnp.argsort(block_scores, axis=-1), axis=-1)
    halves = (block_rank >= most).astype(jnp.int32)
    offset_scores = jax.random.randint(keys[1], (2, N_DOM, READ_SPAN), 0, 1 << 20, dtype=jnp.int32)
    offset_scores = offset_scores * READ_SPAN + jnp.arange(READ_SPAN, dtype=jnp.int32)
    offset_rank = jnp.argsort(jnp.argsort(offset_scores, axis=-1), axis=-1)
    groups = (offset_rank >= quarter).astype(jnp.int32)
    leaders = offset_rank % quarter == 0
    readers = jax.random.randint(keys[2], (2, N_DOM, block_count, 1), 2, quarter + 1, dtype=jnp.int32)
    scores = jax.random.randint(keys[3], (2, N_DOM, block_count, READ_SPAN), 1, 1 << 20, dtype=jnp.int32)
    scores = scores * READ_SPAN + jnp.arange(READ_SPAN, dtype=jnp.int32)
    scores = jnp.where(leaders[:, :, None, :], jnp.arange(READ_SPAN, dtype=jnp.int32), scores)
    matching = groups[:, :, None, :] == halves[:, :, :, None]
    scores = jnp.where(matching, scores, scores + (1 << 24))
    ranking = jnp.argsort(jnp.argsort(scores, axis=-1), axis=-1)
    chosen = (ranking < readers).astype(jnp.int32)
    flipped = chosen[::-1]
    pieces = [jnp.roll(flipped[:, :, :, offset], offset, axis=1) for offset in range(READ_SPAN)]
    return jnp.stack(pieces, axis=2)


def draw_counts(key, part):
    first, second = jax.random.split(jax.random.fold_in(key, 37))
    shape = (2, ROWS * N_DOM, READ_SPAN * ROWS)
    amount = jax.random.randint(first, shape, 1, 4, dtype=jnp.int32)
    present = (jax.random.randint(second, shape, 0, 16, dtype=jnp.int32) == 0).astype(jnp.int32)
    return amount * present


def levels(rng, extent, shards, low, high):
    gain = 1.0
    for axis_at, shards_of in shards:
        steps = jax.random.uniform(jax.random.fold_in(jax.random.fold_in(rng, 6), axis_at), (shards_of,), jnp.float32, low / len(shards), high / len(shards))
        gain = gain * jnp.repeat(jnp.exp(steps), extent[axis_at] // shards_of).reshape((-1,) + (1,) * (len(extent) - 1 - axis_at))
    return gain


def scatter_about(stream_key, extent, deviation, most, cuts=(), kind=jnp.bfloat16):
    result = jax.random.normal(stream_key, extent, jnp.float32) * deviation
    if len(cuts) > 0:
        result = levels(stream_key, extent, cuts, -0.22, 0.18) * result
    return jnp.clip(result, min=-most, max=most).astype(kind)


def setup_inputs(seed: int = 0) -> dict:
    key_list = jax.random.split(jax.random.key(seed), 11)
    features = scatter_about(key_list[0], (2, NODES, D), 1.0, 6.0, ((0, 2), (1, 64)))
    live_rows = draw_live_rows(jax.random.fold_in(key_list[10], 71), 0)
    listed = draw_listed(jax.random.fold_in(key_list[10], 71), 0)
    counts = draw_counts(jax.random.fold_in(key_list[10], 71), 0)
    cotangent = scatter_about(key_list[4], (2, NODES, D), 1.0, 6.0, ((0, 2), (1, 64)))
    q_weight = scatter_about(key_list[5], (D, HIDDEN_SIZE), D ** -0.5, 0.1875)
    q_bias = scatter_about(key_list[6], (HIDDEN_SIZE,), 0.5, 3.0, (), jnp.float32)
    self_weight = scatter_about(key_list[7], (D, D), (D + HIDDEN_SIZE) ** -0.5, 0.109375)
    nb_weight = scatter_about(key_list[8], (HIDDEN_SIZE, D), (D + HIDDEN_SIZE) ** -0.5, 0.109375)
    out_bias = scatter_about(key_list[9], (D,), 0.5, 3.0, (), jnp.float32)
    return {"features": features, "live_rows": live_rows, "listed": listed, "counts": counts, "cotangent": cotangent, "q_weight": q_weight, "q_bias": q_bias, "self_weight": self_weight, "nb_weight": nb_weight, "out_bias": out_bias}


epsilon = 1e-06

def neighbour_rows(features, live_count, q_weight, q_bias):
    row_count = features.shape[0]
    pre_act = jnp.dot(features, q_weight, preferred_element_type=jnp.float32) + q_bias
    keep_rows = (jnp.arange(row_count, dtype=jnp.int32) < live_count)[:, None]
    message = jnp.where(keep_rows, jnp.maximum(pre_act, 0.0), 0.0).astype(jnp.bfloat16)
    return (pre_act, message)

def tile_weights(table, lists, source_live):
    reach, block_count = lists.shape
    row_count = table.shape[0]
    block_rows = row_count // block_count
    listed_cols = jnp.repeat(lists, block_rows, axis=1)
    living = (jnp.arange(row_count, dtype=jnp.int32)[None, :] < source_live[:, None]).astype(jnp.int32)
    chosen = (listed_cols * living).reshape(1, reach * row_count)
    return (table * chosen).astype(jnp.float32).astype(jnp.bfloat16)

def layer_forward(features, live_count, weight_tiles, messages, self_weight, nb_weight, out_bias):
    row_count = features.shape[0]
    degree = 1.0 + lax.optimization_barrier(jnp.sum(weight_tiles.astype(jnp.float32), axis=1, keepdims=True))
    summed = jnp.dot(weight_tiles, messages.reshape(-1, messages.shape[-1]), preferred_element_type=jnp.float32)
    pooled = (summed / degree).astype(jnp.bfloat16)
    pre_act = jnp.dot(features, self_weight, preferred_element_type=jnp.float32)
    pre_act = pre_act + jnp.dot(pooled, nb_weight, preferred_element_type=jnp.float32) + out_bias
    activated = jnp.maximum(pre_act, 0.0)
    inv_norm = lax.rsqrt(lax.optimization_barrier(jnp.mean(activated * activated, axis=1, keepdims=True)) + epsilon)
    keep_rows = (jnp.arange(row_count, dtype=jnp.int32) < live_count)[:, None]
    embedded = jnp.where(keep_rows, activated * inv_norm, 0.0).astype(jnp.bfloat16)
    return (embedded, pre_act, activated, inv_norm, degree, keep_rows)

def layer_backward(cotangent, keep_rows, pre_act, activated, inv_norm, degree, self_weight, nb_weight):
    width = activated.shape[1]
    upstream = jnp.where(keep_rows, cotangent.astype(jnp.float32), 0.0)
    inner = lax.optimization_barrier(jnp.sum(upstream * activated, axis=1, keepdims=True)) / width
    grad_act = inv_norm * upstream - activated * inv_norm * inv_norm * inv_norm * inner
    grad_pre = jnp.where(pre_act > 0, grad_act, 0.0).astype(jnp.bfloat16)
    contract = (((1,), (1,)), ((), ()))
    grad_self = lax.dot_general(grad_pre, self_weight, contract, preferred_element_type=jnp.float32)
    grad_nb = lax.dot_general(grad_pre, nb_weight, contract, preferred_element_type=jnp.float32)
    grad_pooled = (grad_nb / degree).astype(jnp.bfloat16)
    return (grad_self, grad_pooled)

def finish_owner(grad_message, keep_rows, neighbour_pre, grad_self, q_weight):
    grad_neighbour = jnp.where(keep_rows & (neighbour_pre > 0), grad_message, 0.0).astype(jnp.bfloat16)
    contract = (((1,), (1,)), ((), ()))
    total = grad_self + lax.dot_general(grad_neighbour, q_weight, contract, preferred_element_type=jnp.float32)
    return jnp.where(keep_rows, total, 0.0).astype(jnp.bfloat16)

def reference(features, live_rows, listed, counts, cotangent, q_weight, q_bias, self_weight, nb_weight, out_bias):
    device_count = 2 * N_DOM
    row_count = features.shape[1] // N_DOM
    width = features.shape[2]
    hidden = q_weight.shape[1]
    reach = listed.shape[2]
    block_rows = row_count // listed.shape[3]
    own_rows = features.reshape(device_count, row_count, width)
    lives = live_rows.reshape(device_count)
    lists = listed.reshape(device_count, reach, listed.shape[3])
    tables = counts.reshape(device_count, row_count, reach * row_count)
    upstream = cotangent.reshape(device_count, row_count, width)
    offsets = jnp.arange(reach, dtype=jnp.int32)
    messages = lax.map(lambda pair: neighbour_rows(pair[0], pair[1], q_weight, q_bias)[1], (own_rows, lives))

    def reader_pass(device):
        group_index = device // N_DOM
        position = device % N_DOM
        source_ids = ((1 - group_index) * N_DOM + (position - offsets) % N_DOM).astype(jnp.int32)
        weight_tiles = tile_weights(tables[device], lists[device], lives[source_ids])
        outcome = layer_forward(own_rows[device], lives[device], weight_tiles, messages[source_ids], self_weight, nb_weight, out_bias)
        embedded, pre_act, activated, inv_norm, degree, keep_rows = outcome
        grad_self, grad_pooled = layer_backward(upstream[device], keep_rows, pre_act, activated, inv_norm, degree, self_weight, nb_weight)
        return (embedded, grad_self, grad_pooled)
    embedded, grad_self, grad_pooled = lax.map(reader_pass, jnp.arange(device_count, dtype=jnp.int32))

    def owner_pass(device):
        group_index = device // N_DOM
        position = device % N_DOM
        own_live = lives[device]
        living = (jnp.arange(row_count, dtype=jnp.int32) < own_live).astype(jnp.int32)
        grad_message = jnp.zeros((row_count, hidden), jnp.float32)
        for offset in range(reach):
            reader = ((1 - group_index) * N_DOM + (position + offset) % N_DOM).astype(jnp.int32)
            listed_cols = jnp.repeat(lists[reader][offset], block_rows)
            column = lax.dynamic_slice_in_dim(tables[reader], offset * row_count, row_count, 1)
            tile = (column * (listed_cols * living)[None, :]).astype(jnp.float32).astype(jnp.bfloat16)
            grad_message = grad_message + lax.dot_general(tile, grad_pooled[reader], (((0,), (0,)), ((), ())), preferred_element_type=jnp.float32)
        neighbour_pre = neighbour_rows(own_rows[device], own_live, q_weight, q_bias)[0]
        keep_rows = (jnp.arange(row_count, dtype=jnp.int32) < own_live)[:, None]
        return finish_owner(grad_message, keep_rows, neighbour_pre, grad_self[device], q_weight)
    grads = lax.map(owner_pass, jnp.arange(device_count, dtype=jnp.int32))
    return (embedded.reshape(2, -1, width), grads.reshape(2, -1, width))
```

```python
import jax
import jax.numpy as jnp
from jax import lax
from jax.experimental import pallas as pl
from jax.experimental.pallas import tpu as pltpu
from jax.sharding import PartitionSpec as P

EPS = 1e-06
DEAD = 16384.0
LIMIT = 8192.0
F32 = jnp.float32
BF16 = jnp.bfloat16
VMEM = pl.BlockSpec(memory_space=pltpu.VMEM)
SMEM = pl.BlockSpec(memory_space=pltpu.SMEM)


def dot(a, b, ca=1, cb=0):
    return lax.dot_general(a, b, (((ca,), (cb,)), ((), ())), preferred_element_type=F32)


def call(kernel, outs, ins, in_specs=None, scratch=(), limit=24, flops=0):
    return pl.pallas_call(
        kernel,
        out_shape=[jax.ShapeDtypeStruct(s, d) for s, d in outs],
        in_specs=in_specs or [VMEM] * len(ins),
        out_specs=[VMEM] * len(outs),
        scratch_shapes=list(scratch),
        compiler_params=pltpu.CompilerParams(vmem_limit_bytes=limit << 20),
        cost_estimate=pl.CostEstimate(flops=flops, bytes_accessed=1 << 20, transcendentals=0),
    )(*ins)


def route(x, shift):
    count = lax.axis_size("dom")
    pairs = [
        (s * count + j, (1 - s) * count + (j + shift) % count)
        for s in range(2)
        for j in range(count)
    ]
    return lax.ppermute(x, ("side", "dom"), pairs)


def pick_kernel(block, live_ref, wanted_ref, x_ref, *outs):
    live = live_ref[0]
    for o, out in enumerate(outs):
        start = wanted_ref[o] * block
        row = lax.broadcasted_iota(jnp.int32, (block, 1), 0) + start
        x = x_ref[pl.ds(pl.multiple_of(start, block), block), :].astype(F32)
        out[...] = jnp.where(row < live, x, DEAD).astype(BF16)


def tiles_kernel(block, lists_ref, counts_ref, x_ref, sw_ref, tiles_ref, tiles_t_ref, self_ref):
    reach = tiles_ref.shape[1] // block
    for o in range(reach):
        first = counts_ref[:, o * 2 * block : (o * 2 + 1) * block]
        second = counts_ref[:, (o * 2 + 1) * block : (o * 2 + 2) * block]
        tile = (first * lists_ref[o, 0] + second * lists_ref[o, 1]).astype(F32)
        tiles_ref[:, o * block : (o + 1) * block] = tile.astype(BF16)
        tiles_t_ref[o * block : (o + 1) * block, :] = tile.T.astype(BF16)
    self_ref[...] = dot(x_ref[...], sw_ref[...])


def message_kernel(block, first, last, *refs):
    size = len(range(first, last))
    blocks = refs[:size]
    q_ref, qb_ref, tiles_ref, acc_in, deg_in, msg_ref, acc_ref, deg_ref = refs[size:]
    x = jnp.concatenate([b[...] for b in blocks], axis=0)
    keep = x[:, :128].astype(F32) < LIMIT
    tiles = tiles_ref[:, first * block : last * block]
    deg_ref[...] = deg_in[...] + dot(tiles, jnp.where(keep, 1.0, 0.0).astype(BF16))
    keep = keep[:, :1]
    hidden = q_ref.shape[1]
    step = 512
    for n in range(hidden // step):
        cols = slice(n * step, (n + 1) * step)
        pre = dot(x, q_ref[:, cols]) + qb_ref[:, cols]
        msg = jnp.where(keep, jnp.maximum(pre, 0.0), 0.0).astype(BF16)
        msg_ref[:, cols] = msg
        acc_ref[:, cols] = acc_in[:, cols] + dot(tiles, msg)


def layer_kernel(
    live_ref, acc_ref, deg_ref, self_ref, up_ref, sw_ref, nb_ref, ob_ref,
    emb_ref, gself_ref, gpool_ref, pre_ref,
):
    rows, width = self_ref.shape
    inv_deg = 1.0 / (1.0 + deg_ref[:, :1])
    pooled = (acc_ref[...] * inv_deg).astype(BF16)
    step = 512
    for n in range(width // step):
        cols = slice(n * step, (n + 1) * step)
        pre_ref[:, cols] = self_ref[:, cols] + dot(pooled, nb_ref[:, cols]) + ob_ref[:, cols]
    pre = pre_ref[...]
    act = jnp.maximum(pre, 0.0)
    inv = lax.rsqrt(jnp.mean(act * act, axis=1, keepdims=True) + EPS)
    keep = lax.broadcasted_iota(jnp.int32, (rows, 1), 0) < live_ref[0]
    emb_ref[...] = jnp.where(keep, act * inv, 0.0).astype(BF16)
    up = jnp.where(keep, up_ref[...].astype(F32), 0.0)
    inner = jnp.sum(up * act, axis=1, keepdims=True) / width
    g = inv * up - act * (inv * inv * inv * inner)
    g = jnp.where(pre > 0, g, 0.0).astype(BF16)
    for n in range(nb_ref.shape[0] // step):
        cols = slice(n * step, (n + 1) * step)
        gpool_ref[:, cols] = (dot(g, nb_ref[cols, :], 1, 1) * inv_deg).astype(BF16)
    for n in range(width // step):
        cols = slice(n * step, (n + 1) * step)
        gself_ref[:, cols] = dot(g, sw_ref[cols, :], 1, 1)


def back_kernel(block, first, last, skip, *refs):
    size = last - first
    tt_ref, gpool_ref, msg_ref, q_ref = refs[:4]
    outs = refs[4 : 4 + size]
    gn_ref = refs[4 + size]
    tt = tt_ref[first * block : last * block, :]
    step = 512
    for n in range(gpool_ref.shape[1] // step):
        cols = slice(n * step, (n + 1) * step)
        g = dot(tt, gpool_ref[:, cols])
        live = msg_ref[skip * block : (skip + size) * block, cols].astype(F32) > 0
        gn_ref[:, cols] = jnp.where(live, g, 0.0).astype(BF16)
    gn = gn_ref[...]
    for n in range(q_ref.shape[0] // step):
        cols = slice(n * step, (n + 1) * step)
        part = dot(gn, q_ref[cols, :], 1, 1).astype(BF16)
        for i, out in enumerate(outs):
            out[:, cols] = part[i * block : (i + 1) * block]


def finish_kernel(block, live_ref, wanted_ref, gself_ref, *refs):
    parts, (out_ref, sum_ref) = refs[:-2], refs[-2:]
    sum_ref[...] = gself_ref[...]
    for o, part in enumerate(parts):
        at = pl.ds(pl.multiple_of(wanted_ref[o] * block, block), block)
        sum_ref[at, :] += part[...].astype(F32)
    keep = lax.broadcasted_iota(jnp.int32, (sum_ref.shape[0], 1), 0) < live_ref[0]
    out_ref[...] = jnp.where(keep, sum_ref[...], 0.0).astype(BF16)


def local(x, live, listed, counts, cotangent, q, qb, sw, nb, ob):
    x, lists, counts, up = x[0], listed[0, 0], counts[0], cotangent[0]
    live = live.reshape(1)
    rows, width = x.shape
    hidden = q.shape[1]
    reach, block_count = lists.shape
    block = rows // block_count
    qb, ob = qb[None], ob[None]
    second = lists[:, 1]
    row = jnp.pad(second, (0, 128 - reach))[None]
    wanted = jnp.concatenate([route(row, -o)[0, o : o + 1] for o in range(reach)])
    sent = call(
        lambda *r: pick_kernel(block, *r),
        [((block, width), BF16)] * reach,
        (live, wanted, x),
        [SMEM, SMEM, VMEM],
    )
    got = [route(b, o) for o, b in enumerate(sent)]
    tiles, tiles_t, self_pre = call(
        lambda *r: tiles_kernel(block, *r),
        [((rows, reach * block), BF16), ((reach * block, rows), BF16), ((rows, width), F32)],
        (lists, counts, x, sw),
        [SMEM] + [VMEM] * 3,
        flops=2 * rows * width * width,
    )
    acc = jnp.zeros((rows, hidden), F32)
    deg = jnp.zeros((rows, 128), F32)
    messages = {}
    for first, last in ((0, 4), (4, 8)):
        size = last - first
        msg, acc, deg = call(
            lambda *r, f=first, l=last: message_kernel(block, f, l, *r),
            [((size * block, hidden), BF16), ((rows, hidden), F32), ((rows, 128), F32)],
            (*got[first:last], q, qb, tiles, acc, deg),
            flops=2 * size * block * hidden * (width + rows),
        )
        for o in range(first, last):
            messages[o] = (msg, o - first)
    emb, gself, gpool = call(
        layer_kernel,
        [((rows, width), BF16), ((rows, width), F32), ((rows, hidden), BF16)],
        (live, acc, deg, self_pre, up, sw, nb, ob),
        [SMEM] + [VMEM] * 7,
        scratch=[pltpu.VMEM((rows, width), F32)],
        flops=2 * rows * width * (2 * hidden + width),
    )
    back = [None] * reach
    for first, last in ((6, 8), (4, 6), (2, 4), (0, 2)):
        size = last - first
        msg, skip = messages[first]
        parts = call(
            lambda *r, f=first, l=last, k=skip: back_kernel(block, f, l, k, *r),
            [((block, width), BF16)] * size,
            (tiles_t, gpool, msg, q),
            scratch=[pltpu.VMEM((size * block, hidden), BF16)],
            flops=2 * size * block * hidden * (width + rows),
        )
        for i, part in enumerate(parts):
            back[first + i] = route(part, -(first + i))
    (grad,) = call(
        lambda *r: finish_kernel(block, *r),
        [((rows, width), BF16)],
        (live, wanted, gself, *back),
        [SMEM, SMEM] + [VMEM] * (1 + reach),
        scratch=[pltpu.VMEM((rows, width), F32)],
    )
    return emb[None], grad[None]


def solution(mesh):
    data = P("side", "dom", None)
    return jax.shard_map(
        local,
        mesh=mesh,
        in_specs=(
            data,
            P("side", "dom"),
            P("side", "dom", None, None),
            data,
            data,
            P(),
            P(),
            P(),
            P(),
            P(),
        ),
        out_specs=(data, data),
        check_vma=False,
    )
```

```python
import jax
import jax.numpy as jnp
from jax import lax
from jax.experimental import pallas as pl
from jax.experimental.pallas import tpu as pltpu
from jax.sharding import PartitionSpec as P

EPS = 1e-06
DEAD = 16384.0
LIMIT = 8192.0
LINE = 4
F32 = jnp.float32
BF16 = jnp.bfloat16
VMEM = pl.BlockSpec(memory_space=pltpu.VMEM)
SMEM = pl.BlockSpec(memory_space=pltpu.SMEM)


def dot(a, b, ca=1, cb=0):
    return lax.dot_general(a, b, (((ca,), (cb,)), ((), ())), preferred_element_type=F32)


def call(kernel, outs, ins, in_specs=None, scratch=(), limit=24, flops=0):
    return pl.pallas_call(
        kernel,
        out_shape=[jax.ShapeDtypeStruct(s, d) for s, d in outs],
        in_specs=in_specs or [VMEM] * len(ins),
        out_specs=[VMEM] * len(outs),
        scratch_shapes=list(scratch),
        compiler_params=pltpu.CompilerParams(vmem_limit_bytes=limit << 20),
        cost_estimate=pl.CostEstimate(flops=flops, bytes_accessed=1 << 20, transcendentals=0),
    )(*ins)


def swap_rows(x, shift):
    count = lax.axis_size("dom")
    pairs = [
        (s * count + j, (1 - s) * count + (j + shift) % count)
        for s in range(2)
        for j in range(count)
    ]
    return lax.ppermute(x, ("side", "dom"), pairs)


def along(x, d):
    count = lax.axis_size("dom")
    pairs = [(j, j // LINE * LINE + (j + d) % LINE) for j in range(count)]
    return lax.ppermute(x, "dom", pairs)


def near(p, d):
    return jnp.where(p >= d, d + LINE, d)


def far(p, d):
    return jnp.where(p >= d, d, d + LINE)


def at_block(index, block):
    return pl.ds(pl.multiple_of(index * block, block), block)


def pick_near_kernel(block, place_ref, m1, m2, m3, below_ref, *outs):
    for d, (meta, out) in enumerate(zip((m1, m2, m3), outs), 1):
        p = lax.rem(place_ref[0] + d, LINE)
        out[...] = below_ref[at_block(meta[0, near(p, d)], block), :]


def pick_far_kernel(block, place_ref, m1, m2, m3, same_ref, below_ref, *outs):
    for d, (meta, out) in enumerate(zip((m1, m2, m3), outs), 1):
        p = lax.rem(place_ref[0] + d, LINE)
        at = at_block(meta[0, far(p, d)], block)

        @pl.when(p >= d)
        def _():
            out[...] = same_ref[at, :]

        @pl.when(p < d)
        def _():
            out[...] = below_ref[at, :]


def slots(p):
    return [0, LINE] + [near(p, d) for d in range(1, LINE)] + [far(p, d) for d in range(1, LINE)]


def tiles_kernel(block, place_ref, lists_ref, counts_ref, x_ref, sw_ref, tiles_ref, tiles_t_ref, self_ref):
    for i, o in enumerate(slots(place_ref[0])):
        first, second = lists_ref[o, 0], lists_ref[o, 1]
        at = pl.ds(pl.multiple_of((o * 2 + second) * block, block), block)
        tile = (counts_ref[:, at] * (first + second)).astype(F32)
        tiles_ref[:, i * block : (i + 1) * block] = tile.astype(BF16)
        tiles_t_ref[i * block : (i + 1) * block, :] = tile.T.astype(BF16)
    self_ref[...] = dot(x_ref[...], sw_ref[...])


def message_kernel(block, first, last, *refs):
    size = last - first
    if first == 0:
        lists_ref, same_ref, below_ref = refs[:3]
        held = [same_ref[at_block(lists_ref[0, 1], block), :]]
        held += [below_ref[at_block(lists_ref[LINE, 1], block), :]]
        refs = refs[3:]
        held += [b[...] for b in refs[: size - 2]]
        refs = refs[size - 2 :]
    else:
        held = [b[...] for b in refs[:size]]
        refs = refs[size:]
    q_ref, qb_ref, tiles_ref = refs[:3]
    acc_in, deg_in = refs[3:5] if first else (None, None)
    msg_ref, acc_ref, deg_ref = refs[-3:]
    x = jnp.concatenate(held, axis=0)
    keep = x[:, :128].astype(F32) < LIMIT
    tiles = tiles_ref[:, first * block : last * block]
    deg = dot(tiles, jnp.where(keep, 1.0, 0.0).astype(BF16))
    deg_ref[...] = deg + deg_in[...] if first else deg
    keep = keep[:, :1]
    hidden = q_ref.shape[1]
    step = 512
    for n in range(hidden // step):
        cols = slice(n * step, (n + 1) * step)
        pre = dot(x, q_ref[:, cols]) + qb_ref[:, cols]
        msg = jnp.where(keep, jnp.maximum(pre, 0.0), 0.0).astype(BF16)
        msg_ref[:, cols] = msg
        acc = dot(tiles, msg)
        acc_ref[:, cols] = acc + acc_in[:, cols] if first else acc


def layer_kernel(
    live_ref, acc_ref, deg_ref, self_ref, up_ref, sw_ref, nb_ref, ob_ref,
    emb_ref, gself_ref, gpool_ref, pre_ref,
):
    rows, width = self_ref.shape
    inv_deg = 1.0 / (1.0 + deg_ref[:, :1])
    pooled = (acc_ref[...] * inv_deg).astype(BF16)
    step = 512
    for n in range(width // step):
        cols = slice(n * step, (n + 1) * step)
        pre_ref[:, cols] = self_ref[:, cols] + dot(pooled, nb_ref[:, cols]) + ob_ref[:, cols]
    pre = pre_ref[...]
    act = jnp.maximum(pre, 0.0)
    inv = lax.rsqrt(jnp.mean(act * act, axis=1, keepdims=True) + EPS)
    keep = lax.broadcasted_iota(jnp.int32, (rows, 1), 0) < live_ref[0]
    emb_ref[...] = jnp.where(keep, act * inv, 0.0).astype(BF16)
    up = jnp.where(keep, up_ref[...].astype(F32), 0.0)
    inner = jnp.sum(up * act, axis=1, keepdims=True) / width
    g = inv * up - act * (inv * inv * inv * inner)
    g = jnp.where(pre > 0, g, 0.0).astype(BF16)
    for n in range(nb_ref.shape[0] // step):
        cols = slice(n * step, (n + 1) * step)
        gpool_ref[:, cols] = (dot(g, nb_ref[cols, :], 1, 1) * inv_deg).astype(BF16)
    for n in range(width // step):
        cols = slice(n * step, (n + 1) * step)
        gself_ref[:, cols] = dot(g, sw_ref[cols, :], 1, 1)


def back_kernel(block, first, last, skip, *refs):
    size = last - first
    tt_ref, gpool_ref, msg_ref, q_ref = refs[:4]
    outs = refs[4 : 4 + size]
    gn_ref = refs[4 + size]
    tt = tt_ref[first * block : last * block, :]
    step = 512
    for n in range(gpool_ref.shape[1] // step):
        cols = slice(n * step, (n + 1) * step)
        g = dot(tt, gpool_ref[:, cols])
        live = msg_ref[skip * block : (skip + size) * block, cols].astype(F32) > 0
        gn_ref[:, cols] = jnp.where(live, g, 0.0).astype(BF16)
    gn = gn_ref[...]
    for n in range(q_ref.shape[0] // step):
        cols = slice(n * step, (n + 1) * step)
        part = dot(gn, q_ref[cols, :], 1, 1).astype(BF16)
        for i, out in enumerate(outs):
            out[:, cols] = part[i * block : (i + 1) * block]


def sum_far_kernel(block, place_ref, lists_ref, m1, m2, m3, own_ref, c1, c2, c3, same_ref, below_ref, same, below):
    same[...] = jnp.zeros_like(same)
    below[...] = jnp.zeros_like(below)
    same[at_block(lists_ref[0, 1], block), :] = own_ref[...].astype(F32)
    for d, (meta, part) in enumerate(zip((m1, m2, m3), (c1, c2, c3)), 1):
        p = lax.rem(place_ref[0] + d, LINE)
        at = at_block(meta[0, far(p, d)], block)

        @pl.when(p >= d)
        def _():
            same[at, :] += part[...].astype(F32)

        @pl.when(p < d)
        def _():
            below[at, :] += part[...].astype(F32)

    same_ref[...] = same[...].astype(BF16)
    below_ref[...] = below[...].astype(BF16)


def sum_near_kernel(block, place_ref, lists_ref, m1, m2, m3, own_ref, d1, d2, d3, out_ref, total):
    total[...] = jnp.zeros_like(total)
    total[at_block(lists_ref[LINE, 1], block), :] = own_ref[...].astype(F32)
    for d, (meta, part) in enumerate(zip((m1, m2, m3), (d1, d2, d3)), 1):
        p = lax.rem(place_ref[0] + d, LINE)
        total[at_block(meta[0, near(p, d)], block), :] += part[...].astype(F32)
    out_ref[...] = total[...].astype(BF16)


def finish_kernel(live_ref, gself_ref, a_ref, b_ref, c_ref, out_ref):
    total = gself_ref[...] + a_ref[...].astype(F32) + b_ref[...].astype(F32) + c_ref[...].astype(F32)
    keep = lax.broadcasted_iota(jnp.int32, (total.shape[0], 1), 0) < live_ref[0]
    out_ref[...] = jnp.where(keep, total, 0.0).astype(BF16)


def local(x, live, listed, counts, cotangent, q, qb, sw, nb, ob):
    x, lists, counts, up = x[0], listed[0, 0], counts[0], cotangent[0]
    live = live.reshape(1)
    rows, width = x.shape
    hidden = q.shape[1]
    reach, block_count = lists.shape
    block = rows // block_count
    qb, ob = qb[None], ob[None]
    place = (lax.axis_index("dom") % LINE).astype(jnp.int32).reshape(1)
    keep = lax.broadcasted_iota(jnp.int32, (rows, 1), 0) < live[0]
    marked = jnp.where(keep, x, jnp.asarray(DEAD, BF16))
    row = jnp.pad(lists[:, 1], (0, 128 - reach))[None]
    below = swap_rows(marked, LINE)
    same = swap_rows(marked, 0)
    metas = [along(row, -d) for d in range(1, LINE)]
    below2 = swap_rows(marked, 2 * LINE)
    one = ((block, width), BF16)
    three = [SMEM] * 4
    picked = call(
        lambda *r: pick_near_kernel(block, *r), [one] * 3, (place, *metas, below), three + [VMEM]
    )
    got_near = [along(b, d) for d, b in enumerate(picked, 1)]
    picked = call(
        lambda *r: pick_far_kernel(block, *r),
        [one] * 3,
        (place, *metas, same, below2),
        three + [VMEM] * 2,
    )
    got_far = [along(b, d) for d, b in enumerate(picked, 1)]
    tiles, tiles_t, self_pre = call(
        lambda *r: tiles_kernel(block, *r),
        [((rows, reach * block), BF16), ((reach * block, rows), BF16), ((rows, width), F32)],
        (place, lists, counts, x, sw),
        [SMEM] * 2 + [VMEM] * 3,
        flops=2 * rows * width * width,
    )
    split = 2 + LINE - 1

    def message(first, last, ins, specs):
        size = last - first
        return call(
            lambda *r: message_kernel(block, first, last, *r),
            [((size * block, hidden), BF16), ((rows, hidden), F32), ((rows, 128), F32)],
            ins,
            specs,
            flops=2 * size * block * hidden * (width + rows),
        )

    msg_a, acc, deg = message(
        0, split, (lists, same, below, *got_near, q, qb, tiles), [SMEM] + [VMEM] * 8
    )
    msg_b, acc, deg = message(split, reach, (*got_far, q, qb, tiles, acc, deg), [VMEM] * 8)
    emb, gself, gpool = call(
        layer_kernel,
        [((rows, width), BF16), ((rows, width), F32), ((rows, hidden), BF16)],
        (live, acc, deg, self_pre, up, sw, nb, ob),
        [SMEM] + [VMEM] * 7,
        scratch=[pltpu.VMEM((rows, width), F32)],
        flops=2 * rows * width * (2 * hidden + width),
    )

    def back(first, last, msg, skip):
        size = last - first
        return call(
            lambda *r: back_kernel(block, first, last, skip, *r),
            [one] * size,
            (tiles_t, gpool, msg, q),
            scratch=[pltpu.VMEM((size * block, hidden), BF16)],
            flops=2 * size * block * hidden * (width + rows),
        )

    back_far = [along(b, -d) for d, b in enumerate(back(split, reach, msg_b, 0), 1)]
    back_near = [along(b, -d) for d, b in enumerate(back(2, split, msg_a, 2), 1)]
    own_same, own_below = back(0, 2, msg_a, 0)
    two = ((rows, width), BF16)
    total = pltpu.VMEM((rows, width), F32)
    sum_same, sum_below2 = call(
        lambda *r: sum_far_kernel(block, *r),
        [two, two],
        (place, lists, *metas, own_same, *back_far),
        [SMEM] * 5 + [VMEM] * 4,
        scratch=[total, total],
    )
    g_below2 = swap_rows(sum_below2, -2 * LINE)
    g_same = swap_rows(sum_same, 0)
    (sum_below,) = call(
        lambda *r: sum_near_kernel(block, *r),
        [two],
        (place, lists, *metas, own_below, *back_near),
        [SMEM] * 5 + [VMEM] * 4,
        scratch=[total],
    )
    g_below = swap_rows(sum_below, -LINE)
    (grad,) = call(
        finish_kernel, [two], (live, gself, g_same, g_below, g_below2), [SMEM] + [VMEM] * 4
    )
    return emb[None], grad[None]


def solution(mesh):
    data = P("side", "dom", None)
    return jax.shard_map(
        local,
        mesh=mesh,
        in_specs=(
            data,
            P("side", "dom"),
            P("side", "dom", None, None),
            data,
            data,
            P(),
            P(),
            P(),
            P(),
            P(),
        ),
        out_specs=(data, data),
        check_vma=False,
    )
```

```python
import jax
import jax.numpy as jnp
from jax import lax
from jax.experimental import pallas as pl
from jax.experimental.pallas import tpu as pltpu
from jax.sharding import PartitionSpec as P

EPS = 1e-06
DEAD = 16384.0
LIMIT = 8192.0
LINE = 4
F32 = jnp.float32
BF16 = jnp.bfloat16
VMEM = pl.BlockSpec(memory_space=pltpu.VMEM)
HELD = pl.BlockSpec(memory_space=pl.ANY)
SMEM = pl.BlockSpec(memory_space=pltpu.SMEM)


def dot(a, b, ca=1, cb=0):
    return lax.dot_general(a, b, (((ca,), (cb,)), ((), ())), preferred_element_type=F32)


def call(kernel, outs, ins, in_specs=None, scratch=(), limit=24, flops=0):
    return pl.pallas_call(
        kernel,
        out_shape=[jax.ShapeDtypeStruct(s, d) for s, d in outs],
        in_specs=in_specs or [VMEM] * len(ins),
        out_specs=[VMEM] * len(outs),
        scratch_shapes=list(scratch),
        compiler_params=pltpu.CompilerParams(vmem_limit_bytes=limit << 20),
        cost_estimate=pl.CostEstimate(flops=flops, bytes_accessed=1 << 20, transcendentals=0),
    )(*ins)


def swap_rows(x, shift):
    count = lax.axis_size("dom")
    pairs = [
        (s * count + j, (1 - s) * count + (j + shift) % count)
        for s in range(2)
        for j in range(count)
    ]
    return lax.ppermute(x, ("side", "dom"), pairs)


def along(x, d):
    count = lax.axis_size("dom")
    pairs = [(j, j // LINE * LINE + (j + d) % LINE) for j in range(count)]
    return lax.ppermute(x, "dom", pairs)


def near(p, d):
    return jnp.where(p >= d, d + LINE, d)


def far(p, d):
    return jnp.where(p >= d, d, d + LINE)


def at_block(index, block):
    return pl.ds(pl.multiple_of(index * block, block), block)


def pick_near_kernel(block, place_ref, m1, m2, m3, below_ref, _, *outs):
    for d, (meta, out) in enumerate(zip((m1, m2, m3), outs), 1):
        p = lax.rem(place_ref[0] + d, LINE)
        out[...] = below_ref[at_block(meta[0, near(p, d)], block), :]


def pick_far_kernel(block, place_ref, m1, m2, m3, same_ref, below_ref, *outs):
    for d, (meta, out) in enumerate(zip((m1, m2, m3), outs), 1):
        p = lax.rem(place_ref[0] + d, LINE)
        at = at_block(meta[0, far(p, d)], block)

        @pl.when(p >= d)
        def _():
            out[...] = same_ref[at, :]

        @pl.when(p < d)
        def _():
            out[...] = below_ref[at, :]


def slots(p):
    return [0, LINE] + [near(p, d) for d in range(1, LINE)] + [far(p, d) for d in range(1, LINE)]


def tiles_kernel(block, place_ref, lists_ref, counts_ref, x_ref, sw_ref, tiles_ref, tiles_t_ref, self_ref):
    for i, o in enumerate(slots(place_ref[0])):
        first, second = lists_ref[o, 0], lists_ref[o, 1]
        at = pl.ds(pl.multiple_of((o * 2 + second) * block, block), block)
        tile = (counts_ref[:, at] * (first + second)).astype(F32)
        tiles_ref[:, i * block : (i + 1) * block] = tile.astype(BF16)
        tiles_t_ref[i * block : (i + 1) * block, :] = tile.T.astype(BF16)
    self_ref[...] = dot(x_ref[...], sw_ref[...])


def message_kernel(block, first, last, *refs):
    size = last - first
    if first == 0:
        lists_ref, same_ref, below_ref = refs[:3]
        held = [same_ref[at_block(lists_ref[0, 1], block), :]]
        held += [below_ref[at_block(lists_ref[LINE, 1], block), :]]
        refs = refs[3:]
        held += [b[...] for b in refs[: size - 2]]
        refs = refs[size - 2 :]
    else:
        held = [b[...] for b in refs[:size]]
        refs = refs[size:]
    q_ref, qb_ref, tiles_ref = refs[:3]
    acc_in, deg_in = refs[3:5] if first else (None, None)
    msg_ref, acc_ref, deg_ref = refs[-3:]
    x = jnp.concatenate(held, axis=0)
    keep = x[:, :128].astype(F32) < LIMIT
    tiles = tiles_ref[:, first * block : last * block]
    deg = dot(tiles, jnp.where(keep, 1.0, 0.0).astype(BF16))
    deg_ref[...] = deg + deg_in[...] if first else deg
    keep = keep[:, :1]
    hidden = q_ref.shape[1]
    step = 512
    for n in range(hidden // step):
        cols = slice(n * step, (n + 1) * step)
        pre = dot(x, q_ref[:, cols]) + qb_ref[:, cols]
        msg = jnp.where(keep, jnp.maximum(pre, 0.0), 0.0).astype(BF16)
        msg_ref[:, cols] = msg
        acc = dot(tiles, msg)
        acc_ref[:, cols] = acc + acc_in[:, cols] if first else acc


def layer_kernel(
    live_ref, acc_ref, deg_ref, self_ref, up_ref, sw_ref, nb_ref, ob_ref,
    emb_ref, gself_ref, gpool_ref, pre_ref,
):
    rows, width = self_ref.shape
    inv_deg = 1.0 / (1.0 + deg_ref[:, :1])
    pooled = (acc_ref[...] * inv_deg).astype(BF16)
    step = 512
    for n in range(width // step):
        cols = slice(n * step, (n + 1) * step)
        pre_ref[:, cols] = self_ref[:, cols] + dot(pooled, nb_ref[:, cols]) + ob_ref[:, cols]
    pre = pre_ref[...]
    act = jnp.maximum(pre, 0.0)
    inv = lax.rsqrt(jnp.mean(act * act, axis=1, keepdims=True) + EPS)
    keep = lax.broadcasted_iota(jnp.int32, (rows, 1), 0) < live_ref[0]
    emb_ref[...] = jnp.where(keep, act * inv, 0.0).astype(BF16)
    up = jnp.where(keep, up_ref[...].astype(F32), 0.0)
    inner = jnp.sum(up * act, axis=1, keepdims=True) / width
    g = inv * up - act * (inv * inv * inv * inner)
    g = jnp.where(pre > 0, g, 0.0).astype(BF16)
    for n in range(nb_ref.shape[0] // step):
        cols = slice(n * step, (n + 1) * step)
        gpool_ref[:, cols] = (dot(g, nb_ref[cols, :], 1, 1) * inv_deg).astype(BF16)
    for n in range(width // step):
        cols = slice(n * step, (n + 1) * step)
        gself_ref[:, cols] = dot(g, sw_ref[cols, :], 1, 1)


def back_kernel(block, first, last, skip, *refs):
    size = last - first
    tt_ref, gpool_ref, msg_ref, q_ref = refs[:4]
    outs = refs[4 : 4 + size]
    gn_ref = refs[4 + size]
    tt = tt_ref[first * block : last * block, :]
    step = 512
    for n in range(gpool_ref.shape[1] // step):
        cols = slice(n * step, (n + 1) * step)
        g = dot(tt, gpool_ref[:, cols])
        live = msg_ref[skip * block : (skip + size) * block, cols].astype(F32) > 0
        gn_ref[:, cols] = jnp.where(live, g, 0.0).astype(BF16)
    gn = gn_ref[...]
    for n in range(q_ref.shape[0] // step):
        cols = slice(n * step, (n + 1) * step)
        part = dot(gn, q_ref[cols, :], 1, 1).astype(BF16)
        for i, out in enumerate(outs):
            out[:, cols] = part[i * block : (i + 1) * block]


def sum_far_kernel(block, place_ref, lists_ref, m1, m2, m3, own_ref, c1, c2, c3, same_ref, below_ref, same, below):
    same[...] = jnp.zeros_like(same)
    below[...] = jnp.zeros_like(below)
    same[at_block(lists_ref[0, 1], block), :] = own_ref[...].astype(F32)
    for d, (meta, part) in enumerate(zip((m1, m2, m3), (c1, c2, c3)), 1):
        p = lax.rem(place_ref[0] + d, LINE)
        at = at_block(meta[0, far(p, d)], block)

        @pl.when(p >= d)
        def _():
            same[at, :] += part[...].astype(F32)

        @pl.when(p < d)
        def _():
            below[at, :] += part[...].astype(F32)

    same_ref[...] = same[...].astype(BF16)
    below_ref[...] = below[...].astype(BF16)


def sum_near_kernel(block, place_ref, lists_ref, m1, m2, m3, own_ref, d1, d2, d3, out_ref, total):
    total[...] = jnp.zeros_like(total)
    total[at_block(lists_ref[LINE, 1], block), :] = own_ref[...].astype(F32)
    for d, (meta, part) in enumerate(zip((m1, m2, m3), (d1, d2, d3)), 1):
        p = lax.rem(place_ref[0] + d, LINE)
        total[at_block(meta[0, near(p, d)], block), :] += part[...].astype(F32)
    out_ref[...] = total[...].astype(BF16)


def finish_kernel(live_ref, gself_ref, a_ref, b_ref, c_ref, out_ref):
    total = gself_ref[...] + a_ref[...].astype(F32) + b_ref[...].astype(F32) + c_ref[...].astype(F32)
    keep = lax.broadcasted_iota(jnp.int32, (total.shape[0], 1), 0) < live_ref[0]
    out_ref[...] = jnp.where(keep, total, 0.0).astype(BF16)


def local(x, live, listed, counts, cotangent, q, qb, sw, nb, ob):
    x, lists, counts, up = x[0], listed[0, 0], counts[0], cotangent[0]
    live = live.reshape(1)
    rows, width = x.shape
    hidden = q.shape[1]
    reach, block_count = lists.shape
    block = rows // block_count
    qb, ob = qb[None], ob[None]
    place = (lax.axis_index("dom") % LINE).astype(jnp.int32).reshape(1)
    keep = lax.broadcasted_iota(jnp.int32, (rows, 1), 0) < live[0]
    marked = jnp.where(keep, x, jnp.asarray(DEAD, BF16))
    row = jnp.pad(lists[:, 1], (0, 128 - reach))[None]
    below = swap_rows(marked, LINE)
    same = swap_rows(marked, 0)
    metas = [along(row, -d) for d in range(1, LINE)]
    later, *metas = lax.optimization_barrier((marked, *metas))
    below2 = swap_rows(later, 2 * LINE)
    one = ((block, width), BF16)
    three = [SMEM] * 4
    tiles, tiles_t, self_pre = call(
        lambda *r: tiles_kernel(block, *r),
        [((rows, reach * block), BF16), ((reach * block, rows), BF16), ((rows, width), F32)],
        (place, lists, counts, x, sw),
        [SMEM] * 2 + [VMEM] * 3,
        flops=2 * rows * width * width,
    )
    picked = call(
        lambda *r: pick_near_kernel(block, *r), [one] * 3, (place, *metas, below, tiles), three + [VMEM, HELD]
    )
    got_near = [along(b, d) for d, b in enumerate(picked, 1)]
    picked = call(
        lambda *r: pick_far_kernel(block, *r),
        [one] * 3,
        (place, *metas, same, below2),
        three + [VMEM] * 2,
    )
    got_far = [along(b, d) for d, b in enumerate(picked, 1)]
    split = 2 + LINE - 1

    def message(first, last, ins, specs):
        size = last - first
        return call(
            lambda *r: message_kernel(block, first, last, *r),
            [((size * block, hidden), BF16), ((rows, hidden), F32), ((rows, 128), F32)],
            ins,
            specs,
            flops=2 * size * block * hidden * (width + rows),
        )

    msg_a, acc, deg = message(
        0, split, (lists, same, below, *got_near, q, qb, tiles), [SMEM] + [VMEM] * 8
    )
    msg_b, acc, deg = message(split, reach, (*got_far, q, qb, tiles, acc, deg), [VMEM] * 8)
    emb, gself, gpool = call(
        layer_kernel,
        [((rows, width), BF16), ((rows, width), F32), ((rows, hidden), BF16)],
        (live, acc, deg, self_pre, up, sw, nb, ob),
        [SMEM] + [VMEM] * 7,
        scratch=[pltpu.VMEM((rows, width), F32)],
        flops=2 * rows * width * (2 * hidden + width),
    )

    def back(first, last, msg, skip):
        size = last - first
        return call(
            lambda *r: back_kernel(block, first, last, skip, *r),
            [one] * size,
            (tiles_t, gpool, msg, q),
            scratch=[pltpu.VMEM((size * block, hidden), BF16)],
            flops=2 * size * block * hidden * (width + rows),
        )

    back_far = [along(b, -d) for d, b in enumerate(back(split, reach, msg_b, 0), 1)]
    back_near = [along(b, -d) for d, b in enumerate(back(2, split, msg_a, 2), 1)]
    own_same, own_below = back(0, 2, msg_a, 0)
    two = ((rows, width), BF16)
    total = pltpu.VMEM((rows, width), F32)
    sum_same, sum_below2 = call(
        lambda *r: sum_far_kernel(block, *r),
        [two, two],
        (place, lists, *metas, own_same, *back_far),
        [SMEM] * 5 + [VMEM] * 4,
        scratch=[total, total],
    )
    g_below2 = swap_rows(sum_below2, -2 * LINE)
    g_same = swap_rows(sum_same, 0)
    (sum_below,) = call(
        lambda *r: sum_near_kernel(block, *r),
        [two],
        (place, lists, *metas, own_below, *back_near),
        [SMEM] * 5 + [VMEM] * 4,
        scratch=[total],
    )
    g_below = swap_rows(sum_below, -LINE)
    (grad,) = call(
        finish_kernel, [two], (live, gself, g_same, g_below, g_below2), [SMEM] + [VMEM] * 4
    )
    return emb[None], grad[None]


def solution(mesh):
    data = P("side", "dom", None)
    return jax.shard_map(
        local,
        mesh=mesh,
        in_specs=(
            data,
            P("side", "dom"),
            P("side", "dom", None, None),
            data,
            data,
            P(),
            P(),
            P(),
            P(),
            P(),
        ),
        out_specs=(data, data),
        check_vma=False,
    )
```

```python
import jax
import jax.numpy as jnp
from jax import lax
from jax.experimental import pallas as pl
from jax.experimental.pallas import tpu as pltpu
from jax.sharding import PartitionSpec as P

EPS = 1e-06
DEAD = 16384.0
LIMIT = 8192.0
MICROSECOND = 10**9
LINE = 4
F32 = jnp.float32
BF16 = jnp.bfloat16
VMEM = pl.BlockSpec(memory_space=pltpu.VMEM)
HELD = pl.BlockSpec(memory_space=pl.ANY)
SMEM = pl.BlockSpec(memory_space=pltpu.SMEM)


def dot(a, b, ca=1, cb=0):
    return lax.dot_general(a, b, (((ca,), (cb,)), ((), ())), preferred_element_type=F32)


def call(kernel, outs, ins, in_specs=None, scratch=(), limit=24, flops=0):
    return pl.pallas_call(
        kernel,
        out_shape=[jax.ShapeDtypeStruct(s, d) for s, d in outs],
        in_specs=in_specs or [VMEM] * len(ins),
        out_specs=[VMEM] * len(outs),
        scratch_shapes=list(scratch),
        compiler_params=pltpu.CompilerParams(vmem_limit_bytes=limit << 20),
        cost_estimate=pl.CostEstimate(flops=flops, bytes_accessed=1 << 20, transcendentals=0),
    )(*ins)


def swap_rows(x, shift):
    count = lax.axis_size("dom")
    pairs = [
        (s * count + j, (1 - s) * count + (j + shift) % count)
        for s in range(2)
        for j in range(count)
    ]
    return lax.ppermute(x, ("side", "dom"), pairs)


def along(x, d):
    count = lax.axis_size("dom")
    pairs = [(j, j // LINE * LINE + (j + d) % LINE) for j in range(count)]
    return lax.ppermute(x, "dom", pairs)


def straight(x, d, back=False):
    count = lax.axis_size("dom")
    pairs = []
    for s in range(2):
        for j in range(count):
            to = j + d if j % LINE + d < LINE else j + d + LINE
            pair = (s * count + j, (1 - s) * count + to % count)
            pairs.append(pair[::-1] if back else pair)
    return lax.ppermute(x, ("side", "dom"), pairs)


def near(p, d):
    return jnp.where(p >= d, d + LINE, d)


def far(p, d):
    return jnp.where(p >= d, d, d + LINE)


def at_block(index, block):
    return pl.ds(pl.multiple_of(index * block, block), block)


def pick_kernel(block, offset, place_ref, m1, m2, m3, rows_ref, *refs):
    outs = refs[-3:]
    for d, (meta, out) in enumerate(zip((m1, m2, m3), outs), 1):
        p = lax.rem(place_ref[0] + d, LINE)
        out[...] = rows_ref[at_block(meta[0, offset(p, d)], block), :]


def slots(p):
    return [0, LINE] + [far(p, d) for d in range(1, LINE)] + [near(p, d) for d in range(1, LINE)]


def tiles_kernel(block, place_ref, lists_ref, counts_ref, x_ref, sw_ref, tiles_ref, tiles_t_ref, self_ref):
    for i, o in enumerate(slots(place_ref[0])):
        first, second = lists_ref[o, 0], lists_ref[o, 1]
        at = pl.ds(pl.multiple_of((o * 2 + second) * block, block), block)
        tile = (counts_ref[:, at] * (first + second)).astype(F32)
        tiles_ref[:, i * block : (i + 1) * block] = tile.astype(BF16)
        tiles_t_ref[i * block : (i + 1) * block, :] = tile.T.astype(BF16)
    self_ref[...] = dot(x_ref[...], sw_ref[...])


def message_kernel(block, first, last, *refs):
    size = last - first
    if first == 0:
        lists_ref, same_ref, below_ref = refs[:3]
        held = [same_ref[at_block(lists_ref[0, 1], block), :]]
        held += [below_ref[at_block(lists_ref[LINE, 1], block), :]]
        refs = refs[3:]
        held += [b[...] for b in refs[: size - 2]]
        refs = refs[size - 2 :]
    else:
        held = [b[...] for b in refs[:size]]
        refs = refs[size:]
    q_ref, qb_ref, tiles_ref = refs[:3]
    acc_in, deg_in = refs[3:5] if first else (None, None)
    msg_ref, acc_ref, deg_ref = refs[-3:]
    x = jnp.concatenate(held, axis=0)
    keep = x[:, :128].astype(F32) < LIMIT
    tiles = tiles_ref[:, first * block : last * block]
    deg = dot(tiles, jnp.where(keep, 1.0, 0.0).astype(BF16))
    deg_ref[...] = deg + deg_in[...] if first else deg
    keep = keep[:, :1]
    hidden = q_ref.shape[1]
    step = 512
    for n in range(hidden // step):
        cols = slice(n * step, (n + 1) * step)
        pre = dot(x, q_ref[:, cols]) + qb_ref[:, cols]
        msg = jnp.where(keep, jnp.maximum(pre, 0.0), 0.0).astype(BF16)
        msg_ref[:, cols] = msg
        acc = dot(tiles, msg)
        acc_ref[:, cols] = acc + acc_in[:, cols] if first else acc


def layer_kernel(
    live_ref, acc_ref, deg_ref, self_ref, up_ref, sw_ref, nb_ref, ob_ref,
    emb_ref, gself_ref, gpool_ref, pre_ref,
):
    rows, width = self_ref.shape
    inv_deg = 1.0 / (1.0 + deg_ref[:, :1])
    pooled = (acc_ref[...] * inv_deg).astype(BF16)
    step = 512
    for n in range(width // step):
        cols = slice(n * step, (n + 1) * step)
        pre_ref[:, cols] = self_ref[:, cols] + dot(pooled, nb_ref[:, cols]) + ob_ref[:, cols]
    pre = pre_ref[...]
    act = jnp.maximum(pre, 0.0)
    inv = lax.rsqrt(jnp.mean(act * act, axis=1, keepdims=True) + EPS)
    keep = lax.broadcasted_iota(jnp.int32, (rows, 1), 0) < live_ref[0]
    emb_ref[...] = jnp.where(keep, act * inv, 0.0).astype(BF16)
    up = jnp.where(keep, up_ref[...].astype(F32), 0.0)
    inner = jnp.sum(up * act, axis=1, keepdims=True) / width
    g = inv * up - act * (inv * inv * inv * inner)
    g = jnp.where(pre > 0, g, 0.0).astype(BF16)
    for n in range(nb_ref.shape[0] // step):
        cols = slice(n * step, (n + 1) * step)
        gpool_ref[:, cols] = (dot(g, nb_ref[cols, :], 1, 1) * inv_deg).astype(BF16)
    for n in range(width // step):
        cols = slice(n * step, (n + 1) * step)
        gself_ref[:, cols] = dot(g, sw_ref[cols, :], 1, 1)


def back_dot(block, first, last, skip, tt_ref, gpool_ref, msg_ref, q_ref, gn_ref, store):
    tt = tt_ref[first * block : last * block, :]
    at = slice(skip * block, (skip + last - first) * block)
    step = 512
    for n in range(gpool_ref.shape[1] // step):
        cols = slice(n * step, (n + 1) * step)
        live = msg_ref[at, cols].astype(F32) > 0
        gn_ref[:, cols] = jnp.where(live, dot(tt, gpool_ref[:, cols]), 0.0).astype(BF16)
    gn = gn_ref[...]
    for n in range(q_ref.shape[0] // step):
        cols = slice(n * step, (n + 1) * step)
        store(cols, dot(gn, q_ref[cols, :], 1, 1))


def back_kernel(block, first, last, skip, tt_ref, gpool_ref, msg_ref, q_ref, _, *refs):
    outs, gn_ref = refs[:-1], refs[-1]

    def store(cols, part):
        for i, out in enumerate(outs):
            out[:, cols] = part[i * block : (i + 1) * block].astype(BF16)

    back_dot(block, first, last, skip, tt_ref, gpool_ref, msg_ref, q_ref, gn_ref, store)


def back_own_kernel(block, lists_ref, tt_ref, gpool_ref, msg_ref, q_ref, _, same_ref, below_ref, gn_ref):
    same_ref[...] = jnp.zeros_like(same_ref)
    at = at_block(lists_ref[0, 1], block)

    def store(cols, part):
        same_ref[at, cols] = part[:block].astype(BF16)
        below_ref[:, cols] = part[block:].astype(BF16)

    back_dot(block, 0, 2, 0, tt_ref, gpool_ref, msg_ref, q_ref, gn_ref, store)


def sum_near_kernel(block, place_ref, lists_ref, m1, m2, m3, own_ref, d1, d2, d3, out_ref, total):
    total[...] = jnp.zeros_like(total)
    total[at_block(lists_ref[LINE, 1], block), :] = own_ref[...].astype(F32)
    for d, (meta, part) in enumerate(zip((m1, m2, m3), (d1, d2, d3)), 1):
        p = lax.rem(place_ref[0] + d, LINE)
        total[at_block(meta[0, near(p, d)], block), :] += part[...].astype(F32)
    out_ref[...] = total[...].astype(BF16)


def place_kernel(block, place_ref, m1, m2, m3, gself_ref, c1, c2, c3, total_ref):
    total_ref[...] = gself_ref[...]
    for d, (meta, part) in enumerate(zip((m1, m2, m3), (c1, c2, c3)), 1):
        p = lax.rem(place_ref[0] + d, LINE)
        total_ref[at_block(meta[0, far(p, d)], block), :] += part[...].astype(F32)


def finish_kernel(live_ref, total_ref, same_ref, below_ref, out_ref):
    total = total_ref[...] + same_ref[...].astype(F32) + below_ref[...].astype(F32)
    keep = lax.broadcasted_iota(jnp.int32, (total.shape[0], 1), 0) < live_ref[0]
    out_ref[...] = jnp.where(keep, total, 0.0).astype(BF16)


def local(x, live, listed, counts, cotangent, q, qb, sw, nb, ob):
    x, lists, counts, up = x[0], listed[0, 0], counts[0], cotangent[0]
    live = live.reshape(1)
    rows, width = x.shape
    hidden = q.shape[1]
    reach, block_count = lists.shape
    block = rows // block_count
    qb, ob = qb[None], ob[None]
    place = (lax.axis_index("dom") % LINE).astype(jnp.int32).reshape(1)
    keep = lax.broadcasted_iota(jnp.int32, (rows, 1), 0) < live[0]
    marked = jnp.where(keep, x, jnp.asarray(DEAD, BF16))
    row = jnp.pad(lists[:, 1], (0, 128 - reach))[None]
    steps = range(1, LINE)
    one, two = ((block, width), BF16), ((rows, width), BF16)

    def pick(offset, metas, held, after):
        return call(
            lambda *r: pick_kernel(block, offset, *r),
            [one] * len(steps),
            (place, *metas, held, *after),
            [SMEM] * (1 + len(steps)) + [VMEM] + [HELD] * len(after),
        )

    below = swap_rows(marked, LINE)
    far_metas = [straight(row, d, back=True) for d in steps]
    near_metas = [along(row, -d) for d in steps]
    same = swap_rows(marked, 0)
    far_sent = pick(far, far_metas, marked, (same, *near_metas))
    got_far = [straight(b, d) for d, b in zip(steps, far_sent)]
    tiles, tiles_t, self_pre = call(
        lambda *r: tiles_kernel(block, *r),
        [((rows, reach * block), BF16), ((reach * block, rows), BF16), ((rows, width), F32)],
        (place, lists, counts, x, sw),
        [SMEM] * 2 + [VMEM] * 3,
        flops=2 * rows * width * width,
    )
    near_sent = pick(near, near_metas, below, (tiles,))
    got_near = [along(b, d) for d, b in zip(steps, near_sent)]
    split = 1 + LINE

    def message(first, last, ins, specs):
        size = last - first
        return call(
            lambda *r: message_kernel(block, first, last, *r),
            [((size * block, hidden), BF16), ((rows, hidden), F32), ((rows, 128), F32)],
            ins,
            specs,
            flops=2 * size * block * hidden * (width + rows),
        )

    msg_a, acc, deg = message(
        0, split, (lists, same, below, *got_far, q, qb, tiles), [SMEM] + [VMEM] * 8
    )
    msg_b, acc, deg = message(split, reach, (*got_near, q, qb, tiles, acc, deg), [VMEM] * 8)
    emb, gself, gpool = call(
        layer_kernel,
        [two, ((rows, width), F32), ((rows, hidden), BF16)],
        (live, acc, deg, self_pre, up, sw, nb, ob),
        [SMEM] + [VMEM] * 7,
        scratch=[pltpu.VMEM((rows, width), F32)],
        flops=2 * rows * width * (2 * hidden + width),
    )

    def back(kernel, outs, first, last, msg, after, lead=()):
        size = last - first
        return call(
            kernel,
            outs,
            (*lead, tiles_t, gpool, msg, q, after),
            [SMEM] * len(lead) + [VMEM] * 4 + [HELD],
            scratch=[pltpu.VMEM((size * block, hidden), BF16)],
            flops=2 * size * block * hidden * (width + rows),
        )

    near_back = back(
        lambda *r: back_kernel(block, split, reach, 0, *r), [one] * 3, split, reach, msg_b, gself
    )
    back_near = [along(b, -d) for d, b in zip(steps, near_back)]
    far_back = back(
        lambda *r: back_kernel(block, 2, split, 2, *r), [one] * 3, 2, split, msg_a, near_back[0]
    )
    back_far = [straight(b, d, back=True) for d, b in zip(steps, far_back)]
    own_same, own_below = back(
        lambda *r: back_own_kernel(block, *r), [two, one], 0, 2, msg_a, far_back[0], (lists,)
    )
    g_same = swap_rows(own_same, 0)
    total = pltpu.VMEM((rows, width), F32)
    (sum_below,) = call(
        lambda *r: sum_near_kernel(block, *r),
        [two],
        (place, lists, *near_metas, own_below, *back_near),
        [SMEM] * 5 + [VMEM] * 4,
        scratch=[total],
        flops=20 * MICROSECOND,
    )
    g_below = swap_rows(sum_below, -LINE)
    (placed,) = call(
        lambda *r: place_kernel(block, *r),
        [((rows, width), F32)],
        (place, *far_metas, gself, *back_far),
        [SMEM] * 4 + [VMEM] * 4,
        flops=20 * MICROSECOND,
    )
    (grad,) = call(finish_kernel, [two], (live, placed, g_same, g_below), [SMEM] + [VMEM] * 3)
    return emb[None], grad[None]


def solution(mesh):
    data = P("side", "dom", None)
    return jax.shard_map(
        local,
        mesh=mesh,
        in_specs=(
            data,
            P("side", "dom"),
            P("side", "dom", None, None),
            data,
            data,
            P(),
            P(),
            P(),
            P(),
            P(),
        ),
        out_specs=(data, data),
        check_vma=False,
    )
```

```python
import jax
import jax.numpy as jnp
from jax import lax
from jax.experimental import pallas as pl
from jax.experimental.pallas import tpu as pltpu
from jax.sharding import PartitionSpec as P

EPS = 1e-06
DEAD = 16384.0
LIMIT = 8192.0
MICROSECOND = 10**9
LINE = 4
F32 = jnp.float32
BF16 = jnp.bfloat16
VMEM = pl.BlockSpec(memory_space=pltpu.VMEM)
HELD = pl.BlockSpec(memory_space=pl.ANY)
SMEM = pl.BlockSpec(memory_space=pltpu.SMEM)


def dot(a, b, ca=1, cb=0):
    return lax.dot_general(a, b, (((ca,), (cb,)), ((), ())), preferred_element_type=F32)


def call(kernel, outs, ins, in_specs=None, scratch=(), limit=24, flops=0):
    return pl.pallas_call(
        kernel,
        out_shape=[jax.ShapeDtypeStruct(s, d) for s, d in outs],
        in_specs=in_specs or [VMEM] * len(ins),
        out_specs=[VMEM] * len(outs),
        scratch_shapes=list(scratch),
        compiler_params=pltpu.CompilerParams(vmem_limit_bytes=limit << 20),
        cost_estimate=pl.CostEstimate(flops=flops, bytes_accessed=1 << 20, transcendentals=0),
    )(*ins)


def swap_rows(x, shift):
    count = lax.axis_size("dom")
    pairs = [
        (s * count + j, (1 - s) * count + (j + shift) % count)
        for s in range(2)
        for j in range(count)
    ]
    return lax.ppermute(x, ("side", "dom"), pairs)


def along(x, d):
    count = lax.axis_size("dom")
    pairs = [(j, j // LINE * LINE + (j + d) % LINE) for j in range(count)]
    return lax.ppermute(x, "dom", pairs)


def straight_back(x, d):
    count = lax.axis_size("dom")
    pairs = []
    for s in range(2):
        for j in range(count):
            to = j + d if j % LINE + d < LINE else j + d + LINE
            pairs.append(((1 - s) * count + to % count, s * count + j))
    return lax.ppermute(x, ("side", "dom"), pairs)


def near(p, d):
    return jnp.where(p >= d, d + LINE, d)


def far(p, d):
    return jnp.where(p >= d, d, d + LINE)


def at_block(index, block):
    return pl.ds(pl.multiple_of(index * block, block), block)


def pick_near_kernel(block, place_ref, m1, m2, m3, rows_ref, _, *outs):
    for d, (meta, out) in enumerate(zip((m1, m2, m3), outs), 1):
        p = lax.rem(place_ref[0] + d, LINE)
        out[...] = rows_ref[at_block(meta[0, near(p, d)], block), :]


def pick_far_kernel(block, place_ref, m1, m2, m3, same_ref, below_ref, *outs):
    for d, (meta, out) in enumerate(zip((m1, m2, m3), outs), 1):
        p = lax.rem(place_ref[0] + d, LINE)
        at = at_block(meta[0, far(p, d)], block)

        @pl.when(p >= d)
        def _():
            out[...] = same_ref[at, :]

        @pl.when(p < d)
        def _():
            out[...] = below_ref[at, :]


def slots(p):
    return [0, LINE] + [near(p, d) for d in range(1, LINE)] + [far(p, d) for d in range(1, LINE)]


def tiles_kernel(block, place_ref, lists_ref, counts_ref, x_ref, sw_ref, tiles_ref, tiles_t_ref, self_ref):
    for i, o in enumerate(slots(place_ref[0])):
        first, second = lists_ref[o, 0], lists_ref[o, 1]
        at = pl.ds(pl.multiple_of((o * 2 + second) * block, block), block)
        tile = (counts_ref[:, at] * (first + second)).astype(F32)
        tiles_ref[:, i * block : (i + 1) * block] = tile.astype(BF16)
        tiles_t_ref[i * block : (i + 1) * block, :] = tile.T.astype(BF16)
    self_ref[...] = dot(x_ref[...], sw_ref[...])


def message_kernel(block, first, last, *refs):
    size = last - first
    if first == 0:
        lists_ref, same_ref, below_ref = refs[:3]
        held = [same_ref[at_block(lists_ref[0, 1], block), :]]
        held += [below_ref[at_block(lists_ref[LINE, 1], block), :]]
        refs = refs[3:]
        held += [b[...] for b in refs[: size - 2]]
        refs = refs[size - 2 :]
    else:
        held = [b[...] for b in refs[:size]]
        refs = refs[size:]
    q_ref, qb_ref, tiles_ref = refs[:3]
    acc_in, deg_in = refs[3:5] if first else (None, None)
    msg_ref, acc_ref, deg_ref = refs[-3:]
    x = jnp.concatenate(held, axis=0)
    keep = x[:, :128].astype(F32) < LIMIT
    tiles = tiles_ref[:, first * block : last * block]
    deg = dot(tiles, jnp.where(keep, 1.0, 0.0).astype(BF16))
    deg_ref[...] = deg + deg_in[...] if first else deg
    keep = keep[:, :1]
    hidden = q_ref.shape[1]
    step = 512
    for n in range(hidden // step):
        cols = slice(n * step, (n + 1) * step)
        pre = dot(x, q_ref[:, cols]) + qb_ref[:, cols]
        msg = jnp.where(keep, jnp.maximum(pre, 0.0), 0.0).astype(BF16)
        msg_ref[:, cols] = msg
        acc = dot(tiles, msg)
        acc_ref[:, cols] = acc + acc_in[:, cols] if first else acc


def layer_kernel(
    block, live_ref, got_ref, q_ref, qb_ref, tiles_ref, acc_ref, deg_ref, self_ref, up_ref, nb_ref, ob_ref, tt_ref,
    msg_ref, g_ref, gpool_ref, pre_ref, last_ref, near1, near2, near3, pooled_ref, gn_ref,
):
    rows, width = self_ref.shape
    hidden = nb_ref.shape[0]
    step = 512
    x = got_ref[...]
    keep = x[:, :128].astype(F32) < LIMIT
    tiles = tiles_ref[:, -block:]
    deg = deg_ref[...] + dot(tiles, jnp.where(keep, 1.0, 0.0).astype(BF16))
    inv_deg = 1.0 / (1.0 + deg[:, :1])
    keep = keep[:, :1]
    for n in range(hidden // step):
        cols = slice(n * step, (n + 1) * step)
        pre = dot(x, q_ref[:, cols]) + qb_ref[:, cols]
        msg = jnp.where(keep, jnp.maximum(pre, 0.0), 0.0).astype(BF16)
        last_ref[:, cols] = msg
        pooled_ref[:, cols] = ((acc_ref[:, cols] + dot(tiles, msg)) * inv_deg).astype(BF16)
    pooled = pooled_ref[...]
    for n in range(width // step):
        cols = slice(n * step, (n + 1) * step)
        pre_ref[:, cols] = self_ref[:, cols] + dot(pooled, nb_ref[:, cols]) + ob_ref[:, cols]
    pre = pre_ref[...]
    act = jnp.maximum(pre, 0.0)
    inv = lax.rsqrt(jnp.mean(act * act, axis=1, keepdims=True) + EPS)
    keep = lax.broadcasted_iota(jnp.int32, (rows, 1), 0) < live_ref[0]
    up = jnp.where(keep, up_ref[...].astype(F32), 0.0)
    inner = jnp.sum(up * act, axis=1, keepdims=True) / width
    g = inv * up - act * (inv * inv * inv * inner)
    g = jnp.where(pre > 0, g, 0.0).astype(BF16)
    g_ref[...] = g
    for n in range(hidden // step):
        cols = slice(n * step, (n + 1) * step)
        gpool_ref[:, cols] = (dot(g, nb_ref[cols, :], 1, 1) * inv_deg).astype(BF16)

    def store(cols, part):
        for i, out in enumerate((near1, near2, near3)):
            out[:, cols] = part[i * block : (i + 1) * block].astype(BF16)

    back_dot(2 * block, tt_ref, gpool_ref, [msg_ref[2 * block :, :]], q_ref, gn_ref, store)


def back_dot(first, tt_ref, gpool_ref, messages, q_ref, gn_ref, store):
    rows = gn_ref.shape[0]
    tt = tt_ref[first : first + rows, :]
    step = 512
    for n in range(gpool_ref.shape[1] // step):
        cols = slice(n * step, (n + 1) * step)
        live = jnp.concatenate([m[:, cols] for m in messages], axis=0).astype(F32) > 0
        gn_ref[:, cols] = jnp.where(live, dot(tt, gpool_ref[:, cols]), 0.0).astype(BF16)
    gn = gn_ref[...]
    for n in range(q_ref.shape[0] // step):
        cols = slice(n * step, (n + 1) * step)
        store(cols, dot(gn, q_ref[cols, :], 1, 1))


def back_far_kernel(block, place_ref, lists_ref, tt_ref, gpool_ref, early_ref, last_ref, q_ref, _, *refs):
    outs, gn_ref = refs[:-1], refs[-1]
    width = q_ref.shape[0]

    def store(cols, part):
        for i, out in enumerate(outs):
            out[:, cols] = part[i * block : (i + 1) * block].astype(BF16)

    for d, out in enumerate(outs, 1):
        which = lists_ref[far(place_ref[0], d), 1].astype(F32)
        out[:, width:] = jnp.full((block, 128), which, F32).astype(BF16)
    messages = [early_ref[...], last_ref[...]]
    back_dot((1 + LINE) * block, tt_ref, gpool_ref, messages, q_ref, gn_ref, store)


def back_own_kernel(
    block, lists_ref, live_ref, tt_ref, gpool_ref, msg_ref, q_ref, g_ref, sw_ref, pre_ref, _,
    same_ref, below_ref, gself_ref, emb_ref, gn_ref,
):
    same_ref[...] = jnp.zeros_like(same_ref)
    at = at_block(lists_ref[0, 1], block)

    def store(cols, part):
        same_ref[at, cols] = part[:block].astype(BF16)
        below_ref[:, cols] = part[block:].astype(BF16)

    back_dot(0, tt_ref, gpool_ref, [msg_ref[: 2 * block, :]], q_ref, gn_ref, store)
    rows, width = pre_ref.shape
    step = 512
    for n in range(width // step):
        cols = slice(n * step, (n + 1) * step)
        gself_ref[:, cols] = dot(g_ref[...], sw_ref[cols, :], 1, 1)
    act = jnp.maximum(pre_ref[...], 0.0)
    inv = lax.rsqrt(jnp.mean(act * act, axis=1, keepdims=True) + EPS)
    keep = lax.broadcasted_iota(jnp.int32, (rows, 1), 0) < live_ref[0]
    emb_ref[...] = jnp.where(keep, act * inv, 0.0).astype(BF16)


def sum_near_kernel(block, place_ref, lists_ref, m1, m2, m3, own_ref, d1, d2, d3, out_ref, total):
    total[...] = jnp.zeros_like(total)
    total[at_block(lists_ref[LINE, 1], block), :] = own_ref[...].astype(F32)
    for d, (meta, part) in enumerate(zip((m1, m2, m3), (d1, d2, d3)), 1):
        p = lax.rem(place_ref[0] + d, LINE)
        total[at_block(meta[0, near(p, d)], block), :] += part[...].astype(F32)
    out_ref[...] = total[...].astype(BF16)


def place_kernel(gself_ref, c1, c2, c3, total_ref):
    block, width = c1.shape[0], gself_ref.shape[1]
    first, second = gself_ref[:block, :], gself_ref[block:, :]
    for part in (c1, c2, c3):
        grad = part[:, :width].astype(F32)
        late = part[:, width : width + 1].astype(F32) > 0.5
        first += jnp.where(late, 0.0, grad)
        second += jnp.where(late, grad, 0.0)
    total_ref[:block, :] = first
    total_ref[block:, :] = second


def finish_kernel(live_ref, total_ref, same_ref, below_ref, out_ref):
    total = total_ref[...] + same_ref[...].astype(F32) + below_ref[...].astype(F32)
    keep = lax.broadcasted_iota(jnp.int32, (total.shape[0], 1), 0) < live_ref[0]
    out_ref[...] = jnp.where(keep, total, 0.0).astype(BF16)


def local(x, live, listed, counts, cotangent, q, qb, sw, nb, ob):
    x, lists, counts, up = x[0], listed[0, 0], counts[0], cotangent[0]
    live = live.reshape(1)
    rows, width = x.shape
    hidden = q.shape[1]
    reach, block_count = lists.shape
    block = rows // block_count
    qb, ob = qb[None], ob[None]
    place = (lax.axis_index("dom") % LINE).astype(jnp.int32).reshape(1)
    keep = lax.broadcasted_iota(jnp.int32, (rows, 1), 0) < live[0]
    marked = jnp.where(keep, x, jnp.asarray(DEAD, BF16))
    row = jnp.pad(lists[:, 1], (0, 128 - reach))[None]
    steps = range(1, LINE)
    one, two = ((block, width), BF16), ((rows, width), BF16)

    below = swap_rows(marked, LINE)
    same = swap_rows(marked, 0)
    metas = [along(row, -d) for d in steps]
    later, *metas = lax.optimization_barrier((marked, *metas))
    below2 = swap_rows(later, 2 * LINE)
    scalars = [SMEM] * (1 + len(steps))
    tiles, tiles_t, self_pre = call(
        lambda *r: tiles_kernel(block, *r),
        [((rows, reach * block), BF16), ((reach * block, rows), BF16), ((rows, width), F32)],
        (place, lists, counts, x, sw),
        [SMEM] * 2 + [VMEM] * 3,
        flops=2 * rows * width * width,
    )
    sent = call(
        lambda *r: pick_near_kernel(block, *r),
        [one] * len(steps),
        (place, *metas, below, tiles),
        scalars + [VMEM, HELD],
    )
    got_near = [along(b, d) for d, b in zip(steps, sent)]
    sent = call(
        lambda *r: pick_far_kernel(block, *r),
        [one] * len(steps),
        (place, *metas, same, below2),
        scalars + [VMEM] * 2,
    )
    got_far = [along(b, d) for d, b in zip(steps, sent)]
    split = 1 + LINE

    def message(first, last, ins, specs):
        size = last - first
        return call(
            lambda *r: message_kernel(block, first, last, *r),
            [((size * block, hidden), BF16), ((rows, hidden), F32), ((rows, 128), F32)],
            ins,
            specs,
            flops=2 * size * block * hidden * (width + rows),
        )

    msg_a, acc, deg = message(
        0, split, (lists, same, below, *got_near, q, qb, tiles), [SMEM] + [VMEM] * 8
    )
    msg_b, acc, deg = message(
        split, reach - 1, (*got_far[:-1], q, qb, tiles, acc, deg), [VMEM] * (5 + len(steps) - 1)
    )
    gn = pltpu.VMEM((3 * block, hidden), BF16)
    g, gpool, pre, msg_c, *near_back = call(
        lambda *r: layer_kernel(block, *r),
        [two, ((rows, hidden), BF16), ((rows, width), F32), ((block, hidden), BF16)] + [one] * 3,
        (live, got_far[-1], q, qb, tiles, acc, deg, self_pre, up, nb, ob, tiles_t, msg_a),
        [SMEM] + [VMEM] * 12,
        scratch=[pltpu.VMEM((rows, hidden), BF16), gn],
        flops=8 * MICROSECOND,
    )
    back_near = [along(b, -d) for d, b in zip(steps, near_back)]
    far_back = call(
        lambda *r: back_far_kernel(block, *r),
        [((block, width + 128), BF16)] * 3,
        (place, lists, tiles_t, gpool, msg_b, msg_c, q, near_back[0]),
        [SMEM] * 2 + [VMEM] * 5 + [HELD],
        scratch=[gn],
        flops=2 * MICROSECOND,
    )
    back_far = [straight_back(b, d) for d, b in zip(steps, far_back)]
    own_same, own_below, gself, emb = call(
        lambda *r: back_own_kernel(block, *r),
        [two, one, ((rows, width), F32), two],
        (lists, live, tiles_t, gpool, msg_a, q, g, sw, pre, far_back[0]),
        [SMEM] * 2 + [VMEM] * 7 + [HELD],
        scratch=[pltpu.VMEM((2 * block, hidden), BF16)],
        flops=3 * MICROSECOND,
    )
    g_same = swap_rows(own_same, 0)
    total = pltpu.VMEM((rows, width), F32)
    (sum_below,) = call(
        lambda *r: sum_near_kernel(block, *r),
        [two],
        (place, lists, *metas, own_below, *back_near),
        [SMEM] * 5 + [VMEM] * 4,
        scratch=[total],
        flops=20 * MICROSECOND,
    )
    g_below = swap_rows(sum_below, -LINE)
    (placed,) = call(
        place_kernel,
        [((rows, width), F32)],
        (gself, *back_far),
        [VMEM] * 4,
        flops=20 * MICROSECOND,
    )
    (grad,) = call(finish_kernel, [two], (live, placed, g_same, g_below), [SMEM] + [VMEM] * 3)
    return emb[None], grad[None]


def solution(mesh):
    data = P("side", "dom", None)
    return jax.shard_map(
        local,
        mesh=mesh,
        in_specs=(
            data,
            P("side", "dom"),
            P("side", "dom", None, None),
            data,
            data,
            P(),
            P(),
            P(),
            P(),
            P(),
        ),
        out_specs=(data, data),
        check_vma=False,
    )
```

```python
import jax
import jax.numpy as jnp
from jax import lax
from jax.experimental import pallas as pl
from jax.experimental.pallas import tpu as pltpu
from jax.sharding import PartitionSpec as P

EPS = 1e-06
DEAD = 16384.0
LIMIT = 8192.0
MICROSECOND = 10**9
FAR_ORDER = (1, 3, 2)
LINE = 4
F32 = jnp.float32
BF16 = jnp.bfloat16
VMEM = pl.BlockSpec(memory_space=pltpu.VMEM)
HELD = pl.BlockSpec(memory_space=pl.ANY)
SMEM = pl.BlockSpec(memory_space=pltpu.SMEM)


def dot(a, b, ca=1, cb=0):
    return lax.dot_general(a, b, (((ca,), (cb,)), ((), ())), preferred_element_type=F32)


def call(kernel, outs, ins, in_specs=None, scratch=(), limit=24, flops=0):
    return pl.pallas_call(
        kernel,
        out_shape=[jax.ShapeDtypeStruct(s, d) for s, d in outs],
        in_specs=in_specs or [VMEM] * len(ins),
        out_specs=[VMEM] * len(outs),
        scratch_shapes=list(scratch),
        compiler_params=pltpu.CompilerParams(vmem_limit_bytes=limit << 20),
        cost_estimate=pl.CostEstimate(flops=flops, bytes_accessed=1 << 20, transcendentals=0),
    )(*ins)


def swap_rows(x, shift):
    count = lax.axis_size("dom")
    pairs = [
        (s * count + j, (1 - s) * count + (j + shift) % count)
        for s in range(2)
        for j in range(count)
    ]
    return lax.ppermute(x, ("side", "dom"), pairs)


def along(x, d):
    count = lax.axis_size("dom")
    pairs = [(j, j // LINE * LINE + (j + d) % LINE) for j in range(count)]
    return lax.ppermute(x, "dom", pairs)


def straight_back(x, d):
    count = lax.axis_size("dom")
    pairs = []
    for s in range(2):
        for j in range(count):
            to = j + d if j % LINE + d < LINE else j + d + LINE
            pairs.append(((1 - s) * count + to % count, s * count + j))
    return lax.ppermute(x, ("side", "dom"), pairs)


def near(p, d):
    return jnp.where(p >= d, d + LINE, d)


def far(p, d):
    return jnp.where(p >= d, d, d + LINE)


def at_block(index, block):
    return pl.ds(pl.multiple_of(index * block, block), block)


def pick_near_kernel(block, place_ref, m1, m2, m3, rows_ref, _, *outs):
    for d, (meta, out) in enumerate(zip((m1, m2, m3), outs), 1):
        p = lax.rem(place_ref[0] + d, LINE)
        out[...] = rows_ref[at_block(meta[0, near(p, d)], block), :]


def pick_far_kernel(block, place_ref, m1, m2, m3, same_ref, below_ref, *outs):
    for d, (meta, out) in enumerate(zip((m1, m2, m3), outs), 1):
        p = lax.rem(place_ref[0] + d, LINE)
        at = at_block(meta[0, far(p, d)], block)

        @pl.when(p >= d)
        def _():
            out[...] = same_ref[at, :]

        @pl.when(p < d)
        def _():
            out[...] = below_ref[at, :]


def slots(p):
    return [0, LINE] + [near(p, d) for d in range(1, LINE)] + [far(p, d) for d in FAR_ORDER]


def tiles_kernel(block, place_ref, lists_ref, counts_ref, x_ref, sw_ref, tiles_ref, tiles_t_ref, self_ref):
    for i, o in enumerate(slots(place_ref[0])):
        first, second = lists_ref[o, 0], lists_ref[o, 1]
        at = pl.ds(pl.multiple_of((o * 2 + second) * block, block), block)
        tile = (counts_ref[:, at] * (first + second)).astype(F32)
        tiles_ref[:, i * block : (i + 1) * block] = tile.astype(BF16)
        tiles_t_ref[i * block : (i + 1) * block, :] = tile.T.astype(BF16)
    self_ref[...] = dot(x_ref[...], sw_ref[...])


def message_kernel(block, first, last, *refs):
    size = last - first
    if first == 0:
        lists_ref, same_ref, below_ref = refs[:3]
        held = [same_ref[at_block(lists_ref[0, 1], block), :]]
        held += [below_ref[at_block(lists_ref[LINE, 1], block), :]]
        refs = refs[3:]
        held += [b[...] for b in refs[: size - 2]]
        refs = refs[size - 2 :]
    else:
        held = [b[...] for b in refs[:size]]
        refs = refs[size:]
    q_ref, qb_ref, tiles_ref = refs[:3]
    acc_in, deg_in = refs[3:5] if first else (None, None)
    msg_ref, acc_ref, deg_ref = refs[-3:]
    x = jnp.concatenate(held, axis=0)
    keep = x[:, :128].astype(F32) < LIMIT
    tiles = tiles_ref[:, first * block : last * block]
    deg = dot(tiles, jnp.where(keep, 1.0, 0.0).astype(BF16))
    deg_ref[...] = deg + deg_in[...] if first else deg
    keep = keep[:, :1]
    hidden = q_ref.shape[1]
    step = 512
    for n in range(hidden // step):
        cols = slice(n * step, (n + 1) * step)
        pre = dot(x, q_ref[:, cols]) + qb_ref[:, cols]
        msg = jnp.where(keep, jnp.maximum(pre, 0.0), 0.0).astype(BF16)
        msg_ref[:, cols] = msg
        acc = dot(tiles, msg)
        acc_ref[:, cols] = acc + acc_in[:, cols] if first else acc


def layer_kernel(
    block, live_ref, place_ref, lists_ref, got_ref, q_ref, qb_ref, tiles_ref, acc_ref, deg_ref, self_ref, up_ref, nb_ref, ob_ref, tt_ref,
    early_ref, g_ref, gpool_ref, pre_ref, out1, out2, out3, pooled_ref, gn_ref, last_ref,
):
    rows, width = self_ref.shape
    hidden = nb_ref.shape[0]
    step = 512
    x = got_ref[...]
    keep = x[:, :128].astype(F32) < LIMIT
    tiles = tiles_ref[:, -block:]
    deg = deg_ref[...] + dot(tiles, jnp.where(keep, 1.0, 0.0).astype(BF16))
    inv_deg = 1.0 / (1.0 + deg[:, :1])
    keep = keep[:, :1]
    for n in range(hidden // step):
        cols = slice(n * step, (n + 1) * step)
        pre = dot(x, q_ref[:, cols]) + qb_ref[:, cols]
        msg = jnp.where(keep, jnp.maximum(pre, 0.0), 0.0).astype(BF16)
        last_ref[:, cols] = msg
        pooled_ref[:, cols] = ((acc_ref[:, cols] + dot(tiles, msg)) * inv_deg).astype(BF16)
    pooled = pooled_ref[...]
    for n in range(width // step):
        cols = slice(n * step, (n + 1) * step)
        pre_ref[:, cols] = self_ref[:, cols] + dot(pooled, nb_ref[:, cols]) + ob_ref[:, cols]
    pre = pre_ref[...]
    act = jnp.maximum(pre, 0.0)
    inv = lax.rsqrt(jnp.mean(act * act, axis=1, keepdims=True) + EPS)
    keep = lax.broadcasted_iota(jnp.int32, (rows, 1), 0) < live_ref[0]
    up = jnp.where(keep, up_ref[...].astype(F32), 0.0)
    inner = jnp.sum(up * act, axis=1, keepdims=True) / width
    g = inv * up - act * (inv * inv * inv * inner)
    g = jnp.where(pre > 0, g, 0.0).astype(BF16)
    g_ref[...] = g
    for n in range(hidden // step):
        cols = slice(n * step, (n + 1) * step)
        gpool_ref[:, cols] = (dot(g, nb_ref[cols, :], 1, 1) * inv_deg).astype(BF16)

    outs = (out1, out2, out3)

    def store(cols, part):
        for i, out in enumerate(outs):
            out[:, cols] = part[i * block : (i + 1) * block].astype(BF16)

    for d, out in zip(FAR_ORDER, outs):
        which = lists_ref[far(place_ref[0], d), 1].astype(F32)
        out[:, width:] = jnp.full((block, 128), which, F32).astype(BF16)
    first = (1 + LINE) * block
    back_dot(first, tt_ref, gpool_ref, [early_ref[...], last_ref[...]], q_ref, gn_ref, store)


def back_dot(first, tt_ref, gpool_ref, messages, q_ref, gn_ref, store):
    rows = gn_ref.shape[0]
    tt = tt_ref[first : first + rows, :]
    step = 512
    for n in range(gpool_ref.shape[1] // step):
        cols = slice(n * step, (n + 1) * step)
        live = jnp.concatenate([m[:, cols] for m in messages], axis=0).astype(F32) > 0
        gn_ref[:, cols] = jnp.where(live, dot(tt, gpool_ref[:, cols]), 0.0).astype(BF16)
    gn = gn_ref[...]
    for n in range(q_ref.shape[0] // step):
        cols = slice(n * step, (n + 1) * step)
        store(cols, dot(gn, q_ref[cols, :], 1, 1))


def back_near_kernel(block, tt_ref, gpool_ref, msg_ref, q_ref, _, *refs):
    outs, gn_ref = refs[:-1], refs[-1]

    def store(cols, part):
        for i, out in enumerate(outs):
            out[:, cols] = part[i * block : (i + 1) * block].astype(BF16)

    back_dot(2 * block, tt_ref, gpool_ref, [msg_ref[2 * block :, :]], q_ref, gn_ref, store)


def back_own_kernel(
    block, lists_ref, live_ref, tt_ref, gpool_ref, msg_ref, q_ref, g_ref, sw_ref, pre_ref, _,
    same_ref, below_ref, gself_ref, emb_ref, gn_ref,
):
    same_ref[...] = jnp.zeros_like(same_ref)
    at = at_block(lists_ref[0, 1], block)

    def store(cols, part):
        same_ref[at, cols] = part[:block].astype(BF16)
        below_ref[:, cols] = part[block:].astype(BF16)

    back_dot(0, tt_ref, gpool_ref, [msg_ref[: 2 * block, :]], q_ref, gn_ref, store)
    rows, width = pre_ref.shape
    step = 512
    for n in range(width // step):
        cols = slice(n * step, (n + 1) * step)
        gself_ref[:, cols] = dot(g_ref[...], sw_ref[cols, :], 1, 1)
    act = jnp.maximum(pre_ref[...], 0.0)
    inv = lax.rsqrt(jnp.mean(act * act, axis=1, keepdims=True) + EPS)
    keep = lax.broadcasted_iota(jnp.int32, (rows, 1), 0) < live_ref[0]
    emb_ref[...] = jnp.where(keep, act * inv, 0.0).astype(BF16)


def sum_near_kernel(block, place_ref, lists_ref, m1, m2, m3, own_ref, d1, d2, d3, out_ref, total):
    total[...] = jnp.zeros_like(total)
    total[at_block(lists_ref[LINE, 1], block), :] = own_ref[...].astype(F32)
    for d, (meta, part) in enumerate(zip((m1, m2, m3), (d1, d2, d3)), 1):
        p = lax.rem(place_ref[0] + d, LINE)
        total[at_block(meta[0, near(p, d)], block), :] += part[...].astype(F32)
    out_ref[...] = total[...].astype(BF16)


def place_kernel(gself_ref, c1, c2, c3, total_ref):
    block, width = c1.shape[0], gself_ref.shape[1]
    first, second = gself_ref[:block, :], gself_ref[block:, :]
    for part in (c1, c2, c3):
        grad = part[:, :width].astype(F32)
        late = part[:, width : width + 1].astype(F32) > 0.5
        first += jnp.where(late, 0.0, grad)
        second += jnp.where(late, grad, 0.0)
    total_ref[:block, :] = first
    total_ref[block:, :] = second


def finish_kernel(live_ref, total_ref, same_ref, below_ref, out_ref):
    total = total_ref[...] + same_ref[...].astype(F32) + below_ref[...].astype(F32)
    keep = lax.broadcasted_iota(jnp.int32, (total.shape[0], 1), 0) < live_ref[0]
    out_ref[...] = jnp.where(keep, total, 0.0).astype(BF16)


def local(x, live, listed, counts, cotangent, q, qb, sw, nb, ob):
    x, lists, counts, up = x[0], listed[0, 0], counts[0], cotangent[0]
    live = live.reshape(1)
    rows, width = x.shape
    hidden = q.shape[1]
    reach, block_count = lists.shape
    block = rows // block_count
    qb, ob = qb[None], ob[None]
    place = (lax.axis_index("dom") % LINE).astype(jnp.int32).reshape(1)
    keep = lax.broadcasted_iota(jnp.int32, (rows, 1), 0) < live[0]
    marked = jnp.where(keep, x, jnp.asarray(DEAD, BF16))
    row = jnp.pad(lists[:, 1], (0, 128 - reach))[None]
    steps = range(1, LINE)
    one, two = ((block, width), BF16), ((rows, width), BF16)

    below = swap_rows(marked, LINE)
    same = swap_rows(marked, 0)
    metas = [along(row, -d) for d in steps]
    later, *metas = lax.optimization_barrier((marked, *metas))
    below2 = swap_rows(later, 2 * LINE)
    scalars = [SMEM] * (1 + len(steps))
    tiles, tiles_t, self_pre = call(
        lambda *r: tiles_kernel(block, *r),
        [((rows, reach * block), BF16), ((reach * block, rows), BF16), ((rows, width), F32)],
        (place, lists, counts, x, sw),
        [SMEM] * 2 + [VMEM] * 3,
        flops=2 * rows * width * width,
    )
    sent = call(
        lambda *r: pick_near_kernel(block, *r),
        [one] * len(steps),
        (place, *metas, below, tiles),
        scalars + [VMEM, HELD],
    )
    got_near = [along(b, d) for d, b in zip(steps, sent)]
    sent = call(
        lambda *r: pick_far_kernel(block, *r),
        [one] * len(steps),
        (place, *metas, same, below2),
        scalars + [VMEM] * 2,
    )
    got_far = [along(sent[d - 1], d) for d in FAR_ORDER]
    split = 1 + LINE

    def message(first, last, ins, specs):
        size = last - first
        return call(
            lambda *r: message_kernel(block, first, last, *r),
            [((size * block, hidden), BF16), ((rows, hidden), F32), ((rows, 128), F32)],
            ins,
            specs,
            flops=2 * size * block * hidden * (width + rows),
        )

    msg_a, acc, deg = message(
        0, split, (lists, same, below, *got_near, q, qb, tiles), [SMEM] + [VMEM] * 8
    )
    msg_b, acc, deg = message(
        split, reach - 1, (*got_far[:-1], q, qb, tiles, acc, deg), [VMEM] * (5 + len(steps) - 1)
    )
    gn = pltpu.VMEM((3 * block, hidden), BF16)
    g, gpool, pre, *far_back = call(
        lambda *r: layer_kernel(block, *r),
        [two, ((rows, hidden), BF16), ((rows, width), F32)] + [((block, width + 128), BF16)] * 3,
        (
            live, place, lists, got_far[-1], q, qb, tiles, acc, deg, self_pre, up, nb, ob, tiles_t,
            msg_b,
        ),
        [SMEM] * 3 + [VMEM] * 12,
        scratch=[pltpu.VMEM((rows, hidden), BF16), gn, pltpu.VMEM((block, hidden), BF16)],
        flops=8 * MICROSECOND,
    )
    back_far = [straight_back(b, d) for d, b in zip(FAR_ORDER, far_back)]
    near_back = call(
        lambda *r: back_near_kernel(block, *r),
        [one] * 3,
        (tiles_t, gpool, msg_a, q, far_back[0]),
        [VMEM] * 4 + [HELD],
        scratch=[gn],
        flops=2 * MICROSECOND,
    )
    back_near = [along(b, -d) for d, b in zip(steps, near_back)]
    own_same, own_below, gself, emb = call(
        lambda *r: back_own_kernel(block, *r),
        [two, one, ((rows, width), F32), two],
        (lists, live, tiles_t, gpool, msg_a, q, g, sw, pre, near_back[0]),
        [SMEM] * 2 + [VMEM] * 7 + [HELD],
        scratch=[pltpu.VMEM((2 * block, hidden), BF16)],
        flops=3 * MICROSECOND,
    )
    g_same = swap_rows(own_same, 0)
    total = pltpu.VMEM((rows, width), F32)
    (sum_below,) = call(
        lambda *r: sum_near_kernel(block, *r),
        [two],
        (place, lists, *metas, own_below, *back_near),
        [SMEM] * 5 + [VMEM] * 4,
        scratch=[total],
        flops=20 * MICROSECOND,
    )
    g_below = swap_rows(sum_below, -LINE)
    (placed,) = call(
        place_kernel,
        [((rows, width), F32)],
        (gself, *back_far),
        [VMEM] * 4,
        flops=20 * MICROSECOND,
    )
    (grad,) = call(finish_kernel, [two], (live, placed, g_same, g_below), [SMEM] + [VMEM] * 3)
    return emb[None], grad[None]


def solution(mesh):
    data = P("side", "dom", None)
    return jax.shard_map(
        local,
        mesh=mesh,
        in_specs=(
            data,
            P("side", "dom"),
            P("side", "dom", None, None),
            data,
            data,
            P(),
            P(),
            P(),
            P(),
            P(),
        ),
        out_specs=(data, data),
        check_vma=False,
    )
```

```python
import jax
import jax.numpy as jnp
from jax import lax
from jax.experimental import pallas as pl
from jax.experimental.pallas import tpu as pltpu
from jax.sharding import PartitionSpec as P

EPS = 1e-06
DEAD = 16384.0
LIMIT = 8192.0
MICROSECOND = 10**9
LINE = 4
F32 = jnp.float32
BF16 = jnp.bfloat16
VMEM = pl.BlockSpec(memory_space=pltpu.VMEM)
HELD = pl.BlockSpec(memory_space=pl.ANY)
SMEM = pl.BlockSpec(memory_space=pltpu.SMEM)


def dot(a, b, ca=1, cb=0):
    return lax.dot_general(a, b, (((ca,), (cb,)), ((), ())), preferred_element_type=F32)


def call(kernel, outs, ins, in_specs=None, scratch=(), limit=24, flops=0):
    return pl.pallas_call(
        kernel,
        out_shape=[jax.ShapeDtypeStruct(s, d) for s, d in outs],
        in_specs=in_specs or [VMEM] * len(ins),
        out_specs=[VMEM] * len(outs),
        scratch_shapes=list(scratch),
        compiler_params=pltpu.CompilerParams(vmem_limit_bytes=limit << 20),
        cost_estimate=pl.CostEstimate(flops=flops, bytes_accessed=1 << 20, transcendentals=0),
    )(*ins)


def swap_rows(x, shift):
    count = lax.axis_size("dom")
    pairs = [
        (s * count + j, (1 - s) * count + (j + shift) % count)
        for s in range(2)
        for j in range(count)
    ]
    return lax.ppermute(x, ("side", "dom"), pairs)


def along(x, d):
    count = lax.axis_size("dom")
    pairs = [(j, j // LINE * LINE + (j + d) % LINE) for j in range(count)]
    return lax.ppermute(x, "dom", pairs)


def far_route(x, d):
    count = lax.axis_size("dom")
    pairs = []
    for s in range(2):
        for j in range(count):
            wraps = j % LINE < d
            to = j - d - LINE if wraps and d > 1 else j - d
            group = s if wraps and d == 1 else 1 - s
            pairs.append((s * count + j, group * count + to % count))
    return lax.ppermute(x, ("side", "dom"), pairs)


def near(p, d):
    return jnp.where(p >= d, d + LINE, d)


def far(p, d):
    return jnp.where(p >= d, d, d + LINE)


def at_block(index, block):
    return pl.ds(pl.multiple_of(index * block, block), block)


def pick_near_kernel(block, place_ref, m1, m2, m3, rows_ref, _, *outs):
    for d, (meta, out) in enumerate(zip((m1, m2, m3), outs), 1):
        p = lax.rem(place_ref[0] + d, LINE)
        out[...] = rows_ref[at_block(meta[0, near(p, d)], block), :]


def pick_far_kernel(block, place_ref, m1, m2, m3, same_ref, below_ref, *outs):
    for d, (meta, out) in enumerate(zip((m1, m2, m3), outs), 1):
        p = lax.rem(place_ref[0] + d, LINE)
        at = at_block(meta[0, far(p, d)], block)

        @pl.when(p >= d)
        def _():
            out[...] = same_ref[at, :]

        @pl.when(p < d)
        def _():
            out[...] = below_ref[at, :]


def slots(p):
    return [0, LINE] + [near(p, d) for d in range(1, LINE)] + [far(p, d) for d in range(1, LINE)]


def tiles_kernel(block, place_ref, lists_ref, counts_ref, x_ref, sw_ref, *refs):
    tiles_ref, tiles_t_ref, self_ref = refs[-3:]
    for i, o in enumerate(slots(place_ref[0])):
        first, second = lists_ref[o, 0], lists_ref[o, 1]
        at = pl.ds(pl.multiple_of((o * 2 + second) * block, block), block)
        tile = (counts_ref[:, at] * (first + second)).astype(F32)
        tiles_ref[:, i * block : (i + 1) * block] = tile.astype(BF16)
        tiles_t_ref[i * block : (i + 1) * block, :] = tile.T.astype(BF16)
    self_ref[...] = dot(x_ref[...], sw_ref[...])


def message_kernel(block, first, last, *refs):
    size = last - first
    if first == 0:
        lists_ref, same_ref, below_ref = refs[:3]
        held = [same_ref[at_block(lists_ref[0, 1], block), :]]
        held += [below_ref[at_block(lists_ref[LINE, 1], block), :]]
        refs = refs[3:]
        held += [b[...] for b in refs[: size - 2]]
        refs = refs[size - 2 :]
    else:
        held = [b[...] for b in refs[:size]]
        refs = refs[size:]
    q_ref, qb_ref, tiles_ref = refs[:3]
    acc_in, deg_in = refs[3:5] if first else (None, None)
    msg_ref, acc_ref, deg_ref = refs[-3:]
    x = jnp.concatenate(held, axis=0)
    keep = x[:, :128].astype(F32) < LIMIT
    tiles = tiles_ref[:, first * block : last * block]
    deg = dot(tiles, jnp.where(keep, 1.0, 0.0).astype(BF16))
    deg_ref[...] = deg + deg_in[...] if first else deg
    keep = keep[:, :1]
    hidden = q_ref.shape[1]
    step = 512
    for n in range(hidden // step):
        cols = slice(n * step, (n + 1) * step)
        pre = dot(x, q_ref[:, cols]) + qb_ref[:, cols]
        msg = jnp.where(keep, jnp.maximum(pre, 0.0), 0.0).astype(BF16)
        msg_ref[:, cols] = msg
        acc = dot(tiles, msg)
        acc_ref[:, cols] = acc + acc_in[:, cols] if first else acc


def layer_kernel(
    block, live_ref, got_a, got_b, q_ref, qb_ref, tiles_ref, acc_ref, deg_ref, self_ref, up_ref, nb_ref, ob_ref, tt_ref,
    msg_ref, g_ref, gpool_ref, pre_ref, last_ref, near1, near2, near3, pooled_ref, gn_ref,
):
    rows, width = self_ref.shape
    hidden = nb_ref.shape[0]
    step = 512
    x = jnp.concatenate([got_a[...], got_b[...]], axis=0)
    keep = x[:, :128].astype(F32) < LIMIT
    tiles = tiles_ref[:, -2 * block :]
    deg = deg_ref[...] + dot(tiles, jnp.where(keep, 1.0, 0.0).astype(BF16))
    inv_deg = 1.0 / (1.0 + deg[:, :1])
    keep = keep[:, :1]
    for n in range(hidden // step):
        cols = slice(n * step, (n + 1) * step)
        pre = dot(x, q_ref[:, cols]) + qb_ref[:, cols]
        msg = jnp.where(keep, jnp.maximum(pre, 0.0), 0.0).astype(BF16)
        last_ref[:, cols] = msg
        pooled_ref[:, cols] = ((acc_ref[:, cols] + dot(tiles, msg)) * inv_deg).astype(BF16)
    pooled = pooled_ref[...]
    for n in range(width // step):
        cols = slice(n * step, (n + 1) * step)
        pre_ref[:, cols] = self_ref[:, cols] + dot(pooled, nb_ref[:, cols]) + ob_ref[:, cols]
    pre = pre_ref[...]
    act = jnp.maximum(pre, 0.0)
    inv = lax.rsqrt(jnp.mean(act * act, axis=1, keepdims=True) + EPS)
    keep = lax.broadcasted_iota(jnp.int32, (rows, 1), 0) < live_ref[0]
    up = jnp.where(keep, up_ref[...].astype(F32), 0.0)
    inner = jnp.sum(up * act, axis=1, keepdims=True) / width
    g = inv * up - act * (inv * inv * inv * inner)
    g = jnp.where(pre > 0, g, 0.0).astype(BF16)
    g_ref[...] = g
    for n in range(hidden // step):
        cols = slice(n * step, (n + 1) * step)
        gpool_ref[:, cols] = (dot(g, nb_ref[cols, :], 1, 1) * inv_deg).astype(BF16)

    def store(cols, part):
        for i, out in enumerate((near1, near2, near3)):
            out[:, cols] = part[i * block : (i + 1) * block].astype(BF16)

    back_dot(2 * block, tt_ref, gpool_ref, [msg_ref[2 * block :, :]], q_ref, gn_ref, store)


def back_dot(first, tt_ref, gpool_ref, messages, q_ref, gn_ref, store):
    rows = gn_ref.shape[0]
    tt = tt_ref[first : first + rows, :]
    step = 512
    for n in range(gpool_ref.shape[1] // step):
        cols = slice(n * step, (n + 1) * step)
        live = jnp.concatenate([m[:, cols] for m in messages], axis=0).astype(F32) > 0
        gn_ref[:, cols] = jnp.where(live, dot(tt, gpool_ref[:, cols]), 0.0).astype(BF16)
    gn = gn_ref[...]
    for n in range(q_ref.shape[0] // step):
        cols = slice(n * step, (n + 1) * step)
        store(cols, dot(gn, q_ref[cols, :], 1, 1))


def back_far_kernel(block, tt_ref, gpool_ref, early_ref, last_ref, q_ref, _, *refs):
    outs, gn_ref = refs[:-1], refs[-1]

    def store(cols, part):
        for i, out in enumerate(outs):
            out[:, cols] = part[i * block : (i + 1) * block].astype(BF16)

    messages = [early_ref[...], last_ref[...]]
    back_dot((1 + LINE) * block, tt_ref, gpool_ref, messages, q_ref, gn_ref, store)


def back_own_kernel(
    block, lists_ref, live_ref, tt_ref, gpool_ref, msg_ref, q_ref, g_ref, sw_ref, pre_ref, _,
    same_ref, below_ref, gself_ref, emb_ref, gn_ref,
):
    same_ref[...] = jnp.zeros_like(same_ref)
    at = at_block(lists_ref[0, 1], block)

    def store(cols, part):
        same_ref[at, cols] = part[:block].astype(BF16)
        below_ref[:, cols] = part[block:].astype(BF16)

    back_dot(0, tt_ref, gpool_ref, [msg_ref[: 2 * block, :]], q_ref, gn_ref, store)
    rows, width = pre_ref.shape
    step = 512
    for n in range(width // step):
        cols = slice(n * step, (n + 1) * step)
        gself_ref[:, cols] = dot(g_ref[...], sw_ref[cols, :], 1, 1)
    act = jnp.maximum(pre_ref[...], 0.0)
    inv = lax.rsqrt(jnp.mean(act * act, axis=1, keepdims=True) + EPS)
    keep = lax.broadcasted_iota(jnp.int32, (rows, 1), 0) < live_ref[0]
    emb_ref[...] = jnp.where(keep, act * inv, 0.0).astype(BF16)


def sum_near_kernel(block, place_ref, lists_ref, f1, m1, m2, m3, own_ref, c1, d1, d2, d3, out_ref, total):
    total[...] = jnp.zeros_like(total)
    total[at_block(lists_ref[LINE, 1], block), :] = own_ref[...].astype(F32)
    for d, (meta, part) in enumerate(zip((m1, m2, m3), (d1, d2, d3)), 1):
        p = lax.rem(place_ref[0] + d, LINE)
        total[at_block(meta[0, near(p, d)], block), :] += part[...].astype(F32)

    @pl.when(place_ref[0] == LINE - 1)
    def _():
        total[at_block(f1[0, far(0, 1)], block), :] += c1[...].astype(F32)

    out_ref[...] = total[...].astype(BF16)


def place_kernel(block, place_ref, f1, f2, f3, gself_ref, c1, c2, c3, total_ref):
    total_ref[...] = gself_ref[...]
    for d, (meta, part) in enumerate(zip((f1, f2, f3), (c1, c2, c3)), 1):
        p = lax.rem(place_ref[0] + d, LINE)

        @pl.when((d > 1) | (p >= d))
        def _():
            total_ref[at_block(meta[0, far(p, d)], block), :] += part[...].astype(F32)


def finish_kernel(live_ref, total_ref, same_ref, below_ref, out_ref):
    total = total_ref[...] + same_ref[...].astype(F32) + below_ref[...].astype(F32)
    keep = lax.broadcasted_iota(jnp.int32, (total.shape[0], 1), 0) < live_ref[0]
    out_ref[...] = jnp.where(keep, total, 0.0).astype(BF16)


def local(x, live, listed, counts, cotangent, q, qb, sw, nb, ob):
    x, lists, counts, up = x[0], listed[0, 0], counts[0], cotangent[0]
    live = live.reshape(1)
    rows, width = x.shape
    hidden = q.shape[1]
    reach, block_count = lists.shape
    block = rows // block_count
    qb, ob = qb[None], ob[None]
    place = (lax.axis_index("dom") % LINE).astype(jnp.int32).reshape(1)
    keep = lax.broadcasted_iota(jnp.int32, (rows, 1), 0) < live[0]
    marked = jnp.where(keep, x, jnp.asarray(DEAD, BF16))
    row = jnp.pad(lists[:, 1], (0, 128 - reach))[None]
    steps = range(1, LINE)
    one, two = ((block, width), BF16), ((rows, width), BF16)

    below = swap_rows(marked, LINE)
    same = swap_rows(marked, 0)
    metas = [along(row, -d) for d in steps]
    later, row, *metas = lax.optimization_barrier((marked, row, *metas))
    below2 = swap_rows(later, 2 * LINE)
    far_metas = [far_route(row, d) for d in steps]
    scalars = [SMEM] * (1 + len(steps))
    tiles, tiles_t, self_pre = call(
        lambda *r: tiles_kernel(block, *r),
        [((rows, reach * block), BF16), ((reach * block, rows), BF16), ((rows, width), F32)],
        (place, lists, counts, x, sw, same, *far_metas),
        [SMEM] * 2 + [VMEM] * 3 + [HELD] * (1 + len(steps)),
        flops=2 * rows * width * width,
    )
    sent = call(
        lambda *r: pick_near_kernel(block, *r),
        [one] * len(steps),
        (place, *metas, below, tiles),
        scalars + [VMEM, HELD],
    )
    got_near = [along(b, d) for d, b in zip(steps, sent)]
    sent = call(
        lambda *r: pick_far_kernel(block, *r),
        [one] * len(steps),
        (place, *metas, same, below2),
        scalars + [VMEM] * 2,
    )
    got_far = [along(b, d) for d, b in zip(steps, sent)]
    split = 1 + LINE

    def message(first, last, ins, specs):
        size = last - first
        return call(
            lambda *r: message_kernel(block, first, last, *r),
            [((size * block, hidden), BF16), ((rows, hidden), F32), ((rows, 128), F32)],
            ins,
            specs,
            flops=2 * size * block * hidden * (width + rows),
        )

    msg_a, acc, deg = message(
        0, split, (lists, same, below, *got_near, q, qb, tiles), [SMEM] + [VMEM] * 8
    )
    msg_b, acc, deg = message(
        split, split + 1, (got_far[0], q, qb, tiles, acc, deg), [VMEM] * 6
    )
    gn = pltpu.VMEM((3 * block, hidden), BF16)
    g, gpool, pre, msg_c, *near_back = call(
        lambda *r: layer_kernel(block, *r),
        [two, ((rows, hidden), BF16), ((rows, width), F32), ((2 * block, hidden), BF16)] + [one] * 3,
        (live, *got_far[1:], q, qb, tiles, acc, deg, self_pre, up, nb, ob, tiles_t, msg_a),
        [SMEM] + [VMEM] * 13,
        scratch=[pltpu.VMEM((rows, hidden), BF16), gn],
        flops=8 * MICROSECOND,
    )
    back_near = [along(b, -d) for d, b in zip(steps, near_back)]
    gate = swap_rows(lax.optimization_barrier((row, near_back[0]))[0], 0)
    far_back = call(
        lambda *r: back_far_kernel(block, *r),
        [one] * 3,
        (tiles_t, gpool, msg_b, msg_c, q, gate),
        [VMEM] * 5 + [HELD],
        scratch=[gn],
        flops=2 * MICROSECOND,
    )
    back_far = [far_route(b, d) for d, b in zip(steps, far_back)]
    own_same, own_below, gself, emb = call(
        lambda *r: back_own_kernel(block, *r),
        [two, one, ((rows, width), F32), two],
        (lists, live, tiles_t, gpool, msg_a, q, g, sw, pre, far_back[0]),
        [SMEM] * 2 + [VMEM] * 7 + [HELD],
        scratch=[pltpu.VMEM((2 * block, hidden), BF16)],
        flops=3 * MICROSECOND,
    )
    g_same = swap_rows(own_same, 0)
    total = pltpu.VMEM((rows, width), F32)
    (sum_below,) = call(
        lambda *r: sum_near_kernel(block, *r),
        [two],
        (place, lists, far_metas[0], *metas, own_below, back_far[0], *back_near),
        [SMEM] * 6 + [VMEM] * 5,
        scratch=[total],
        flops=20 * MICROSECOND,
    )
    g_below = swap_rows(sum_below, -LINE)
    (placed,) = call(
        lambda *r: place_kernel(block, *r),
        [((rows, width), F32)],
        (place, *far_metas, gself, *back_far),
        [SMEM] * 4 + [VMEM] * 4,
        flops=20 * MICROSECOND,
    )
    (grad,) = call(finish_kernel, [two], (live, placed, g_same, g_below), [SMEM] + [VMEM] * 3)
    return emb[None], grad[None]


def solution(mesh):
    data = P("side", "dom", None)
    return jax.shard_map(
        local,
        mesh=mesh,
        in_specs=(
            data,
            P("side", "dom"),
            P("side", "dom", None, None),
            data,
            data,
            P(),
            P(),
            P(),
            P(),
            P(),
        ),
        out_specs=(data, data),
        check_vma=False,
    )
```

```python
import jax
import jax.numpy as jnp
from jax import lax
from jax.experimental import pallas as pl
from jax.experimental.pallas import tpu as pltpu
from jax.sharding import PartitionSpec as P

EPS = 1e-06
DEAD = 16384.0
LIMIT = 8192.0
MICROSECOND = 10**9
LINE = 4
F32 = jnp.float32
BF16 = jnp.bfloat16
VMEM = pl.BlockSpec(memory_space=pltpu.VMEM)
HELD = pl.BlockSpec(memory_space=pl.ANY)
SMEM = pl.BlockSpec(memory_space=pltpu.SMEM)


def dot(a, b, ca=1, cb=0):
    return lax.dot_general(a, b, (((ca,), (cb,)), ((), ())), preferred_element_type=F32)


def call(kernel, outs, ins, in_specs=None, scratch=(), limit=24, flops=0):
    return pl.pallas_call(
        kernel,
        out_shape=[jax.ShapeDtypeStruct(s, d) for s, d in outs],
        in_specs=in_specs or [VMEM] * len(ins),
        out_specs=[VMEM] * len(outs),
        scratch_shapes=list(scratch),
        compiler_params=pltpu.CompilerParams(vmem_limit_bytes=limit << 20),
        cost_estimate=pl.CostEstimate(flops=flops, bytes_accessed=1 << 20, transcendentals=0),
    )(*ins)


def swap_rows(x, shift):
    count = lax.axis_size("dom")
    pairs = [
        (s * count + j, (1 - s) * count + (j + shift) % count)
        for s in range(2)
        for j in range(count)
    ]
    return lax.ppermute(x, ("side", "dom"), pairs)


def along(x, d):
    count = lax.axis_size("dom")
    pairs = [(j, j // LINE * LINE + (j + d) % LINE) for j in range(count)]
    return lax.ppermute(x, "dom", pairs)


def straight_back(x, d):
    count = lax.axis_size("dom")
    pairs = []
    for s in range(2):
        for j in range(count):
            to = j + d if j % LINE + d < LINE else j + d + LINE
            pairs.append(((1 - s) * count + to % count, s * count + j))
    return lax.ppermute(x, ("side", "dom"), pairs)


def near(p, d):
    return jnp.where(p >= d, d + LINE, d)


def far(p, d):
    return jnp.where(p >= d, d, d + LINE)


def at_block(index, block):
    return pl.ds(pl.multiple_of(index * block, block), block)


def pick_near_kernel(block, place_ref, m1, m2, m3, rows_ref, *outs):
    for d, (meta, out) in enumerate(zip((m1, m2, m3), outs), 1):
        p = lax.rem(place_ref[0] + d, LINE)
        out[...] = rows_ref[at_block(meta[0, near(p, d)], block), :]


def pick_far_kernel(block, place_ref, m1, m2, m3, same_ref, below_ref, *outs):
    for d, (meta, out) in enumerate(zip((m1, m2, m3), outs), 1):
        p = lax.rem(place_ref[0] + d, LINE)
        at = at_block(meta[0, far(p, d)], block)

        @pl.when(p >= d)
        def _():
            out[...] = same_ref[at, :]

        @pl.when(p < d)
        def _():
            out[...] = below_ref[at, :]


def slots(p):
    return [0, LINE] + [near(p, d) for d in range(1, LINE)] + [far(p, d) for d in range(1, LINE)]


def tiles_kernel(block, place_ref, lists_ref, counts_ref, x_ref, sw_ref, _, tiles_ref, tiles_t_ref, self_ref):
    for i, o in enumerate(slots(place_ref[0])):
        first, second = lists_ref[o, 0], lists_ref[o, 1]
        at = pl.ds(pl.multiple_of((o * 2 + second) * block, block), block)
        tile = (counts_ref[:, at] * (first + second)).astype(F32)
        tiles_ref[:, i * block : (i + 1) * block] = tile.astype(BF16)
        tiles_t_ref[i * block : (i + 1) * block, :] = tile.T.astype(BF16)
    self_ref[...] = dot(x_ref[...], sw_ref[...])


def message_kernel(block, first, last, *refs):
    size = last - first
    if first == 0:
        lists_ref, same_ref, below_ref = refs[:3]
        held = [same_ref[at_block(lists_ref[0, 1], block), :]]
        held += [below_ref[at_block(lists_ref[LINE, 1], block), :]]
        refs = refs[3:]
        held += [b[...] for b in refs[: size - 2]]
        refs = refs[size - 2 :]
    else:
        held = [b[...] for b in refs[:size]]
        refs = refs[size:]
    q_ref, qb_ref, tiles_ref = refs[:3]
    acc_in, deg_in = refs[3:5] if first else (None, None)
    msg_ref, acc_ref, deg_ref = refs[-3:]
    x = jnp.concatenate(held, axis=0)
    keep = x[:, :128].astype(F32) < LIMIT
    tiles = tiles_ref[:, first * block : last * block]
    deg = dot(tiles, jnp.where(keep, 1.0, 0.0).astype(BF16))
    deg_ref[...] = deg + deg_in[...] if first else deg
    keep = keep[:, :1]
    hidden = q_ref.shape[1]
    step = 512
    for n in range(hidden // step):
        cols = slice(n * step, (n + 1) * step)
        pre = dot(x, q_ref[:, cols]) + qb_ref[:, cols]
        msg = jnp.where(keep, jnp.maximum(pre, 0.0), 0.0).astype(BF16)
        msg_ref[:, cols] = msg
        acc = dot(tiles, msg)
        acc_ref[:, cols] = acc + acc_in[:, cols] if first else acc


def layer_kernel(
    block, live_ref, got_a, got_b, q_ref, qb_ref, tiles_ref, acc_ref, deg_ref, self_ref, up_ref, nb_ref, ob_ref, tt_ref,
    msg_ref, g_ref, gpool_ref, pre_ref, last_ref, near1, near2, near3, pooled_ref, gn_ref,
):
    rows, width = self_ref.shape
    hidden = nb_ref.shape[0]
    step = 512
    x = jnp.concatenate([got_a[...], got_b[...]], axis=0)
    keep = x[:, :128].astype(F32) < LIMIT
    tiles = tiles_ref[:, -2 * block :]
    deg = deg_ref[...] + dot(tiles, jnp.where(keep, 1.0, 0.0).astype(BF16))
    inv_deg = 1.0 / (1.0 + deg[:, :1])
    keep = keep[:, :1]
    for n in range(hidden // step):
        cols = slice(n * step, (n + 1) * step)
        pre = dot(x, q_ref[:, cols]) + qb_ref[:, cols]
        msg = jnp.where(keep, jnp.maximum(pre, 0.0), 0.0).astype(BF16)
        last_ref[:, cols] = msg
        pooled_ref[:, cols] = ((acc_ref[:, cols] + dot(tiles, msg)) * inv_deg).astype(BF16)
    pooled = pooled_ref[...]
    for n in range(width // step):
        cols = slice(n * step, (n + 1) * step)
        pre_ref[:, cols] = self_ref[:, cols] + dot(pooled, nb_ref[:, cols]) + ob_ref[:, cols]
    pre = pre_ref[...]
    act = jnp.maximum(pre, 0.0)
    inv = lax.rsqrt(jnp.mean(act * act, axis=1, keepdims=True) + EPS)
    keep = lax.broadcasted_iota(jnp.int32, (rows, 1), 0) < live_ref[0]
    up = jnp.where(keep, up_ref[...].astype(F32), 0.0)
    inner = jnp.sum(up * act, axis=1, keepdims=True) / width
    g = inv * up - act * (inv * inv * inv * inner)
    g = jnp.where(pre > 0, g, 0.0).astype(BF16)
    g_ref[...] = g
    for n in range(hidden // step):
        cols = slice(n * step, (n + 1) * step)
        gpool_ref[:, cols] = (dot(g, nb_ref[cols, :], 1, 1) * inv_deg).astype(BF16)

    def store(cols, part):
        for i, out in enumerate((near1, near2, near3)):
            out[:, cols] = part[i * block : (i + 1) * block].astype(BF16)

    back_dot(2 * block, tt_ref, gpool_ref, [msg_ref[2 * block :, :]], q_ref, gn_ref, store)


def back_dot(first, tt_ref, gpool_ref, messages, q_ref, gn_ref, store):
    rows = gn_ref.shape[0]
    tt = tt_ref[first : first + rows, :]
    step = 512
    for n in range(gpool_ref.shape[1] // step):
        cols = slice(n * step, (n + 1) * step)
        live = jnp.concatenate([m[:, cols] for m in messages], axis=0).astype(F32) > 0
        gn_ref[:, cols] = jnp.where(live, dot(tt, gpool_ref[:, cols]), 0.0).astype(BF16)
    gn = gn_ref[...]
    for n in range(q_ref.shape[0] // step):
        cols = slice(n * step, (n + 1) * step)
        store(cols, dot(gn, q_ref[cols, :], 1, 1))


def back_far_kernel(block, place_ref, lists_ref, tt_ref, gpool_ref, early_ref, last_ref, q_ref, _, *refs):
    outs, gn_ref = refs[:-1], refs[-1]
    width = q_ref.shape[0]

    def store(cols, part):
        for i, out in enumerate(outs):
            out[:, cols] = part[i * block : (i + 1) * block].astype(BF16)

    for d, out in enumerate(outs, 1):
        which = lists_ref[far(place_ref[0], d), 1].astype(F32)
        out[:, width:] = jnp.full((block, 128), which, F32).astype(BF16)
    messages = [early_ref[...], last_ref[...]]
    back_dot((1 + LINE) * block, tt_ref, gpool_ref, messages, q_ref, gn_ref, store)


def back_own_kernel(
    block, lists_ref, live_ref, tt_ref, gpool_ref, msg_ref, q_ref, g_ref, sw_ref, pre_ref, _,
    same_ref, below_ref, gself_ref, emb_ref, gn_ref,
):
    same_ref[...] = jnp.zeros_like(same_ref)
    at = at_block(lists_ref[0, 1], block)

    def store(cols, part):
        same_ref[at, cols] = part[:block].astype(BF16)
        below_ref[:, cols] = part[block:].astype(BF16)

    back_dot(0, tt_ref, gpool_ref, [msg_ref[: 2 * block, :]], q_ref, gn_ref, store)
    rows, width = pre_ref.shape
    step = 512
    for n in range(width // step):
        cols = slice(n * step, (n + 1) * step)
        gself_ref[:, cols] = dot(g_ref[...], sw_ref[cols, :], 1, 1)
    act = jnp.maximum(pre_ref[...], 0.0)
    inv = lax.rsqrt(jnp.mean(act * act, axis=1, keepdims=True) + EPS)
    keep = lax.broadcasted_iota(jnp.int32, (rows, 1), 0) < live_ref[0]
    emb_ref[...] = jnp.where(keep, act * inv, 0.0).astype(BF16)


def sum_near_kernel(block, place_ref, lists_ref, m1, m2, m3, own_ref, d1, d2, d3, out_ref, total):
    total[...] = jnp.zeros_like(total)
    total[at_block(lists_ref[LINE, 1], block), :] = own_ref[...].astype(F32)
    for d, (meta, part) in enumerate(zip((m1, m2, m3), (d1, d2, d3)), 1):
        p = lax.rem(place_ref[0] + d, LINE)
        total[at_block(meta[0, near(p, d)], block), :] += part[...].astype(F32)
    out_ref[...] = total[...].astype(BF16)


def place_kernel(gself_ref, c1, c2, c3, total_ref):
    block, width = c1.shape[0], gself_ref.shape[1]
    first, second = gself_ref[:block, :], gself_ref[block:, :]
    for part in (c1, c2, c3):
        grad = part[:, :width].astype(F32)
        late = part[:, width : width + 1].astype(F32) > 0.5
        first += jnp.where(late, 0.0, grad)
        second += jnp.where(late, grad, 0.0)
    total_ref[:block, :] = first
    total_ref[block:, :] = second


def finish_kernel(live_ref, total_ref, same_ref, below_ref, out_ref):
    total = total_ref[...] + same_ref[...].astype(F32) + below_ref[...].astype(F32)
    keep = lax.broadcasted_iota(jnp.int32, (total.shape[0], 1), 0) < live_ref[0]
    out_ref[...] = jnp.where(keep, total, 0.0).astype(BF16)


def local(x, live, listed, counts, cotangent, q, qb, sw, nb, ob):
    x, lists, counts, up = x[0], listed[0, 0], counts[0], cotangent[0]
    live = live.reshape(1)
    rows, width = x.shape
    hidden = q.shape[1]
    reach, block_count = lists.shape
    block = rows // block_count
    qb, ob = qb[None], ob[None]
    place = (lax.axis_index("dom") % LINE).astype(jnp.int32).reshape(1)
    keep = lax.broadcasted_iota(jnp.int32, (rows, 1), 0) < live[0]
    marked = jnp.where(keep, x, jnp.asarray(DEAD, BF16))
    row = jnp.pad(lists[:, 1], (0, 128 - reach))[None]
    steps = range(1, LINE)
    one, two = ((block, width), BF16), ((rows, width), BF16)

    below = swap_rows(marked, LINE)
    same = swap_rows(marked, 0)
    metas = [along(row, -d) for d in steps]
    later, *metas = lax.optimization_barrier((marked, *metas))
    below2 = swap_rows(later, 2 * LINE)
    scalars = [SMEM] * (1 + len(steps))
    sent = call(
        lambda *r: pick_near_kernel(block, *r),
        [one] * len(steps),
        (place, *metas, below),
        scalars + [VMEM],
    )
    got_near = [along(b, d) for d, b in zip(steps, sent)]
    sent = call(
        lambda *r: pick_far_kernel(block, *r),
        [one] * len(steps),
        (place, *metas, same, below2),
        scalars + [VMEM] * 2,
    )
    got_far = [along(b, d) for d, b in zip(steps, sent)]
    tiles, tiles_t, self_pre = call(
        lambda *r: tiles_kernel(block, *r),
        [((rows, reach * block), BF16), ((reach * block, rows), BF16), ((rows, width), F32)],
        (place, lists, counts, x, sw, sent[0]),
        [SMEM] * 2 + [VMEM] * 3 + [HELD],
        flops=2 * rows * width * width,
    )
    split = 1 + LINE

    def message(first, last, ins, specs):
        size = last - first
        return call(
            lambda *r: message_kernel(block, first, last, *r),
            [((size * block, hidden), BF16), ((rows, hidden), F32), ((rows, 128), F32)],
            ins,
            specs,
            flops=2 * size * block * hidden * (width + rows),
        )

    msg_a, acc, deg = message(
        0, split, (lists, same, below, *got_near, q, qb, tiles), [SMEM] + [VMEM] * 8
    )
    msg_b, acc, deg = message(
        split, split + 1, (got_far[0], q, qb, tiles, acc, deg), [VMEM] * 6
    )
    gn = pltpu.VMEM((3 * block, hidden), BF16)
    g, gpool, pre, msg_c, *near_back = call(
        lambda *r: layer_kernel(block, *r),
        [two, ((rows, hidden), BF16), ((rows, width), F32), ((2 * block, hidden), BF16)] + [one] * 3,
        (live, *got_far[1:], q, qb, tiles, acc, deg, self_pre, up, nb, ob, tiles_t, msg_a),
        [SMEM] + [VMEM] * 13,
        scratch=[pltpu.VMEM((rows, hidden), BF16), gn],
        flops=8 * MICROSECOND,
    )
    back_near = [along(b, -d) for d, b in zip(steps, near_back)]
    far_back = call(
        lambda *r: back_far_kernel(block, *r),
        [((block, width + 128), BF16)] * 3,
        (place, lists, tiles_t, gpool, msg_b, msg_c, q, near_back[0]),
        [SMEM] * 2 + [VMEM] * 5 + [HELD],
        scratch=[gn],
        flops=2 * MICROSECOND,
    )
    back_far = [straight_back(b, d) for d, b in zip(steps, far_back)]
    own_same, own_below, gself, emb = call(
        lambda *r: back_own_kernel(block, *r),
        [two, one, ((rows, width), F32), two],
        (lists, live, tiles_t, gpool, msg_a, q, g, sw, pre, far_back[0]),
        [SMEM] * 2 + [VMEM] * 7 + [HELD],
        scratch=[pltpu.VMEM((2 * block, hidden), BF16)],
        flops=3 * MICROSECOND,
    )
    g_same = swap_rows(own_same, 0)
    total = pltpu.VMEM((rows, width), F32)
    (sum_below,) = call(
        lambda *r: sum_near_kernel(block, *r),
        [two],
        (place, lists, *metas, own_below, *back_near),
        [SMEM] * 5 + [VMEM] * 4,
        scratch=[total],
        flops=20 * MICROSECOND,
    )
    g_below = swap_rows(sum_below, -LINE)
    (placed,) = call(
        place_kernel,
        [((rows, width), F32)],
        (gself, *back_far),
        [VMEM] * 4,
        flops=20 * MICROSECOND,
    )
    (grad,) = call(finish_kernel, [two], (live, placed, g_same, g_below), [SMEM] + [VMEM] * 3)
    return emb[None], grad[None]


def solution(mesh):
    data = P("side", "dom", None)
    return jax.shard_map(
        local,
        mesh=mesh,
        in_specs=(
            data,
            P("side", "dom"),
            P("side", "dom", None, None),
            data,
            data,
            P(),
            P(),
            P(),
            P(),
            P(),
        ),
        out_specs=(data, data),
        check_vma=False,
    )
```

```python
import jax
import jax.numpy as jnp
from jax import lax
from jax.experimental import pallas as pl
from jax.experimental.pallas import tpu as pltpu
from jax.sharding import PartitionSpec as P

EPS = 1e-06
DEAD = 16384.0
LIMIT = 8192.0
MICROSECOND = 10**9
LINE = 4
F32 = jnp.float32
BF16 = jnp.bfloat16
VMEM = pl.BlockSpec(memory_space=pltpu.VMEM)
HELD = pl.BlockSpec(memory_space=pl.ANY)
SMEM = pl.BlockSpec(memory_space=pltpu.SMEM)


def dot(a, b, ca=1, cb=0):
    return lax.dot_general(a, b, (((ca,), (cb,)), ((), ())), preferred_element_type=F32)


def call(kernel, outs, ins, in_specs=None, scratch=(), limit=24, flops=0):
    return pl.pallas_call(
        kernel,
        out_shape=[jax.ShapeDtypeStruct(s, d) for s, d in outs],
        in_specs=in_specs or [VMEM] * len(ins),
        out_specs=[VMEM] * len(outs),
        scratch_shapes=list(scratch),
        compiler_params=pltpu.CompilerParams(vmem_limit_bytes=limit << 20),
        cost_estimate=pl.CostEstimate(flops=flops, bytes_accessed=1 << 20, transcendentals=0),
    )(*ins)


def swap_rows(x, shift):
    count = lax.axis_size("dom")
    pairs = [
        (s * count + j, (1 - s) * count + (j + shift) % count)
        for s in range(2)
        for j in range(count)
    ]
    return lax.ppermute(x, ("side", "dom"), pairs)


def along(x, d):
    count = lax.axis_size("dom")
    pairs = [(j, j // LINE * LINE + (j + d) % LINE) for j in range(count)]
    return lax.ppermute(x, "dom", pairs)


def straight_back(x, d):
    count = lax.axis_size("dom")
    pairs = []
    for s in range(2):
        for j in range(count):
            to = j + d if j % LINE + d < LINE else j + d + LINE
            pairs.append(((1 - s) * count + to % count, s * count + j))
    return lax.ppermute(x, ("side", "dom"), pairs)


def near(p, d):
    return jnp.where(p >= d, d + LINE, d)


def far(p, d):
    return jnp.where(p >= d, d, d + LINE)


def at_block(index, block):
    return pl.ds(pl.multiple_of(index * block, block), block)


def pick_near_kernel(block, place_ref, m1, m2, m3, rows_ref, *refs):
    outs = refs[-3:]
    for d, (meta, out) in enumerate(zip((m1, m2, m3), outs), 1):
        p = lax.rem(place_ref[0] + d, LINE)
        out[...] = rows_ref[at_block(meta[0, near(p, d)], block), :]


def pick_far_kernel(block, place_ref, m1, m2, m3, same_ref, below_ref, *outs):
    for d, (meta, out) in enumerate(zip((m1, m2, m3), outs), 1):
        p = lax.rem(place_ref[0] + d, LINE)
        at = at_block(meta[0, far(p, d)], block)

        @pl.when(p >= d)
        def _():
            out[...] = same_ref[at, :]

        @pl.when(p < d)
        def _():
            out[...] = below_ref[at, :]


def slots(p):
    return [0, LINE] + [near(p, d) for d in range(1, LINE)] + [far(p, d) for d in range(1, LINE)]


def tiles_kernel(block, place_ref, lists_ref, counts_ref, x_ref, sw_ref, _, tiles_ref, tiles_t_ref, self_ref):
    for i, o in enumerate(slots(place_ref[0])):
        first, second = lists_ref[o, 0], lists_ref[o, 1]
        at = pl.ds(pl.multiple_of((o * 2 + second) * block, block), block)
        tile = (counts_ref[:, at] * (first + second)).astype(F32)
        tiles_ref[:, i * block : (i + 1) * block] = tile.astype(BF16)
        tiles_t_ref[i * block : (i + 1) * block, :] = tile.T.astype(BF16)
    self_ref[...] = dot(x_ref[...], sw_ref[...])


def message_kernel(block, first, last, *refs):
    size = last - first
    if first == 0:
        lists_ref, same_ref, below_ref = refs[:3]
        held = [same_ref[at_block(lists_ref[0, 1], block), :]]
        held += [below_ref[at_block(lists_ref[LINE, 1], block), :]]
        refs = refs[3:]
        held += [b[...] for b in refs[: size - 2]]
        refs = refs[size - 2 :]
    else:
        held = [b[...] for b in refs[:size]]
        refs = refs[size:]
    q_ref, qb_ref, tiles_ref = refs[:3]
    acc_in, deg_in = refs[3:5] if first else (None, None)
    msg_ref, acc_ref, deg_ref = refs[-3:]
    x = jnp.concatenate(held, axis=0)
    keep = x[:, :128].astype(F32) < LIMIT
    tiles = tiles_ref[:, first * block : last * block]
    deg = dot(tiles, jnp.where(keep, 1.0, 0.0).astype(BF16))
    deg_ref[...] = deg + deg_in[...] if first else deg
    keep = keep[:, :1]
    hidden = q_ref.shape[1]
    step = 512
    for n in range(hidden // step):
        cols = slice(n * step, (n + 1) * step)
        pre = dot(x, q_ref[:, cols]) + qb_ref[:, cols]
        msg = jnp.where(keep, jnp.maximum(pre, 0.0), 0.0).astype(BF16)
        msg_ref[:, cols] = msg
        acc = dot(tiles, msg)
        acc_ref[:, cols] = acc + acc_in[:, cols] if first else acc


def layer_kernel(
    block, live_ref, got_a, got_b, q_ref, qb_ref, tiles_ref, acc_ref, deg_ref, self_ref, up_ref, nb_ref, ob_ref, tt_ref,
    msg_ref, g_ref, gpool_ref, pre_ref, last_ref, near1, near2, near3, pooled_ref, gn_ref,
):
    rows, width = self_ref.shape
    hidden = nb_ref.shape[0]
    step = 512
    x = jnp.concatenate([got_a[...], got_b[...]], axis=0)
    keep = x[:, :128].astype(F32) < LIMIT
    tiles = tiles_ref[:, -2 * block :]
    deg = deg_ref[...] + dot(tiles, jnp.where(keep, 1.0, 0.0).astype(BF16))
    inv_deg = 1.0 / (1.0 + deg[:, :1])
    keep = keep[:, :1]
    for n in range(hidden // step):
        cols = slice(n * step, (n + 1) * step)
        pre = dot(x, q_ref[:, cols]) + qb_ref[:, cols]
        msg = jnp.where(keep, jnp.maximum(pre, 0.0), 0.0).astype(BF16)
        last_ref[:, cols] = msg
        pooled_ref[:, cols] = ((acc_ref[:, cols] + dot(tiles, msg)) * inv_deg).astype(BF16)
    pooled = pooled_ref[...]
    for n in range(width // step):
        cols = slice(n * step, (n + 1) * step)
        pre_ref[:, cols] = self_ref[:, cols] + dot(pooled, nb_ref[:, cols]) + ob_ref[:, cols]
    pre = pre_ref[...]
    act = jnp.maximum(pre, 0.0)
    inv = lax.rsqrt(jnp.mean(act * act, axis=1, keepdims=True) + EPS)
    keep = lax.broadcasted_iota(jnp.int32, (rows, 1), 0) < live_ref[0]
    up = jnp.where(keep, up_ref[...].astype(F32), 0.0)
    inner = jnp.sum(up * act, axis=1, keepdims=True) / width
    g = inv * up - act * (inv * inv * inv * inner)
    g = jnp.where(pre > 0, g, 0.0).astype(BF16)
    g_ref[...] = g
    for n in range(hidden // step):
        cols = slice(n * step, (n + 1) * step)
        gpool_ref[:, cols] = (dot(g, nb_ref[cols, :], 1, 1) * inv_deg).astype(BF16)

    def store(cols, part):
        for i, out in enumerate((near1, near2, near3)):
            out[:, cols] = part[i * block : (i + 1) * block].astype(BF16)

    back_dot(2 * block, tt_ref, gpool_ref, [msg_ref[2 * block :, :]], q_ref, gn_ref, store)


def back_dot(first, tt_ref, gpool_ref, messages, q_ref, gn_ref, store):
    rows = gn_ref.shape[0]
    tt = tt_ref[first : first + rows, :]
    step = 512
    for n in range(gpool_ref.shape[1] // step):
        cols = slice(n * step, (n + 1) * step)
        live = jnp.concatenate([m[:, cols] for m in messages], axis=0).astype(F32) > 0
        gn_ref[:, cols] = jnp.where(live, dot(tt, gpool_ref[:, cols]), 0.0).astype(BF16)
    gn = gn_ref[...]
    for n in range(q_ref.shape[0] // step):
        cols = slice(n * step, (n + 1) * step)
        store(cols, dot(gn, q_ref[cols, :], 1, 1))


def back_far_kernel(block, tt_ref, gpool_ref, early_ref, last_ref, q_ref, _, *refs):
    outs, gn_ref = refs[:-1], refs[-1]

    def store(cols, part):
        for i, out in enumerate(outs):
            out[:, cols] = part[i * block : (i + 1) * block].astype(BF16)

    messages = [early_ref[...], last_ref[...]]
    back_dot((1 + LINE) * block, tt_ref, gpool_ref, messages, q_ref, gn_ref, store)


def back_own_kernel(
    block, lists_ref, live_ref, tt_ref, gpool_ref, msg_ref, q_ref, g_ref, sw_ref, pre_ref, _,
    same_ref, below_ref, gself_ref, emb_ref, gn_ref,
):
    same_ref[...] = jnp.zeros_like(same_ref)
    at = at_block(lists_ref[0, 1], block)

    def store(cols, part):
        same_ref[at, cols] = part[:block].astype(BF16)
        below_ref[:, cols] = part[block:].astype(BF16)

    back_dot(0, tt_ref, gpool_ref, [msg_ref[: 2 * block, :]], q_ref, gn_ref, store)
    rows, width = pre_ref.shape
    step = 512
    for n in range(width // step):
        cols = slice(n * step, (n + 1) * step)
        gself_ref[:, cols] = dot(g_ref[...], sw_ref[cols, :], 1, 1)
    act = jnp.maximum(pre_ref[...], 0.0)
    inv = lax.rsqrt(jnp.mean(act * act, axis=1, keepdims=True) + EPS)
    keep = lax.broadcasted_iota(jnp.int32, (rows, 1), 0) < live_ref[0]
    emb_ref[...] = jnp.where(keep, act * inv, 0.0).astype(BF16)


def sum_near_kernel(block, place_ref, lists_ref, m1, m2, m3, own_ref, d1, d2, d3, out_ref, total):
    total[...] = jnp.zeros_like(total)
    total[at_block(lists_ref[LINE, 1], block), :] = own_ref[...].astype(F32)
    for d, (meta, part) in enumerate(zip((m1, m2, m3), (d1, d2, d3)), 1):
        p = lax.rem(place_ref[0] + d, LINE)
        total[at_block(meta[0, near(p, d)], block), :] += part[...].astype(F32)
    out_ref[...] = total[...].astype(BF16)


def place_kernel(block, place_ref, same_ref, two_ref, gself_ref, c1, c2, c3, total_ref):
    total_ref[...] = gself_ref[...]
    for d, part in enumerate((c1, c2, c3), 1):
        p = lax.rem(place_ref[0] + d, LINE)
        o = far(p, d)
        which = jnp.where(p >= d, same_ref[d - 1, o], two_ref[d - 1, o])
        total_ref[at_block(which, block), :] += part[...].astype(F32)


def finish_kernel(live_ref, total_ref, same_ref, below_ref, out_ref):
    total = total_ref[...] + same_ref[...].astype(F32) + below_ref[...].astype(F32)
    keep = lax.broadcasted_iota(jnp.int32, (total.shape[0], 1), 0) < live_ref[0]
    out_ref[...] = jnp.where(keep, total, 0.0).astype(BF16)


def local(x, live, listed, counts, cotangent, q, qb, sw, nb, ob):
    x, lists, counts, up = x[0], listed[0, 0], counts[0], cotangent[0]
    live = live.reshape(1)
    rows, width = x.shape
    hidden = q.shape[1]
    reach, block_count = lists.shape
    block = rows // block_count
    qb, ob = qb[None], ob[None]
    place = (lax.axis_index("dom") % LINE).astype(jnp.int32).reshape(1)
    keep = lax.broadcasted_iota(jnp.int32, (rows, 1), 0) < live[0]
    marked = jnp.where(keep, x, jnp.asarray(DEAD, BF16))
    row = jnp.pad(lists[:, 1], (0, 128 - reach))[None]
    steps = range(1, LINE)
    one, two = ((block, width), BF16), ((rows, width), BF16)

    below = swap_rows(marked, LINE)
    same = swap_rows(marked, 0)
    metas = [along(row, -d) for d in steps]
    later, *metas = lax.optimization_barrier((marked, *metas))
    below2 = swap_rows(later, 2 * LINE)
    gathered = jnp.concatenate(metas, axis=0)
    lists_same = swap_rows(gathered, 0)
    lists_two = swap_rows(gathered, -2 * LINE)
    scalars = [SMEM] * (1 + len(steps))
    sent = call(
        lambda *r: pick_near_kernel(block, *r),
        [one] * len(steps),
        (place, *metas, below, lists_same, lists_two),
        scalars + [VMEM, HELD, HELD],
    )
    got_near = [along(b, d) for d, b in zip(steps, sent)]
    sent = call(
        lambda *r: pick_far_kernel(block, *r),
        [one] * len(steps),
        (place, *metas, same, below2),
        scalars + [VMEM] * 2,
    )
    got_far = [along(b, d) for d, b in zip(steps, sent)]
    tiles, tiles_t, self_pre = call(
        lambda *r: tiles_kernel(block, *r),
        [((rows, reach * block), BF16), ((reach * block, rows), BF16), ((rows, width), F32)],
        (place, lists, counts, x, sw, sent[0]),
        [SMEM] * 2 + [VMEM] * 3 + [HELD],
        flops=2 * rows * width * width,
    )
    split = 1 + LINE

    def message(first, last, ins, specs):
        size = last - first
        return call(
            lambda *r: message_kernel(block, first, last, *r),
            [((size * block, hidden), BF16), ((rows, hidden), F32), ((rows, 128), F32)],
            ins,
            specs,
            flops=2 * size * block * hidden * (width + rows),
        )

    msg_a, acc, deg = message(
        0, split, (lists, same, below, *got_near, q, qb, tiles), [SMEM] + [VMEM] * 8
    )
    msg_b, acc, deg = message(
        split, split + 1, (got_far[0], q, qb, tiles, acc, deg), [VMEM] * 6
    )
    gn = pltpu.VMEM((3 * block, hidden), BF16)
    g, gpool, pre, msg_c, *near_back = call(
        lambda *r: layer_kernel(block, *r),
        [two, ((rows, hidden), BF16), ((rows, width), F32), ((2 * block, hidden), BF16)] + [one] * 3,
        (live, *got_far[1:], q, qb, tiles, acc, deg, self_pre, up, nb, ob, tiles_t, msg_a),
        [SMEM] + [VMEM] * 13,
        scratch=[pltpu.VMEM((rows, hidden), BF16), gn],
        flops=8 * MICROSECOND,
    )
    back_near = [along(b, -d) for d, b in zip(steps, near_back)]
    gate = swap_rows(lax.optimization_barrier((row, near_back[0]))[0], 0)
    far_back = call(
        lambda *r: back_far_kernel(block, *r),
        [one] * 3,
        (tiles_t, gpool, msg_b, msg_c, q, gate),
        [VMEM] * 5 + [HELD],
        scratch=[gn],
        flops=2 * MICROSECOND,
    )
    back_far = [straight_back(b, d) for d, b in zip(steps, far_back)]
    own_same, own_below, gself, emb = call(
        lambda *r: back_own_kernel(block, *r),
        [two, one, ((rows, width), F32), two],
        (lists, live, tiles_t, gpool, msg_a, q, g, sw, pre, far_back[0]),
        [SMEM] * 2 + [VMEM] * 7 + [HELD],
        scratch=[pltpu.VMEM((2 * block, hidden), BF16)],
        flops=3 * MICROSECOND,
    )
    g_same = swap_rows(own_same, 0)
    total = pltpu.VMEM((rows, width), F32)
    (sum_below,) = call(
        lambda *r: sum_near_kernel(block, *r),
        [two],
        (place, lists, *metas, own_below, *back_near),
        [SMEM] * 5 + [VMEM] * 4,
        scratch=[total],
        flops=20 * MICROSECOND,
    )
    g_below = swap_rows(sum_below, -LINE)
    (placed,) = call(
        lambda *r: place_kernel(block, *r),
        [((rows, width), F32)],
        (place, lists_same, lists_two, gself, *back_far),
        [SMEM] * 3 + [VMEM] * 4,
        flops=20 * MICROSECOND,
    )
    (grad,) = call(finish_kernel, [two], (live, placed, g_same, g_below), [SMEM] + [VMEM] * 3)
    return emb[None], grad[None]


def solution(mesh):
    data = P("side", "dom", None)
    return jax.shard_map(
        local,
        mesh=mesh,
        in_specs=(
            data,
            P("side", "dom"),
            P("side", "dom", None, None),
            data,
            data,
            P(),
            P(),
            P(),
            P(),
            P(),
        ),
        out_specs=(data, data),
        check_vma=False,
    )
```

```python
import jax
import jax.numpy as jnp
from jax import lax
from jax.experimental import pallas as pl
from jax.experimental.pallas import tpu as pltpu
from jax.sharding import PartitionSpec as P

EPS = 1e-06
DEAD = 16384.0
LIMIT = 8192.0
MICROSECOND = 10**9
LINE = 4
F32 = jnp.float32
BF16 = jnp.bfloat16
VMEM = pl.BlockSpec(memory_space=pltpu.VMEM)
HELD = pl.BlockSpec(memory_space=pl.ANY)
SMEM = pl.BlockSpec(memory_space=pltpu.SMEM)


def dot(a, b, ca=1, cb=0):
    return lax.dot_general(a, b, (((ca,), (cb,)), ((), ())), preferred_element_type=F32)


def call(kernel, outs, ins, in_specs=None, scratch=(), limit=24, flops=0):
    return pl.pallas_call(
        kernel,
        out_shape=[jax.ShapeDtypeStruct(s, d) for s, d in outs],
        in_specs=in_specs or [VMEM] * len(ins),
        out_specs=[VMEM] * len(outs),
        scratch_shapes=list(scratch),
        compiler_params=pltpu.CompilerParams(vmem_limit_bytes=limit << 20),
        cost_estimate=pl.CostEstimate(flops=flops, bytes_accessed=1 << 20, transcendentals=0),
    )(*ins)


def swap_rows(x, shift):
    count = lax.axis_size("dom")
    pairs = [
        (s * count + j, (1 - s) * count + (j + shift) % count)
        for s in range(2)
        for j in range(count)
    ]
    return lax.ppermute(x, ("side", "dom"), pairs)


def along(x, d):
    count = lax.axis_size("dom")
    pairs = [(j, j // LINE * LINE + (j + d) % LINE) for j in range(count)]
    return lax.ppermute(x, "dom", pairs)


def straight_back(x, d):
    count = lax.axis_size("dom")
    pairs = []
    for s in range(2):
        for j in range(count):
            to = j + d if j % LINE + d < LINE else j + d + LINE
            pairs.append(((1 - s) * count + to % count, s * count + j))
    return lax.ppermute(x, ("side", "dom"), pairs)


def near(p, d):
    return jnp.where(p >= d, d + LINE, d)


def far(p, d):
    return jnp.where(p >= d, d, d + LINE)


def at_block(index, block):
    return pl.ds(pl.multiple_of(index * block, block), block)


def pick_near_kernel(block, place_ref, m1, m2, m3, rows_ref, _, *outs):
    for d, (meta, out) in enumerate(zip((m1, m2, m3), outs), 1):
        p = lax.rem(place_ref[0] + d, LINE)
        out[...] = rows_ref[at_block(meta[0, near(p, d)], block), :]


def pick_far_kernel(block, place_ref, m1, m2, m3, same_ref, below_ref, *outs):
    for d, (meta, out) in enumerate(zip((m1, m2, m3), outs), 1):
        p = lax.rem(place_ref[0] + d, LINE)
        at = at_block(meta[0, far(p, d)], block)

        @pl.when(p >= d)
        def _():
            out[...] = same_ref[at, :]

        @pl.when(p < d)
        def _():
            out[...] = below_ref[at, :]


def slots(p):
    return [0, LINE] + [near(p, d) for d in range(1, LINE)] + [far(p, d) for d in range(1, LINE)]


def tiles_kernel(block, place_ref, lists_ref, counts_ref, x_ref, sw_ref, tiles_ref, tiles_t_ref, self_ref):
    for i, o in enumerate(slots(place_ref[0])):
        first, second = lists_ref[o, 0], lists_ref[o, 1]
        at = pl.ds(pl.multiple_of((o * 2 + second) * block, block), block)
        tile = (counts_ref[:, at] * (first + second)).astype(F32)
        tiles_ref[:, i * block : (i + 1) * block] = tile.astype(BF16)
        tiles_t_ref[i * block : (i + 1) * block, :] = tile.T.astype(BF16)
    self_ref[...] = dot(x_ref[...], sw_ref[...])


def message_kernel(block, first, last, *refs):
    size = last - first
    if first == 0:
        lists_ref, same_ref, below_ref = refs[:3]
        held = [same_ref[at_block(lists_ref[0, 1], block), :]]
        held += [below_ref[at_block(lists_ref[LINE, 1], block), :]]
        refs = refs[3:]
        held += [b[...] for b in refs[: size - 2]]
        refs = refs[size - 2 :]
    else:
        held = [b[...] for b in refs[:size]]
        refs = refs[size:]
    q_ref, qb_ref, tiles_ref = refs[:3]
    acc_in, deg_in = refs[3:5] if first else (None, None)
    msg_ref, acc_ref, deg_ref = refs[-3:]
    x = jnp.concatenate(held, axis=0)
    keep = x[:, :128].astype(F32) < LIMIT
    tiles = tiles_ref[:, first * block : last * block]
    deg = dot(tiles, jnp.where(keep, 1.0, 0.0).astype(BF16))
    deg_ref[...] = deg + deg_in[...] if first else deg
    keep = keep[:, :1]
    hidden = q_ref.shape[1]
    step = 512
    for n in range(hidden // step):
        cols = slice(n * step, (n + 1) * step)
        pre = dot(x, q_ref[:, cols]) + qb_ref[:, cols]
        msg = jnp.where(keep, jnp.maximum(pre, 0.0), 0.0).astype(BF16)
        msg_ref[:, cols] = msg
        acc = dot(tiles, msg)
        acc_ref[:, cols] = acc + acc_in[:, cols] if first else acc


def layer_kernel(
    block, live_ref, got_a, got_b, q_ref, qb_ref, tiles_ref, acc_ref, deg_ref, self_ref, up_ref, nb_ref, ob_ref, tt_ref,
    msg_ref, g_ref, gpool_ref, pre_ref, last_ref, near1, near2, near3, pooled_ref, gn_ref,
):
    rows, width = self_ref.shape
    hidden = nb_ref.shape[0]
    step = 512
    x = jnp.concatenate([got_a[...], got_b[...]], axis=0)
    keep = x[:, :128].astype(F32) < LIMIT
    tiles = tiles_ref[:, -2 * block :]
    deg = deg_ref[...] + dot(tiles, jnp.where(keep, 1.0, 0.0).astype(BF16))
    inv_deg = 1.0 / (1.0 + deg[:, :1])
    keep = keep[:, :1]
    for n in range(hidden // step):
        cols = slice(n * step, (n + 1) * step)
        pre = dot(x, q_ref[:, cols]) + qb_ref[:, cols]
        msg = jnp.where(keep, jnp.maximum(pre, 0.0), 0.0).astype(BF16)
        last_ref[:, cols] = msg
        pooled_ref[:, cols] = ((acc_ref[:, cols] + dot(tiles, msg)) * inv_deg).astype(BF16)
    pooled = pooled_ref[...]
    for n in range(width // step):
        cols = slice(n * step, (n + 1) * step)
        pre_ref[:, cols] = self_ref[:, cols] + dot(pooled, nb_ref[:, cols]) + ob_ref[:, cols]
    pre = pre_ref[...]
    act = jnp.maximum(pre, 0.0)
    inv = lax.rsqrt(jnp.mean(act * act, axis=1, keepdims=True) + EPS)
    keep = lax.broadcasted_iota(jnp.int32, (rows, 1), 0) < live_ref[0]
    up = jnp.where(keep, up_ref[...].astype(F32), 0.0)
    inner = jnp.sum(up * act, axis=1, keepdims=True) / width
    g = inv * up - act * (inv * inv * inv * inner)
    g = jnp.where(pre > 0, g, 0.0).astype(BF16)
    g_ref[...] = g
    for n in range(hidden // step):
        cols = slice(n * step, (n + 1) * step)
        gpool_ref[:, cols] = (dot(g, nb_ref[cols, :], 1, 1) * inv_deg).astype(BF16)

    def store(cols, part):
        for i, out in enumerate((near1, near2, near3)):
            out[:, cols] = part[i * block : (i + 1) * block].astype(BF16)

    back_dot(2 * block, tt_ref, gpool_ref, [msg_ref[2 * block :, :]], q_ref, gn_ref, store)


def back_dot(first, tt_ref, gpool_ref, messages, q_ref, gn_ref, store):
    rows = gn_ref.shape[0]
    tt = tt_ref[first : first + rows, :]
    step = 512
    for n in range(gpool_ref.shape[1] // step):
        cols = slice(n * step, (n + 1) * step)
        live = jnp.concatenate([m[:, cols] for m in messages], axis=0).astype(F32) > 0
        gn_ref[:, cols] = jnp.where(live, dot(tt, gpool_ref[:, cols]), 0.0).astype(BF16)
    gn = gn_ref[...]
    for n in range(q_ref.shape[0] // step):
        cols = slice(n * step, (n + 1) * step)
        store(cols, dot(gn, q_ref[cols, :], 1, 1))


def back_far_kernel(block, place_ref, lists_ref, tt_ref, gpool_ref, early_ref, last_ref, q_ref, _, *refs):
    outs, gn_ref = refs[:-1], refs[-1]
    width = q_ref.shape[0]

    def store(cols, part):
        for i, out in enumerate(outs):
            out[:, cols] = part[i * block : (i + 1) * block].astype(BF16)

    for d, out in enumerate(outs, 1):
        which = lists_ref[far(place_ref[0], d), 1].astype(F32)
        out[:, width:] = jnp.full((block, 128), which, F32).astype(BF16)
    messages = [early_ref[...], last_ref[...]]
    back_dot((1 + LINE) * block, tt_ref, gpool_ref, messages, q_ref, gn_ref, store)


def back_own_kernel(
    block, lists_ref, live_ref, tt_ref, gpool_ref, msg_ref, q_ref, g_ref, sw_ref, pre_ref, _,
    same_ref, below_ref, gself_ref, emb_ref, gn_ref,
):
    same_ref[...] = jnp.zeros_like(same_ref)
    at = at_block(lists_ref[0, 1], block)

    def store(cols, part):
        same_ref[at, cols] = part[:block].astype(BF16)
        below_ref[:, cols] = part[block:].astype(BF16)

    back_dot(0, tt_ref, gpool_ref, [msg_ref[: 2 * block, :]], q_ref, gn_ref, store)
    rows, width = pre_ref.shape
    step = 512
    for n in range(width // step):
        cols = slice(n * step, (n + 1) * step)
        gself_ref[:, cols] = dot(g_ref[...], sw_ref[cols, :], 1, 1)
    act = jnp.maximum(pre_ref[...], 0.0)
    inv = lax.rsqrt(jnp.mean(act * act, axis=1, keepdims=True) + EPS)
    keep = lax.broadcasted_iota(jnp.int32, (rows, 1), 0) < live_ref[0]
    emb_ref[...] = jnp.where(keep, act * inv, 0.0).astype(BF16)


def sum_near_kernel(block, place_ref, lists_ref, m1, m2, m3, own_ref, d1, d2, d3, out_ref, total):
    total[...] = jnp.zeros_like(total)
    total[at_block(lists_ref[LINE, 1], block), :] = own_ref[...].astype(F32)
    for d, (meta, part) in enumerate(zip((m1, m2, m3), (d1, d2, d3)), 1):
        p = lax.rem(place_ref[0] + d, LINE)
        total[at_block(meta[0, near(p, d)], block), :] += part[...].astype(F32)
    out_ref[...] = total[...].astype(BF16)


def place_kernel(gself_ref, c1, c2, c3, total_ref):
    block, width = c1.shape[0], gself_ref.shape[1]
    first, second = gself_ref[:block, :], gself_ref[block:, :]
    for part in (c1, c2, c3):
        grad = part[:, :width].astype(F32)
        late = part[:, width : width + 1].astype(F32) > 0.5
        first += jnp.where(late, 0.0, grad)
        second += jnp.where(late, grad, 0.0)
    total_ref[:block, :] = first
    total_ref[block:, :] = second


def finish_kernel(live_ref, total_ref, same_ref, below_ref, out_ref):
    total = total_ref[...] + same_ref[...].astype(F32) + below_ref[...].astype(F32)
    keep = lax.broadcasted_iota(jnp.int32, (total.shape[0], 1), 0) < live_ref[0]
    out_ref[...] = jnp.where(keep, total, 0.0).astype(BF16)


def local(x, live, listed, counts, cotangent, q, qb, sw, nb, ob):
    x, lists, counts, up = x[0], listed[0, 0], counts[0], cotangent[0]
    live = live.reshape(1)
    rows, width = x.shape
    hidden = q.shape[1]
    reach, block_count = lists.shape
    block = rows // block_count
    qb, ob = qb[None], ob[None]
    place = (lax.axis_index("dom") % LINE).astype(jnp.int32).reshape(1)
    keep = lax.broadcasted_iota(jnp.int32, (rows, 1), 0) < live[0]
    marked = jnp.where(keep, x, jnp.asarray(DEAD, BF16))
    row = jnp.pad(lists[:, 1], (0, 128 - reach))[None]
    steps = range(1, LINE)
    one, two = ((block, width), BF16), ((rows, width), BF16)

    below = swap_rows(marked, LINE)
    same = swap_rows(marked, 0)
    metas = [along(row, -d) for d in steps]
    later, *metas = lax.optimization_barrier((marked, *metas))
    below2 = swap_rows(later, 2 * LINE)
    scalars = [SMEM] * (1 + len(steps))
    tiles, tiles_t, self_pre = call(
        lambda *r: tiles_kernel(block, *r),
        [((rows, reach * block), BF16), ((reach * block, rows), BF16), ((rows, width), F32)],
        (place, lists, counts, x, sw),
        [SMEM] * 2 + [VMEM] * 3,
        flops=2 * rows * width * width,
    )
    sent = call(
        lambda *r: pick_near_kernel(block, *r),
        [one] * len(steps),
        (place, *metas, below, tiles),
        scalars + [VMEM, HELD],
    )
    got_near = [along(b, d) for d, b in zip(steps, sent)]
    sent = call(
        lambda *r: pick_far_kernel(block, *r),
        [one] * len(steps),
        (place, *metas, same, below2),
        scalars + [VMEM] * 2,
    )
    got_far = [along(b, d) for d, b in zip(steps, sent)]
    split = 1 + LINE

    def message(first, last, ins, specs):
        size = last - first
        return call(
            lambda *r: message_kernel(block, first, last, *r),
            [((size * block, hidden), BF16), ((rows, hidden), F32), ((rows, 128), F32)],
            ins,
            specs,
            flops=2 * size * block * hidden * (width + rows),
        )

    msg_a, acc, deg = message(
        0, split, (lists, same, below, *got_near, q, qb, tiles), [SMEM] + [VMEM] * 8
    )
    msg_b, acc, deg = message(
        split, split + 1, (got_far[0], q, qb, tiles, acc, deg), [VMEM] * 6
    )
    gn = pltpu.VMEM((3 * block, hidden), BF16)
    g, gpool, pre, msg_c, *near_back = call(
        lambda *r: layer_kernel(block, *r),
        [two, ((rows, hidden), BF16), ((rows, width), F32), ((2 * block, hidden), BF16)] + [one] * 3,
        (live, *got_far[1:], q, qb, tiles, acc, deg, self_pre, up, nb, ob, tiles_t, msg_a),
        [SMEM] + [VMEM] * 13,
        scratch=[pltpu.VMEM((rows, hidden), BF16), gn],
        flops=8 * MICROSECOND,
    )
    back_near = [along(b, -d) for d, b in zip(steps, near_back)]
    far_back = call(
        lambda *r: back_far_kernel(block, *r),
        [((block, width + 128), BF16)] * 3,
        (place, lists, tiles_t, gpool, msg_b, msg_c, q, near_back[0]),
        [SMEM] * 2 + [VMEM] * 5 + [HELD],
        scratch=[gn],
        flops=2 * MICROSECOND,
    )
    back_far = [straight_back(b, d) for d, b in zip(steps, far_back)]
    own_same, own_below, gself, emb = call(
        lambda *r: back_own_kernel(block, *r),
        [two, one, ((rows, width), F32), two],
        (lists, live, tiles_t, gpool, msg_a, q, g, sw, pre, far_back[0]),
        [SMEM] * 2 + [VMEM] * 7 + [HELD],
        scratch=[pltpu.VMEM((2 * block, hidden), BF16)],
        flops=3 * MICROSECOND,
    )
    g_same = swap_rows(own_same, 0)
    total = pltpu.VMEM((rows, width), F32)
    (sum_below,) = call(
        lambda *r: sum_near_kernel(block, *r),
        [two],
        (place, lists, *metas, own_below, *back_near),
        [SMEM] * 5 + [VMEM] * 4,
        scratch=[total],
        flops=20 * MICROSECOND,
    )
    g_below = swap_rows(sum_below, -LINE)
    (placed,) = call(
        place_kernel,
        [((rows, width), F32)],
        (gself, *back_far),
        [VMEM] * 4,
        flops=20 * MICROSECOND,
    )
    (grad,) = call(finish_kernel, [two], (live, placed, g_same, g_below), [SMEM] + [VMEM] * 3)
    return emb[None], grad[None]


def solution(mesh):
    data = P("side", "dom", None)
    return jax.shard_map(
        local,
        mesh=mesh,
        in_specs=(
            data,
            P("side", "dom"),
            P("side", "dom", None, None),
            data,
            data,
            P(),
            P(),
            P(),
            P(),
            P(),
        ),
        out_specs=(data, data),
        check_vma=False,
    )
```

```python
import jax
import jax.numpy as jnp
from jax import lax
from jax.experimental import pallas as pl
from jax.experimental.pallas import tpu as pltpu
from jax.sharding import PartitionSpec as P

EPS = 1e-06
DEAD = 16384.0
LIMIT = 8192.0
MICROSECOND = 10**9
LINE = 4
F32 = jnp.float32
BF16 = jnp.bfloat16
VMEM = pl.BlockSpec(memory_space=pltpu.VMEM)
HELD = pl.BlockSpec(memory_space=pl.ANY)
SMEM = pl.BlockSpec(memory_space=pltpu.SMEM)


def dot(a, b, ca=1, cb=0):
    return lax.dot_general(a, b, (((ca,), (cb,)), ((), ())), preferred_element_type=F32)


def call(kernel, outs, ins, in_specs=None, scratch=(), limit=24, flops=0):
    return pl.pallas_call(
        kernel,
        out_shape=[jax.ShapeDtypeStruct(s, d) for s, d in outs],
        in_specs=in_specs or [VMEM] * len(ins),
        out_specs=[VMEM] * len(outs),
        scratch_shapes=list(scratch),
        compiler_params=pltpu.CompilerParams(vmem_limit_bytes=limit << 20),
        cost_estimate=pl.CostEstimate(flops=flops, bytes_accessed=1 << 20, transcendentals=0),
    )(*ins)


def swap_rows(x, shift):
    count = lax.axis_size("dom")
    pairs = [
        (s * count + j, (1 - s) * count + (j + shift) % count)
        for s in range(2)
        for j in range(count)
    ]
    return lax.ppermute(x, ("side", "dom"), pairs)


def along(x, d):
    count = lax.axis_size("dom")
    pairs = [(j, j // LINE * LINE + (j + d) % LINE) for j in range(count)]
    return lax.ppermute(x, "dom", pairs)


def straight_back(x, d):
    count = lax.axis_size("dom")
    pairs = []
    for s in range(2):
        for j in range(count):
            to = j + d if j % LINE + d < LINE else j + d + LINE
            pairs.append(((1 - s) * count + to % count, s * count + j))
    return lax.ppermute(x, ("side", "dom"), pairs)


def near(p, d):
    return jnp.where(p >= d, d + LINE, d)


def far(p, d):
    return jnp.where(p >= d, d, d + LINE)


def at_block(index, block):
    return pl.ds(pl.multiple_of(index * block, block), block)


def pick_near_kernel(block, place_ref, m1, m2, m3, rows_ref, _, *outs):
    for d, (meta, out) in enumerate(zip((m1, m2, m3), outs), 1):
        p = lax.rem(place_ref[0] + d, LINE)
        out[...] = rows_ref[at_block(meta[0, near(p, d)], block), :]


def pick_far_kernel(block, place_ref, m1, m2, m3, same_ref, below_ref, *outs):
    for d, (meta, out) in enumerate(zip((m1, m2, m3), outs), 1):
        p = lax.rem(place_ref[0] + d, LINE)
        at = at_block(meta[0, far(p, d)], block)

        @pl.when(p >= d)
        def _():
            out[...] = same_ref[at, :]

        @pl.when(p < d)
        def _():
            out[...] = below_ref[at, :]


def slots(p):
    return [0, LINE] + [near(p, d) for d in range(1, LINE)] + [far(p, d) for d in range(1, LINE)]


def tiles_kernel(block, place_ref, lists_ref, counts_ref, x_ref, sw_ref, tiles_ref, tiles_t_ref, self_ref):
    for i, o in enumerate(slots(place_ref[0])):
        first, second = lists_ref[o, 0], lists_ref[o, 1]
        at = pl.ds(pl.multiple_of((o * 2 + second) * block, block), block)
        tile = (counts_ref[:, at] * (first + second)).astype(F32)
        tiles_ref[:, i * block : (i + 1) * block] = tile.astype(BF16)
        tiles_t_ref[i * block : (i + 1) * block, :] = tile.T.astype(BF16)
    self_ref[...] = dot(x_ref[...], sw_ref[...])


def message_kernel(block, first, last, *refs):
    size = last - first
    if first == 0:
        lists_ref, same_ref, below_ref = refs[:3]
        held = [same_ref[at_block(lists_ref[0, 1], block), :]]
        held += [below_ref[at_block(lists_ref[LINE, 1], block), :]]
        refs = refs[3:]
        held += [b[...] for b in refs[: size - 2]]
        refs = refs[size - 2 :]
    else:
        held = [b[...] for b in refs[:size]]
        refs = refs[size:]
    q_ref, qb_ref, tiles_ref = refs[:3]
    acc_in, deg_in = refs[3:5] if first else (None, None)
    msg_ref, acc_ref, deg_ref = refs[-3:]
    x = jnp.concatenate(held, axis=0)
    keep = x[:, :128].astype(F32) < LIMIT
    tiles = tiles_ref[:, first * block : last * block]
    deg = dot(tiles, jnp.where(keep, 1.0, 0.0).astype(BF16))
    deg_ref[...] = deg + deg_in[...] if first else deg
    keep = keep[:, :1]
    hidden = q_ref.shape[1]
    step = 512
    for n in range(hidden // step):
        cols = slice(n * step, (n + 1) * step)
        pre = dot(x, q_ref[:, cols]) + qb_ref[:, cols]
        msg = jnp.where(keep, jnp.maximum(pre, 0.0), 0.0).astype(BF16)
        msg_ref[:, cols] = msg
        acc = dot(tiles, msg)
        acc_ref[:, cols] = acc + acc_in[:, cols] if first else acc


def layer_kernel(
    block, live_ref, got_a, got_b, got_c, q_ref, qb_ref, tiles_ref, acc_ref, deg_ref, self_ref, up_ref, nb_ref, ob_ref, tt_ref,
    msg_ref, g_ref, gpool_ref, pre_ref, last_ref, near1, near2, near3, pooled_ref, gn_ref,
):
    rows, width = self_ref.shape
    hidden = nb_ref.shape[0]
    step = 512
    x = jnp.concatenate([got_a[...], got_b[...], got_c[...]], axis=0)
    keep = x[:, :128].astype(F32) < LIMIT
    tiles = tiles_ref[:, -3 * block :]
    deg = deg_ref[...] + dot(tiles, jnp.where(keep, 1.0, 0.0).astype(BF16))
    inv_deg = 1.0 / (1.0 + deg[:, :1])
    keep = keep[:, :1]
    for n in range(hidden // step):
        cols = slice(n * step, (n + 1) * step)
        pre = dot(x, q_ref[:, cols]) + qb_ref[:, cols]
        msg = jnp.where(keep, jnp.maximum(pre, 0.0), 0.0).astype(BF16)
        last_ref[:, cols] = msg
        pooled_ref[:, cols] = ((acc_ref[:, cols] + dot(tiles, msg)) * inv_deg).astype(BF16)
    pooled = pooled_ref[...]
    for n in range(width // step):
        cols = slice(n * step, (n + 1) * step)
        pre_ref[:, cols] = self_ref[:, cols] + dot(pooled, nb_ref[:, cols]) + ob_ref[:, cols]
    pre = pre_ref[...]
    act = jnp.maximum(pre, 0.0)
    inv = lax.rsqrt(jnp.mean(act * act, axis=1, keepdims=True) + EPS)
    keep = lax.broadcasted_iota(jnp.int32, (rows, 1), 0) < live_ref[0]
    up = jnp.where(keep, up_ref[...].astype(F32), 0.0)
    inner = jnp.sum(up * act, axis=1, keepdims=True) / width
    g = inv * up - act * (inv * inv * inv * inner)
    g = jnp.where(pre > 0, g, 0.0).astype(BF16)
    g_ref[...] = g
    for n in range(hidden // step):
        cols = slice(n * step, (n + 1) * step)
        gpool_ref[:, cols] = (dot(g, nb_ref[cols, :], 1, 1) * inv_deg).astype(BF16)

    def store(cols, part):
        for i, out in enumerate((near1, near2, near3)):
            out[:, cols] = part[i * block : (i + 1) * block].astype(BF16)

    back_dot(2 * block, tt_ref, gpool_ref, [msg_ref[2 * block :, :]], q_ref, gn_ref, store)


def back_dot(first, tt_ref, gpool_ref, messages, q_ref, gn_ref, store):
    rows = gn_ref.shape[0]
    tt = tt_ref[first : first + rows, :]
    step = 512
    for n in range(gpool_ref.shape[1] // step):
        cols = slice(n * step, (n + 1) * step)
        live = jnp.concatenate([m[:, cols] for m in messages], axis=0).astype(F32) > 0
        gn_ref[:, cols] = jnp.where(live, dot(tt, gpool_ref[:, cols]), 0.0).astype(BF16)
    gn = gn_ref[...]
    for n in range(q_ref.shape[0] // step):
        cols = slice(n * step, (n + 1) * step)
        store(cols, dot(gn, q_ref[cols, :], 1, 1))


def back_far_kernel(block, place_ref, lists_ref, tt_ref, gpool_ref, msg_ref, q_ref, _, *refs):
    outs, gn_ref = refs[:-1], refs[-1]
    width = q_ref.shape[0]

    def store(cols, part):
        for i, out in enumerate(outs):
            out[:, cols] = part[i * block : (i + 1) * block].astype(BF16)

    for d, out in enumerate(outs, 1):
        which = lists_ref[far(place_ref[0], d), 1].astype(F32)
        out[:, width:] = jnp.full((block, 128), which, F32).astype(BF16)
    back_dot((1 + LINE) * block, tt_ref, gpool_ref, [msg_ref[...]], q_ref, gn_ref, store)


def back_own_kernel(block, lists_ref, tt_ref, gpool_ref, msg_ref, q_ref, _, same_ref, below_ref, gn_ref):
    same_ref[...] = jnp.zeros_like(same_ref)
    at = at_block(lists_ref[0, 1], block)

    def store(cols, part):
        same_ref[at, cols] = part[:block].astype(BF16)
        below_ref[:, cols] = part[block:].astype(BF16)

    back_dot(0, tt_ref, gpool_ref, [msg_ref[: 2 * block, :]], q_ref, gn_ref, store)


def own_rows_kernel(live_ref, g_ref, sw_ref, pre_ref, _, gself_ref, emb_ref):
    rows, width = pre_ref.shape
    step = 512
    for n in range(width // step):
        cols = slice(n * step, (n + 1) * step)
        gself_ref[:, cols] = dot(g_ref[...], sw_ref[cols, :], 1, 1)
    act = jnp.maximum(pre_ref[...], 0.0)
    inv = lax.rsqrt(jnp.mean(act * act, axis=1, keepdims=True) + EPS)
    keep = lax.broadcasted_iota(jnp.int32, (rows, 1), 0) < live_ref[0]
    emb_ref[...] = jnp.where(keep, act * inv, 0.0).astype(BF16)


def sum_near_kernel(block, place_ref, lists_ref, m1, m2, m3, own_ref, d1, d2, d3, out_ref, total):
    total[...] = jnp.zeros_like(total)
    total[at_block(lists_ref[LINE, 1], block), :] = own_ref[...].astype(F32)
    for d, (meta, part) in enumerate(zip((m1, m2, m3), (d1, d2, d3)), 1):
        p = lax.rem(place_ref[0] + d, LINE)
        total[at_block(meta[0, near(p, d)], block), :] += part[...].astype(F32)
    out_ref[...] = total[...].astype(BF16)


def place_kernel(gself_ref, c1, c2, c3, total_ref):
    block, width = c1.shape[0], gself_ref.shape[1]
    first, second = gself_ref[:block, :], gself_ref[block:, :]
    for part in (c1, c2, c3):
        grad = part[:, :width].astype(F32)
        late = part[:, width : width + 1].astype(F32) > 0.5
        first += jnp.where(late, 0.0, grad)
        second += jnp.where(late, grad, 0.0)
    total_ref[:block, :] = first
    total_ref[block:, :] = second


def finish_kernel(live_ref, total_ref, same_ref, below_ref, out_ref):
    total = total_ref[...] + same_ref[...].astype(F32) + below_ref[...].astype(F32)
    keep = lax.broadcasted_iota(jnp.int32, (total.shape[0], 1), 0) < live_ref[0]
    out_ref[...] = jnp.where(keep, total, 0.0).astype(BF16)


def local(x, live, listed, counts, cotangent, q, qb, sw, nb, ob):
    x, lists, counts, up = x[0], listed[0, 0], counts[0], cotangent[0]
    live = live.reshape(1)
    rows, width = x.shape
    hidden = q.shape[1]
    reach, block_count = lists.shape
    block = rows // block_count
    qb, ob = qb[None], ob[None]
    place = (lax.axis_index("dom") % LINE).astype(jnp.int32).reshape(1)
    keep = lax.broadcasted_iota(jnp.int32, (rows, 1), 0) < live[0]
    marked = jnp.where(keep, x, jnp.asarray(DEAD, BF16))
    row = jnp.pad(lists[:, 1], (0, 128 - reach))[None]
    steps = range(1, LINE)
    one, two = ((block, width), BF16), ((rows, width), BF16)

    below = swap_rows(marked, LINE)
    same = swap_rows(marked, 0)
    metas = [along(row, -d) for d in steps]
    later, *metas = lax.optimization_barrier((marked, *metas))
    below2 = swap_rows(later, 2 * LINE)
    scalars = [SMEM] * (1 + len(steps))
    tiles, tiles_t, self_pre = call(
        lambda *r: tiles_kernel(block, *r),
        [((rows, reach * block), BF16), ((reach * block, rows), BF16), ((rows, width), F32)],
        (place, lists, counts, x, sw),
        [SMEM] * 2 + [VMEM] * 3,
        flops=2 * rows * width * width,
    )
    sent = call(
        lambda *r: pick_near_kernel(block, *r),
        [one] * len(steps),
        (place, *metas, below, tiles),
        scalars + [VMEM, HELD],
    )
    got_near = [along(b, d) for d, b in zip(steps, sent)]
    sent = call(
        lambda *r: pick_far_kernel(block, *r),
        [one] * len(steps),
        (place, *metas, same, below2),
        scalars + [VMEM] * 2,
    )
    got_far = [along(b, d) for d, b in zip(steps, sent)]
    split = 1 + LINE

    def message(first, last, ins, specs):
        size = last - first
        return call(
            lambda *r: message_kernel(block, first, last, *r),
            [((size * block, hidden), BF16), ((rows, hidden), F32), ((rows, 128), F32)],
            ins,
            specs,
            flops=2 * size * block * hidden * (width + rows),
        )

    msg_a, acc, deg = message(
        0, split, (lists, same, below, *got_near, q, qb, tiles), [SMEM] + [VMEM] * 8
    )
    gn = pltpu.VMEM((3 * block, hidden), BF16)
    g, gpool, pre, msg_b, *near_back = call(
        lambda *r: layer_kernel(block, *r),
        [two, ((rows, hidden), BF16), ((rows, width), F32), ((3 * block, hidden), BF16)] + [one] * 3,
        (live, *got_far, q, qb, tiles, acc, deg, self_pre, up, nb, ob, tiles_t, msg_a),
        [SMEM] + [VMEM] * 14,
        scratch=[pltpu.VMEM((rows, hidden), BF16), gn],
        flops=8 * MICROSECOND,
    )
    back_near = [along(b, -d) for d, b in zip(steps, near_back)]
    far_back = call(
        lambda *r: back_far_kernel(block, *r),
        [((block, width + 128), BF16)] * 3,
        (place, lists, tiles_t, gpool, msg_b, q, near_back[0]),
        [SMEM] * 2 + [VMEM] * 4 + [HELD],
        scratch=[gn],
        flops=2 * MICROSECOND,
    )
    back_far = [straight_back(b, d) for d, b in zip(steps, far_back)]
    own_same, own_below = call(
        lambda *r: back_own_kernel(block, *r),
        [two, one],
        (lists, tiles_t, gpool, msg_a, q, far_back[0]),
        [SMEM] + [VMEM] * 4 + [HELD],
        scratch=[pltpu.VMEM((2 * block, hidden), BF16)],
        flops=2 * MICROSECOND,
    )
    g_same = swap_rows(own_same, 0)
    total = pltpu.VMEM((rows, width), F32)
    (sum_below,) = call(
        lambda *r: sum_near_kernel(block, *r),
        [two],
        (place, lists, *metas, own_below, *back_near),
        [SMEM] * 5 + [VMEM] * 4,
        scratch=[total],
        flops=20 * MICROSECOND,
    )
    g_below = swap_rows(sum_below, -LINE)
    gself, emb = call(
        own_rows_kernel,
        [((rows, width), F32), two],
        (live, g, sw, pre, sum_below),
        [SMEM] + [VMEM] * 3 + [HELD],
        flops=2 * MICROSECOND,
    )
    (placed,) = call(
        place_kernel,
        [((rows, width), F32)],
        (gself, *back_far),
        [VMEM] * 4,
        flops=20 * MICROSECOND,
    )
    (grad,) = call(finish_kernel, [two], (live, placed, g_same, g_below), [SMEM] + [VMEM] * 3)
    return emb[None], grad[None]


def solution(mesh):
    data = P("side", "dom", None)
    return jax.shard_map(
        local,
        mesh=mesh,
        in_specs=(
            data,
            P("side", "dom"),
            P("side", "dom", None, None),
            data,
            data,
            P(),
            P(),
            P(),
            P(),
            P(),
        ),
        out_specs=(data, data),
        check_vma=False,
    )
```

```python
import jax
import jax.numpy as jnp
from jax import lax
from jax.experimental import pallas as pl
from jax.experimental.pallas import tpu as pltpu
from jax.sharding import PartitionSpec as P

EPS = 1e-06
DEAD = 16384.0
LIMIT = 8192.0
MICROSECOND = 10**9
LINE = 4
F32 = jnp.float32
BF16 = jnp.bfloat16
VMEM = pl.BlockSpec(memory_space=pltpu.VMEM)
HELD = pl.BlockSpec(memory_space=pl.ANY)
SMEM = pl.BlockSpec(memory_space=pltpu.SMEM)


def dot(a, b, ca=1, cb=0):
    return lax.dot_general(a, b, (((ca,), (cb,)), ((), ())), preferred_element_type=F32)


def call(kernel, outs, ins, in_specs=None, scratch=(), limit=24, flops=0):
    return pl.pallas_call(
        kernel,
        out_shape=[jax.ShapeDtypeStruct(s, d) for s, d in outs],
        in_specs=in_specs or [VMEM] * len(ins),
        out_specs=[VMEM] * len(outs),
        scratch_shapes=list(scratch),
        compiler_params=pltpu.CompilerParams(vmem_limit_bytes=limit << 20),
        cost_estimate=pl.CostEstimate(flops=flops, bytes_accessed=1 << 20, transcendentals=0),
    )(*ins)


def swap_rows(x, shift):
    count = lax.axis_size("dom")
    pairs = [
        (s * count + j, (1 - s) * count + (j + shift) % count)
        for s in range(2)
        for j in range(count)
    ]
    return lax.ppermute(x, ("side", "dom"), pairs)


def along(x, d):
    count = lax.axis_size("dom")
    pairs = [(j, j // LINE * LINE + (j + d) % LINE) for j in range(count)]
    return lax.ppermute(x, "dom", pairs)


def straight_back(x, d):
    count = lax.axis_size("dom")
    pairs = []
    for s in range(2):
        for j in range(count):
            to = j + d if j % LINE + d < LINE else j + d + LINE
            pairs.append(((1 - s) * count + to % count, s * count + j))
    return lax.ppermute(x, ("side", "dom"), pairs)


def near(p, d):
    return jnp.where(p >= d, d + LINE, d)


def far(p, d):
    return jnp.where(p >= d, d, d + LINE)


def at_block(index, block):
    return pl.ds(pl.multiple_of(index * block, block), block)


def pick_near_kernel(block, place_ref, m1, m2, m3, rows_ref, *outs):
    for d, (meta, out) in enumerate(zip((m1, m2, m3), outs), 1):
        p = lax.rem(place_ref[0] + d, LINE)
        out[...] = rows_ref[at_block(meta[0, near(p, d)], block), :]


def pick_far_kernel(block, place_ref, m1, m2, m3, same_ref, below_ref, *outs):
    for d, (meta, out) in enumerate(zip((m1, m2, m3), outs), 1):
        p = lax.rem(place_ref[0] + d, LINE)
        at = at_block(meta[0, far(p, d)], block)

        @pl.when(p >= d)
        def _():
            out[...] = same_ref[at, :]

        @pl.when(p < d)
        def _():
            out[...] = below_ref[at, :]


def slots(p):
    return [0, LINE] + [near(p, d) for d in range(1, LINE)] + [far(p, d) for d in range(1, LINE)]


def tiles_kernel(block, place_ref, lists_ref, counts_ref, x_ref, sw_ref, _, tiles_ref, tiles_t_ref, self_ref):
    for i, o in enumerate(slots(place_ref[0])):
        first, second = lists_ref[o, 0], lists_ref[o, 1]
        at = pl.ds(pl.multiple_of((o * 2 + second) * block, block), block)
        tile = (counts_ref[:, at] * (first + second)).astype(F32)
        tiles_ref[:, i * block : (i + 1) * block] = tile.astype(BF16)
        tiles_t_ref[i * block : (i + 1) * block, :] = tile.T.astype(BF16)
    self_ref[...] = dot(x_ref[...], sw_ref[...])


def message_kernel(block, first, last, *refs):
    size = last - first
    if first == 0:
        lists_ref, same_ref, below_ref = refs[:3]
        held = [same_ref[at_block(lists_ref[0, 1], block), :]]
        held += [below_ref[at_block(lists_ref[LINE, 1], block), :]]
        refs = refs[3:]
        held += [b[...] for b in refs[: size - 2]]
        refs = refs[size - 2 :]
    else:
        held = [b[...] for b in refs[:size]]
        refs = refs[size:]
    q_ref, qb_ref, tiles_ref = refs[:3]
    acc_in, deg_in = refs[3:5] if first else (None, None)
    msg_ref, acc_ref, deg_ref = refs[-3:]
    x = jnp.concatenate(held, axis=0)
    keep = x[:, :128].astype(F32) < LIMIT
    tiles = tiles_ref[:, first * block : last * block]
    deg = dot(tiles, jnp.where(keep, 1.0, 0.0).astype(BF16))
    deg_ref[...] = deg + deg_in[...] if first else deg
    keep = keep[:, :1]
    hidden = q_ref.shape[1]
    step = 512
    for n in range(hidden // step):
        cols = slice(n * step, (n + 1) * step)
        pre = dot(x, q_ref[:, cols]) + qb_ref[:, cols]
        msg = jnp.where(keep, jnp.maximum(pre, 0.0), 0.0).astype(BF16)
        msg_ref[:, cols] = msg
        acc = dot(tiles, msg)
        acc_ref[:, cols] = acc + acc_in[:, cols] if first else acc


def layer_kernel(
    block, live_ref, place_ref, lists_ref, got_a, got_b, got_c, q_ref, qb_ref, tiles_ref, acc_ref, deg_ref, self_ref, up_ref, nb_ref, ob_ref, tt_ref,
    msg_ref, g_ref, gpool_ref, pre_ref, last_ref, near1, near2, near3, far1, pooled_ref, gn_ref,
):
    rows, width = self_ref.shape
    hidden = nb_ref.shape[0]
    step = 512
    x = jnp.concatenate([got_a[...], got_b[...], got_c[...]], axis=0)
    keep = x[:, :128].astype(F32) < LIMIT
    tiles = tiles_ref[:, -3 * block :]
    deg = deg_ref[...] + dot(tiles, jnp.where(keep, 1.0, 0.0).astype(BF16))
    inv_deg = 1.0 / (1.0 + deg[:, :1])
    keep = keep[:, :1]
    for n in range(hidden // step):
        cols = slice(n * step, (n + 1) * step)
        pre = dot(x, q_ref[:, cols]) + qb_ref[:, cols]
        msg = jnp.where(keep, jnp.maximum(pre, 0.0), 0.0).astype(BF16)
        last_ref[:, cols] = msg
        pooled_ref[:, cols] = ((acc_ref[:, cols] + dot(tiles, msg)) * inv_deg).astype(BF16)
    pooled = pooled_ref[...]
    for n in range(width // step):
        cols = slice(n * step, (n + 1) * step)
        pre_ref[:, cols] = self_ref[:, cols] + dot(pooled, nb_ref[:, cols]) + ob_ref[:, cols]
    pre = pre_ref[...]
    act = jnp.maximum(pre, 0.0)
    inv = lax.rsqrt(jnp.mean(act * act, axis=1, keepdims=True) + EPS)
    keep = lax.broadcasted_iota(jnp.int32, (rows, 1), 0) < live_ref[0]
    up = jnp.where(keep, up_ref[...].astype(F32), 0.0)
    inner = jnp.sum(up * act, axis=1, keepdims=True) / width
    g = inv * up - act * (inv * inv * inv * inner)
    g = jnp.where(pre > 0, g, 0.0).astype(BF16)
    g_ref[...] = g
    for n in range(hidden // step):
        cols = slice(n * step, (n + 1) * step)
        gpool_ref[:, cols] = (dot(g, nb_ref[cols, :], 1, 1) * inv_deg).astype(BF16)

    def store(cols, part):
        for i, out in enumerate((near1, near2, near3, far1)):
            out[:, cols] = part[i * block : (i + 1) * block].astype(BF16)

    mark_block(place_ref, lists_ref, 1, far1, width)
    messages = [msg_ref[2 * block :, :], last_ref[:block, :]]
    back_dot(2 * block, tt_ref, gpool_ref, messages, q_ref, gn_ref, store)


def mark_block(place_ref, lists_ref, d, out, width):
    which = lists_ref[far(place_ref[0], d), 1].astype(F32)
    out[:, width:] = jnp.full((out.shape[0], out.shape[1] - width), which, F32).astype(BF16)


def back_dot(first, tt_ref, gpool_ref, messages, q_ref, gn_ref, store):
    rows = gn_ref.shape[0]
    tt = tt_ref[first : first + rows, :]
    step = 512
    for n in range(gpool_ref.shape[1] // step):
        cols = slice(n * step, (n + 1) * step)
        live = jnp.concatenate([m[:, cols] for m in messages], axis=0).astype(F32) > 0
        gn_ref[:, cols] = jnp.where(live, dot(tt, gpool_ref[:, cols]), 0.0).astype(BF16)
    gn = gn_ref[...]
    for n in range(q_ref.shape[0] // step):
        cols = slice(n * step, (n + 1) * step)
        store(cols, dot(gn, q_ref[cols, :], 1, 1))


def back_far_kernel(block, place_ref, lists_ref, tt_ref, gpool_ref, msg_ref, q_ref, _, *refs):
    outs, gn_ref = refs[:-1], refs[-1]
    width = q_ref.shape[0]

    def store(cols, part):
        for i, out in enumerate(outs):
            out[:, cols] = part[i * block : (i + 1) * block].astype(BF16)

    for d, out in enumerate(outs, 2):
        mark_block(place_ref, lists_ref, d, out, width)
    back_dot((2 + LINE) * block, tt_ref, gpool_ref, [msg_ref[block:, :]], q_ref, gn_ref, store)


def back_own_kernel(block, lists_ref, tt_ref, gpool_ref, msg_ref, q_ref, _, same_ref, below_ref, gn_ref):
    same_ref[...] = jnp.zeros_like(same_ref)
    at = at_block(lists_ref[0, 1], block)

    def store(cols, part):
        same_ref[at, cols] = part[:block].astype(BF16)
        below_ref[:, cols] = part[block:].astype(BF16)

    back_dot(0, tt_ref, gpool_ref, [msg_ref[: 2 * block, :]], q_ref, gn_ref, store)


def own_rows_kernel(live_ref, g_ref, sw_ref, pre_ref, _, gself_ref, emb_ref):
    rows, width = pre_ref.shape
    step = 512
    for n in range(width // step):
        cols = slice(n * step, (n + 1) * step)
        gself_ref[:, cols] = dot(g_ref[...], sw_ref[cols, :], 1, 1)
    act = jnp.maximum(pre_ref[...], 0.0)
    inv = lax.rsqrt(jnp.mean(act * act, axis=1, keepdims=True) + EPS)
    keep = lax.broadcasted_iota(jnp.int32, (rows, 1), 0) < live_ref[0]
    emb_ref[...] = jnp.where(keep, act * inv, 0.0).astype(BF16)


def sum_near_kernel(block, place_ref, lists_ref, m1, m2, m3, own_ref, d1, d2, d3, out_ref, total):
    total[...] = jnp.zeros_like(total)
    total[at_block(lists_ref[LINE, 1], block), :] = own_ref[...].astype(F32)
    for d, (meta, part) in enumerate(zip((m1, m2, m3), (d1, d2, d3)), 1):
        p = lax.rem(place_ref[0] + d, LINE)
        total[at_block(meta[0, near(p, d)], block), :] += part[...].astype(F32)
    out_ref[...] = total[...].astype(BF16)


def place_kernel(gself_ref, c1, c2, c3, total_ref):
    block, width = c1.shape[0], gself_ref.shape[1]
    first, second = gself_ref[:block, :], gself_ref[block:, :]
    for part in (c1, c2, c3):
        grad = part[:, :width].astype(F32)
        late = part[:, width : width + 1].astype(F32) > 0.5
        first += jnp.where(late, 0.0, grad)
        second += jnp.where(late, grad, 0.0)
    total_ref[:block, :] = first
    total_ref[block:, :] = second


def finish_kernel(live_ref, total_ref, same_ref, below_ref, out_ref):
    total = total_ref[...] + same_ref[...].astype(F32) + below_ref[...].astype(F32)
    keep = lax.broadcasted_iota(jnp.int32, (total.shape[0], 1), 0) < live_ref[0]
    out_ref[...] = jnp.where(keep, total, 0.0).astype(BF16)


def local(x, live, listed, counts, cotangent, q, qb, sw, nb, ob):
    x, lists, counts, up = x[0], listed[0, 0], counts[0], cotangent[0]
    live = live.reshape(1)
    rows, width = x.shape
    hidden = q.shape[1]
    reach, block_count = lists.shape
    block = rows // block_count
    qb, ob = qb[None], ob[None]
    place = (lax.axis_index("dom") % LINE).astype(jnp.int32).reshape(1)
    keep = lax.broadcasted_iota(jnp.int32, (rows, 1), 0) < live[0]
    marked = jnp.where(keep, x, jnp.asarray(DEAD, BF16))
    row = jnp.pad(lists[:, 1], (0, 128 - reach))[None]
    steps = range(1, LINE)
    one, two = ((block, width), BF16), ((rows, width), BF16)

    below = swap_rows(marked, LINE)
    same = swap_rows(marked, 0)
    metas = [along(row, -d) for d in steps]
    later, *metas = lax.optimization_barrier((marked, *metas))
    below2 = swap_rows(later, 2 * LINE)
    scalars = [SMEM] * (1 + len(steps))
    sent = call(
        lambda *r: pick_near_kernel(block, *r),
        [one] * len(steps),
        (place, *metas, below),
        scalars + [VMEM],
    )
    got_near = [along(b, d) for d, b in zip(steps, sent)]
    sent = call(
        lambda *r: pick_far_kernel(block, *r),
        [one] * len(steps),
        (place, *metas, same, below2),
        scalars + [VMEM] * 2,
    )
    got_far = [along(b, d) for d, b in zip(steps, sent)]
    tiles, tiles_t, self_pre = call(
        lambda *r: tiles_kernel(block, *r),
        [((rows, reach * block), BF16), ((reach * block, rows), BF16), ((rows, width), F32)],
        (place, lists, counts, x, sw, sent[0]),
        [SMEM] * 2 + [VMEM] * 3 + [HELD],
        flops=2 * rows * width * width,
    )
    split = 1 + LINE

    def message(first, last, ins, specs):
        size = last - first
        return call(
            lambda *r: message_kernel(block, first, last, *r),
            [((size * block, hidden), BF16), ((rows, hidden), F32), ((rows, 128), F32)],
            ins,
            specs,
            flops=2 * size * block * hidden * (width + rows),
        )

    msg_a, acc, deg = message(
        0, split, (lists, same, below, *got_near, q, qb, tiles), [SMEM] + [VMEM] * 8
    )
    g, gpool, pre, msg_b, *near_back, far_first = call(
        lambda *r: layer_kernel(block, *r),
        [two, ((rows, hidden), BF16), ((rows, width), F32), ((3 * block, hidden), BF16)] + [one] * 3 + [((block, width + 128), BF16)],
        (live, place, lists, *got_far, q, qb, tiles, acc, deg, self_pre, up, nb, ob, tiles_t, msg_a),
        [SMEM] * 3 + [VMEM] * 14,
        scratch=[pltpu.VMEM((rows, hidden), BF16), pltpu.VMEM((4 * block, hidden), BF16)],
        flops=8 * MICROSECOND,
    )
    back_near = [along(b, -d) for d, b in zip(steps, near_back)]
    far_back = call(
        lambda *r: back_far_kernel(block, *r),
        [((block, width + 128), BF16)] * 2,
        (place, lists, tiles_t, gpool, msg_b, q, near_back[0]),
        [SMEM] * 2 + [VMEM] * 4 + [HELD],
        scratch=[pltpu.VMEM((2 * block, hidden), BF16)],
        flops=2 * MICROSECOND,
    )
    back_far = [straight_back(b, d) for d, b in zip(steps, (far_first, *far_back))]
    own_same, own_below = call(
        lambda *r: back_own_kernel(block, *r),
        [two, one],
        (lists, tiles_t, gpool, msg_a, q, far_back[0]),
        [SMEM] + [VMEM] * 4 + [HELD],
        scratch=[pltpu.VMEM((2 * block, hidden), BF16)],
        flops=2 * MICROSECOND,
    )
    g_same = swap_rows(own_same, 0)
    total = pltpu.VMEM((rows, width), F32)
    (sum_below,) = call(
        lambda *r: sum_near_kernel(block, *r),
        [two],
        (place, lists, *metas, own_below, *back_near),
        [SMEM] * 5 + [VMEM] * 4,
        scratch=[total],
        flops=20 * MICROSECOND,
    )
    g_below = swap_rows(sum_below, -LINE)
    gself, emb = call(
        own_rows_kernel,
        [((rows, width), F32), two],
        (live, g, sw, pre, sum_below),
        [SMEM] + [VMEM] * 3 + [HELD],
        flops=2 * MICROSECOND,
    )
    (placed,) = call(
        place_kernel,
        [((rows, width), F32)],
        (gself, *back_far),
        [VMEM] * 4,
        flops=20 * MICROSECOND,
    )
    (grad,) = call(finish_kernel, [two], (live, placed, g_same, g_below), [SMEM] + [VMEM] * 3)
    return emb[None], grad[None]


def solution(mesh):
    data = P("side", "dom", None)
    return jax.shard_map(
        local,
        mesh=mesh,
        in_specs=(
            data,
            P("side", "dom"),
            P("side", "dom", None, None),
            data,
            data,
            P(),
            P(),
            P(),
            P(),
            P(),
        ),
        out_specs=(data, data),
        check_vma=False,
    )
```

```python
import jax
import jax.numpy as jnp
from jax import lax
from jax.experimental import pallas as pl
from jax.experimental.pallas import tpu as pltpu
from jax.sharding import PartitionSpec as P

EPS = 1e-06
DEAD = 16384.0
LIMIT = 8192.0
MICROSECOND = 10**9
LINE = 4
F32 = jnp.float32
BF16 = jnp.bfloat16
VMEM = pl.BlockSpec(memory_space=pltpu.VMEM)
HELD = pl.BlockSpec(memory_space=pl.ANY)
SMEM = pl.BlockSpec(memory_space=pltpu.SMEM)


def dot(a, b, ca=1, cb=0):
    return lax.dot_general(a, b, (((ca,), (cb,)), ((), ())), preferred_element_type=F32)


def call(kernel, outs, ins, in_specs=None, scratch=(), limit=24, flops=0):
    return pl.pallas_call(
        kernel,
        out_shape=[jax.ShapeDtypeStruct(s, d) for s, d in outs],
        in_specs=in_specs or [VMEM] * len(ins),
        out_specs=[VMEM] * len(outs),
        scratch_shapes=list(scratch),
        compiler_params=pltpu.CompilerParams(vmem_limit_bytes=limit << 20),
        cost_estimate=pl.CostEstimate(flops=flops, bytes_accessed=1 << 20, transcendentals=0),
    )(*ins)


def swap_rows(x, shift):
    count = lax.axis_size("dom")
    pairs = [
        (s * count + j, (1 - s) * count + (j + shift) % count)
        for s in range(2)
        for j in range(count)
    ]
    return lax.ppermute(x, ("side", "dom"), pairs)


def along(x, d):
    count = lax.axis_size("dom")
    pairs = [(j, j // LINE * LINE + (j + d) % LINE) for j in range(count)]
    return lax.ppermute(x, "dom", pairs)


def straight_back(x, d):
    count = lax.axis_size("dom")
    pairs = []
    for s in range(2):
        for j in range(count):
            to = j + d if j % LINE + d < LINE else j + d + LINE
            pairs.append(((1 - s) * count + to % count, s * count + j))
    return lax.ppermute(x, ("side", "dom"), pairs)


def two_back(x):
    count = lax.axis_size("dom")
    pairs = [
        (s * count + j, (1 - s) * count + (j - 2 * LINE) % count)
        for s in range(2)
        for j in range(0, count, LINE)
    ]
    return lax.ppermute(x, ("side", "dom"), pairs)


def turn(x):
    count = lax.axis_size("dom")
    pairs = []
    for s in range(2):
        for j in range(count):
            to = (1 - s) * count + j - 1 if j % LINE else s * count + j + LINE - 1
            pairs.append((s * count + j, to))
    return lax.ppermute(x, ("side", "dom"), pairs)


def near(p, d):
    return jnp.where(p >= d, d + LINE, d)


def far(p, d):
    return jnp.where(p >= d, d, d + LINE)


def at_block(index, block):
    return pl.ds(pl.multiple_of(index * block, block), block)


def pick_near_kernel(block, place_ref, m1, m2, m3, rows_ref, *outs):
    for d, (meta, out) in enumerate(zip((m1, m2, m3), outs), 1):
        p = lax.rem(place_ref[0] + d, LINE)
        out[...] = rows_ref[at_block(meta[0, near(p, d)], block), :]


def pick_far_kernel(block, place_ref, m1, m2, m3, same_ref, below_ref, *outs):
    for d, (meta, out) in enumerate(zip((m1, m2, m3), outs), 1):
        p = lax.rem(place_ref[0] + d, LINE)
        at = at_block(meta[0, far(p, d)], block)

        @pl.when(p >= d)
        def _():
            out[...] = same_ref[at, :]

        @pl.when(p < d)
        def _():
            out[...] = below_ref[at, :]


def slots(p):
    return [0, LINE] + [near(p, d) for d in range(1, LINE)] + [far(p, d) for d in range(1, LINE)]


def tiles_kernel(block, place_ref, lists_ref, counts_ref, x_ref, sw_ref, _, tiles_ref, tiles_t_ref, self_ref):
    for i, o in enumerate(slots(place_ref[0])):
        first, second = lists_ref[o, 0], lists_ref[o, 1]
        at = pl.ds(pl.multiple_of((o * 2 + second) * block, block), block)
        tile = (counts_ref[:, at] * (first + second)).astype(F32)
        tiles_ref[:, i * block : (i + 1) * block] = tile.astype(BF16)
        tiles_t_ref[i * block : (i + 1) * block, :] = tile.T.astype(BF16)
    self_ref[...] = dot(x_ref[...], sw_ref[...])


def message_kernel(block, first, last, *refs):
    size = last - first
    if first == 0:
        lists_ref, same_ref, below_ref = refs[:3]
        held = [same_ref[at_block(lists_ref[0, 1], block), :]]
        held += [below_ref[at_block(lists_ref[LINE, 1], block), :]]
        refs = refs[3:]
        held += [b[...] for b in refs[: size - 2]]
        refs = refs[size - 2 :]
    else:
        held = [b[...] for b in refs[:size]]
        refs = refs[size:]
    q_ref, qb_ref, tiles_ref = refs[:3]
    acc_in, deg_in = refs[3:5] if first else (None, None)
    msg_ref, acc_ref, deg_ref = refs[-3:]
    x = jnp.concatenate(held, axis=0)
    keep = x[:, :128].astype(F32) < LIMIT
    tiles = tiles_ref[:, first * block : last * block]
    deg = dot(tiles, jnp.where(keep, 1.0, 0.0).astype(BF16))
    deg_ref[...] = deg + deg_in[...] if first else deg
    keep = keep[:, :1]
    hidden = q_ref.shape[1]
    step = 512
    for n in range(hidden // step):
        cols = slice(n * step, (n + 1) * step)
        pre = dot(x, q_ref[:, cols]) + qb_ref[:, cols]
        msg = jnp.where(keep, jnp.maximum(pre, 0.0), 0.0).astype(BF16)
        msg_ref[:, cols] = msg
        acc = dot(tiles, msg)
        acc_ref[:, cols] = acc + acc_in[:, cols] if first else acc


def layer_kernel(
    block, live_ref, place_ref, lists_ref, got_a, got_b, got_c, q_ref, qb_ref, tiles_ref, acc_ref, deg_ref, self_ref, up_ref, nb_ref, ob_ref, tt_ref,
    msg_ref, g_ref, gpool_ref, pre_ref, last_ref, near1, near2, near3, far1, pooled_ref, gn_ref,
):
    rows, width = self_ref.shape
    hidden = nb_ref.shape[0]
    step = 512
    x = jnp.concatenate([got_a[...], got_b[...], got_c[...]], axis=0)
    keep = x[:, :128].astype(F32) < LIMIT
    tiles = tiles_ref[:, -3 * block :]
    deg = deg_ref[...] + dot(tiles, jnp.where(keep, 1.0, 0.0).astype(BF16))
    inv_deg = 1.0 / (1.0 + deg[:, :1])
    keep = keep[:, :1]
    for n in range(hidden // step):
        cols = slice(n * step, (n + 1) * step)
        pre = dot(x, q_ref[:, cols]) + qb_ref[:, cols]
        msg = jnp.where(keep, jnp.maximum(pre, 0.0), 0.0).astype(BF16)
        last_ref[:, cols] = msg
        pooled_ref[:, cols] = ((acc_ref[:, cols] + dot(tiles, msg)) * inv_deg).astype(BF16)
    pooled = pooled_ref[...]
    for n in range(width // step):
        cols = slice(n * step, (n + 1) * step)
        pre_ref[:, cols] = self_ref[:, cols] + dot(pooled, nb_ref[:, cols]) + ob_ref[:, cols]
    pre = pre_ref[...]
    act = jnp.maximum(pre, 0.0)
    inv = lax.rsqrt(jnp.mean(act * act, axis=1, keepdims=True) + EPS)
    keep = lax.broadcasted_iota(jnp.int32, (rows, 1), 0) < live_ref[0]
    up = jnp.where(keep, up_ref[...].astype(F32), 0.0)
    inner = jnp.sum(up * act, axis=1, keepdims=True) / width
    g = inv * up - act * (inv * inv * inv * inner)
    g = jnp.where(pre > 0, g, 0.0).astype(BF16)
    g_ref[...] = g
    for n in range(hidden // step):
        cols = slice(n * step, (n + 1) * step)
        gpool_ref[:, cols] = (dot(g, nb_ref[cols, :], 1, 1) * inv_deg).astype(BF16)

    def store(cols, part):
        for i, out in enumerate((near1, near2, near3, far1)):
            out[:, cols] = part[i * block : (i + 1) * block].astype(BF16)

    mark_block(place_ref, lists_ref, 1, far1, width)
    messages = [msg_ref[2 * block :, :], last_ref[:block, :]]
    back_dot(2 * block, tt_ref, gpool_ref, messages, q_ref, gn_ref, store)


def mark_block(place_ref, lists_ref, d, out, width):
    which = lists_ref[far(place_ref[0], d), 1].astype(F32)
    out[:, width:] = jnp.full((out.shape[0], out.shape[1] - width), which, F32).astype(BF16)


def back_dot(first, tt_ref, gpool_ref, messages, q_ref, gn_ref, store):
    rows = gn_ref.shape[0]
    tt = tt_ref[first : first + rows, :]
    step = 512
    for n in range(gpool_ref.shape[1] // step):
        cols = slice(n * step, (n + 1) * step)
        live = jnp.concatenate([m[:, cols] for m in messages], axis=0).astype(F32) > 0
        gn_ref[:, cols] = jnp.where(live, dot(tt, gpool_ref[:, cols]), 0.0).astype(BF16)
    gn = gn_ref[...]
    for n in range(q_ref.shape[0] // step):
        cols = slice(n * step, (n + 1) * step)
        store(cols, dot(gn, q_ref[cols, :], 1, 1))


def back_far_kernel(block, place_ref, lists_ref, tt_ref, gpool_ref, msg_ref, q_ref, _, *refs):
    outs, gn_ref = refs[:-1], refs[-1]
    width = q_ref.shape[0]

    def store(cols, part):
        for i, out in enumerate(outs):
            out[:, cols] = part[i * block : (i + 1) * block].astype(BF16)

    for d, out in enumerate(outs, 2):
        mark_block(place_ref, lists_ref, d, out, width)
    back_dot((2 + LINE) * block, tt_ref, gpool_ref, [msg_ref[block:, :]], q_ref, gn_ref, store)


def back_own_kernel(block, lists_ref, tt_ref, gpool_ref, msg_ref, q_ref, _, same_ref, below_ref, gn_ref):
    same_ref[...] = jnp.zeros_like(same_ref)
    at = at_block(lists_ref[0, 1], block)

    def store(cols, part):
        same_ref[at, cols] = part[:block].astype(BF16)
        below_ref[:, cols] = part[block:].astype(BF16)

    back_dot(0, tt_ref, gpool_ref, [msg_ref[: 2 * block, :]], q_ref, gn_ref, store)


def own_rows_kernel(live_ref, g_ref, sw_ref, pre_ref, _, gself_ref, emb_ref):
    rows, width = pre_ref.shape
    step = 512
    for n in range(width // step):
        cols = slice(n * step, (n + 1) * step)
        gself_ref[:, cols] = dot(g_ref[...], sw_ref[cols, :], 1, 1)
    act = jnp.maximum(pre_ref[...], 0.0)
    inv = lax.rsqrt(jnp.mean(act * act, axis=1, keepdims=True) + EPS)
    keep = lax.broadcasted_iota(jnp.int32, (rows, 1), 0) < live_ref[0]
    emb_ref[...] = jnp.where(keep, act * inv, 0.0).astype(BF16)


def sum_near_kernel(block, place_ref, lists_ref, m1, m2, m3, own_ref, d1, d2, d3, out_ref, total):
    total[...] = jnp.zeros_like(total)
    total[at_block(lists_ref[LINE, 1], block), :] = own_ref[...].astype(F32)
    for d, (meta, part) in enumerate(zip((m1, m2, m3), (d1, d2, d3)), 1):
        p = lax.rem(place_ref[0] + d, LINE)
        total[at_block(meta[0, near(p, d)], block), :] += part[...].astype(F32)
    out_ref[...] = total[...].astype(BF16)


def join_kernel(place_ref, mine_ref, sent_ref, out_ref):
    @pl.when(place_ref[0] == 0)
    def _():
        out_ref[...] = sent_ref[...]

    @pl.when(place_ref[0] > 0)
    def _():
        out_ref[...] = mine_ref[...]


def place_kernel(gself_ref, c1, c2, c3, total_ref):
    block, width = c1.shape[0], gself_ref.shape[1]
    first, second = gself_ref[:block, :], gself_ref[block:, :]
    for part in (c1, c2, c3):
        grad = part[:, :width].astype(F32)
        late = part[:, width : width + 1].astype(F32) > 0.5
        first += jnp.where(late, 0.0, grad)
        second += jnp.where(late, grad, 0.0)
    total_ref[:block, :] = first
    total_ref[block:, :] = second


def finish_kernel(live_ref, total_ref, same_ref, below_ref, out_ref):
    total = total_ref[...] + same_ref[...].astype(F32) + below_ref[...].astype(F32)
    keep = lax.broadcasted_iota(jnp.int32, (total.shape[0], 1), 0) < live_ref[0]
    out_ref[...] = jnp.where(keep, total, 0.0).astype(BF16)


def local(x, live, listed, counts, cotangent, q, qb, sw, nb, ob):
    x, lists, counts, up = x[0], listed[0, 0], counts[0], cotangent[0]
    live = live.reshape(1)
    rows, width = x.shape
    hidden = q.shape[1]
    reach, block_count = lists.shape
    block = rows // block_count
    qb, ob = qb[None], ob[None]
    place = (lax.axis_index("dom") % LINE).astype(jnp.int32).reshape(1)
    keep = lax.broadcasted_iota(jnp.int32, (rows, 1), 0) < live[0]
    marked = jnp.where(keep, x, jnp.asarray(DEAD, BF16))
    row = jnp.pad(lists[:, 1], (0, 128 - reach))[None]
    steps = range(1, LINE)
    one, two = ((block, width), BF16), ((rows, width), BF16)

    below = swap_rows(marked, LINE)
    same = swap_rows(marked, 0)
    metas = [along(row, -d) for d in steps]
    later, *metas = lax.optimization_barrier((marked, *metas))
    below2 = swap_rows(later, 2 * LINE)
    scalars = [SMEM] * (1 + len(steps))
    sent = call(
        lambda *r: pick_near_kernel(block, *r),
        [one] * len(steps),
        (place, *metas, below),
        scalars + [VMEM],
    )
    got_near = [along(b, d) for d, b in zip(steps, sent)]
    sent = call(
        lambda *r: pick_far_kernel(block, *r),
        [one] * len(steps),
        (place, *metas, same, below2),
        scalars + [VMEM] * 2,
    )
    got_far = [along(b, d) for d, b in zip(steps, sent)]
    tiles, tiles_t, self_pre = call(
        lambda *r: tiles_kernel(block, *r),
        [((rows, reach * block), BF16), ((reach * block, rows), BF16), ((rows, width), F32)],
        (place, lists, counts, x, sw, sent[0]),
        [SMEM] * 2 + [VMEM] * 3 + [HELD],
        flops=2 * rows * width * width,
    )
    split = 1 + LINE

    def message(first, last, ins, specs):
        size = last - first
        return call(
            lambda *r: message_kernel(block, first, last, *r),
            [((size * block, hidden), BF16), ((rows, hidden), F32), ((rows, 128), F32)],
            ins,
            specs,
            flops=2 * size * block * hidden * (width + rows),
        )

    msg_a, acc, deg = message(
        0, split, (lists, same, below, *got_near, q, qb, tiles), [SMEM] + [VMEM] * 8
    )
    g, gpool, pre, msg_b, *near_back, far_first = call(
        lambda *r: layer_kernel(block, *r),
        [two, ((rows, hidden), BF16), ((rows, width), F32), ((3 * block, hidden), BF16)] + [one] * 3 + [((block, width + 128), BF16)],
        (live, place, lists, *got_far, q, qb, tiles, acc, deg, self_pre, up, nb, ob, tiles_t, msg_a),
        [SMEM] * 3 + [VMEM] * 14,
        scratch=[pltpu.VMEM((rows, hidden), BF16), pltpu.VMEM((4 * block, hidden), BF16)],
        flops=8 * MICROSECOND,
    )
    back_near = [along(b, -d) for d, b in zip(steps, near_back)]
    far_back = call(
        lambda *r: back_far_kernel(block, *r),
        [((block, width + 128), BF16)] * 2,
        (place, lists, tiles_t, gpool, msg_b, q, near_back[0]),
        [SMEM] * 2 + [VMEM] * 4 + [HELD],
        scratch=[pltpu.VMEM((2 * block, hidden), BF16)],
        flops=2 * MICROSECOND,
    )
    (joined,) = call(
        join_kernel,
        [((block, width + 128), BF16)],
        (place, far_first, two_back(far_first)),
        [SMEM] + [VMEM] * 2,
    )
    back_far = [turn(joined)]
    back_far += [straight_back(b, d) for d, b in zip(steps[1:], far_back)]
    own_same, own_below = call(
        lambda *r: back_own_kernel(block, *r),
        [two, one],
        (lists, tiles_t, gpool, msg_a, q, far_back[0]),
        [SMEM] + [VMEM] * 4 + [HELD],
        scratch=[pltpu.VMEM((2 * block, hidden), BF16)],
        flops=2 * MICROSECOND,
    )
    g_same = swap_rows(own_same, 0)
    total = pltpu.VMEM((rows, width), F32)
    (sum_below,) = call(
        lambda *r: sum_near_kernel(block, *r),
        [two],
        (place, lists, *metas, own_below, *back_near),
        [SMEM] * 5 + [VMEM] * 4,
        scratch=[total],
        flops=20 * MICROSECOND,
    )
    g_below = swap_rows(sum_below, -LINE)
    gself, emb = call(
        own_rows_kernel,
        [((rows, width), F32), two],
        (live, g, sw, pre, sum_below),
        [SMEM] + [VMEM] * 3 + [HELD],
        flops=2 * MICROSECOND,
    )
    (placed,) = call(
        place_kernel,
        [((rows, width), F32)],
        (gself, *back_far),
        [VMEM] * 4,
        flops=20 * MICROSECOND,
    )
    (grad,) = call(finish_kernel, [two], (live, placed, g_same, g_below), [SMEM] + [VMEM] * 3)
    return emb[None], grad[None]


def solution(mesh):
    data = P("side", "dom", None)
    return jax.shard_map(
        local,
        mesh=mesh,
        in_specs=(
            data,
            P("side", "dom"),
            P("side", "dom", None, None),
            data,
            data,
            P(),
            P(),
            P(),
            P(),
            P(),
        ),
        out_specs=(data, data),
        check_vma=False,
    )
```

```python
import jax
import jax.numpy as jnp
from jax import lax
from jax.experimental import pallas as pl
from jax.experimental.pallas import tpu as pltpu
from jax.sharding import PartitionSpec as P

EPS = 1e-06
DEAD = 16384.0
LIMIT = 8192.0
MICROSECOND = 10**9
LINE = 4
F32 = jnp.float32
BF16 = jnp.bfloat16
VMEM = pl.BlockSpec(memory_space=pltpu.VMEM)
HELD = pl.BlockSpec(memory_space=pl.ANY)
SMEM = pl.BlockSpec(memory_space=pltpu.SMEM)


def dot(a, b, ca=1, cb=0):
    return lax.dot_general(a, b, (((ca,), (cb,)), ((), ())), preferred_element_type=F32)


def call(kernel, outs, ins, in_specs=None, scratch=(), limit=24, flops=0):
    return pl.pallas_call(
        kernel,
        out_shape=[jax.ShapeDtypeStruct(s, d) for s, d in outs],
        in_specs=in_specs or [VMEM] * len(ins),
        out_specs=[VMEM] * len(outs),
        scratch_shapes=list(scratch),
        compiler_params=pltpu.CompilerParams(vmem_limit_bytes=limit << 20),
        cost_estimate=pl.CostEstimate(flops=flops, bytes_accessed=1 << 20, transcendentals=0),
    )(*ins)


def swap_rows(x, shift):
    count = lax.axis_size("dom")
    pairs = [
        (s * count + j, (1 - s) * count + (j + shift) % count)
        for s in range(2)
        for j in range(count)
    ]
    return lax.ppermute(x, ("side", "dom"), pairs)


def along(x, d):
    count = lax.axis_size("dom")
    pairs = [(j, j // LINE * LINE + (j + d) % LINE) for j in range(count)]
    return lax.ppermute(x, "dom", pairs)


def straight_back(x, d):
    count = lax.axis_size("dom")
    pairs = []
    for s in range(2):
        for j in range(count):
            to = j + d if j % LINE + d < LINE else j + d + LINE
            pairs.append(((1 - s) * count + to % count, s * count + j))
    return lax.ppermute(x, ("side", "dom"), pairs)


def two_back(x):
    count = lax.axis_size("dom")
    pairs = [
        (s * count + j, (1 - s) * count + (j - 2 * LINE) % count)
        for s in range(2)
        for j in range(0, count, LINE)
    ]
    return lax.ppermute(x, ("side", "dom"), pairs)


def turn(x):
    count = lax.axis_size("dom")
    pairs = []
    for s in range(2):
        for j in range(count):
            to = (1 - s) * count + j - 1 if j % LINE else s * count + j + LINE - 1
            pairs.append((s * count + j, to))
    return lax.ppermute(x, ("side", "dom"), pairs)


def near(p, d):
    return jnp.where(p >= d, d + LINE, d)


def far(p, d):
    return jnp.where(p >= d, d, d + LINE)


def at_block(index, block):
    return pl.ds(pl.multiple_of(index * block, block), block)


def pick_near_kernel(block, place_ref, m1, m2, m3, rows_ref, _, *outs):
    for d, (meta, out) in enumerate(zip((m1, m2, m3), outs), 1):
        p = lax.rem(place_ref[0] + d, LINE)
        out[...] = rows_ref[at_block(meta[0, near(p, d)], block), :]


def pick_far_kernel(block, place_ref, m1, m2, m3, same_ref, below_ref, *outs):
    for d, (meta, out) in enumerate(zip((m1, m2, m3), outs), 1):
        p = lax.rem(place_ref[0] + d, LINE)
        at = at_block(meta[0, far(p, d)], block)

        @pl.when(p >= d)
        def _():
            out[...] = same_ref[at, :]

        @pl.when(p < d)
        def _():
            out[...] = below_ref[at, :]


def slots(p):
    return [0, LINE] + [near(p, d) for d in range(1, LINE)] + [far(p, d) for d in range(1, LINE)]


def tiles_kernel(block, place_ref, lists_ref, counts_ref, x_ref, sw_ref, tiles_ref, tiles_t_ref, self_ref):
    for i, o in enumerate(slots(place_ref[0])):
        first, second = lists_ref[o, 0], lists_ref[o, 1]
        at = pl.ds(pl.multiple_of((o * 2 + second) * block, block), block)
        tile = (counts_ref[:, at] * (first + second)).astype(F32)
        tiles_ref[:, i * block : (i + 1) * block] = tile.astype(BF16)
        tiles_t_ref[i * block : (i + 1) * block, :] = tile.T.astype(BF16)
    self_ref[...] = dot(x_ref[...], sw_ref[...])


def message_kernel(block, first, last, *refs):
    size = last - first
    if first == 0:
        lists_ref, same_ref, below_ref = refs[:3]
        held = [same_ref[at_block(lists_ref[0, 1], block), :]]
        held += [below_ref[at_block(lists_ref[LINE, 1], block), :]]
        refs = refs[3:]
        held += [b[...] for b in refs[: size - 2]]
        refs = refs[size - 2 :]
    else:
        held = [b[...] for b in refs[:size]]
        refs = refs[size:]
    q_ref, qb_ref, tiles_ref = refs[:3]
    acc_in, deg_in = refs[3:5] if first else (None, None)
    msg_ref, acc_ref, deg_ref = refs[-3:]
    x = jnp.concatenate(held, axis=0)
    keep = x[:, :128].astype(F32) < LIMIT
    tiles = tiles_ref[:, first * block : last * block]
    deg = dot(tiles, jnp.where(keep, 1.0, 0.0).astype(BF16))
    deg_ref[...] = deg + deg_in[...] if first else deg
    keep = keep[:, :1]
    hidden = q_ref.shape[1]
    step = 512
    for n in range(hidden // step):
        cols = slice(n * step, (n + 1) * step)
        pre = dot(x, q_ref[:, cols]) + qb_ref[:, cols]
        msg = jnp.where(keep, jnp.maximum(pre, 0.0), 0.0).astype(BF16)
        msg_ref[:, cols] = msg
        acc = dot(tiles, msg)
        acc_ref[:, cols] = acc + acc_in[:, cols] if first else acc


def layer_kernel(
    block, live_ref, place_ref, lists_ref, got_a, got_b, got_c, q_ref, qb_ref, tiles_ref, acc_ref, deg_ref, self_ref, up_ref, nb_ref, ob_ref, tt_ref,
    msg_ref, g_ref, gpool_ref, pre_ref, last_ref, near1, near2, near3, far1, pooled_ref, gn_ref,
):
    rows, width = self_ref.shape
    hidden = nb_ref.shape[0]
    step = 512
    x = jnp.concatenate([got_a[...], got_b[...], got_c[...]], axis=0)
    keep = x[:, :128].astype(F32) < LIMIT
    tiles = tiles_ref[:, -3 * block :]
    deg = deg_ref[...] + dot(tiles, jnp.where(keep, 1.0, 0.0).astype(BF16))
    inv_deg = 1.0 / (1.0 + deg[:, :1])
    keep = keep[:, :1]
    for n in range(hidden // step):
        cols = slice(n * step, (n + 1) * step)
        pre = dot(x, q_ref[:, cols]) + qb_ref[:, cols]
        msg = jnp.where(keep, jnp.maximum(pre, 0.0), 0.0).astype(BF16)
        last_ref[:, cols] = msg
        pooled_ref[:, cols] = ((acc_ref[:, cols] + dot(tiles, msg)) * inv_deg).astype(BF16)
    pooled = pooled_ref[...]
    for n in range(width // step):
        cols = slice(n * step, (n + 1) * step)
        pre_ref[:, cols] = self_ref[:, cols] + dot(pooled, nb_ref[:, cols]) + ob_ref[:, cols]
    pre = pre_ref[...]
    act = jnp.maximum(pre, 0.0)
    inv = lax.rsqrt(jnp.mean(act * act, axis=1, keepdims=True) + EPS)
    keep = lax.broadcasted_iota(jnp.int32, (rows, 1), 0) < live_ref[0]
    up = jnp.where(keep, up_ref[...].astype(F32), 0.0)
    inner = jnp.sum(up * act, axis=1, keepdims=True) / width
    g = inv * up - act * (inv * inv * inv * inner)
    g = jnp.where(pre > 0, g, 0.0).astype(BF16)
    g_ref[...] = g
    for n in range(hidden // step):
        cols = slice(n * step, (n + 1) * step)
        gpool_ref[:, cols] = (dot(g, nb_ref[cols, :], 1, 1) * inv_deg).astype(BF16)

    def store(cols, part):
        for i, out in enumerate((near1, near2, near3, far1)):
            out[:, cols] = part[i * block : (i + 1) * block].astype(BF16)

    mark_block(place_ref, lists_ref, 1, far1, width)
    messages = [msg_ref[2 * block :, :], last_ref[:block, :]]
    back_dot(2 * block, tt_ref, gpool_ref, messages, q_ref, gn_ref, store)


def mark_block(place_ref, lists_ref, d, out, width):
    which = lists_ref[far(place_ref[0], d), 1].astype(F32)
    out[:, width:] = jnp.full((out.shape[0], out.shape[1] - width), which, F32).astype(BF16)


def back_dot(first, tt_ref, gpool_ref, messages, q_ref, gn_ref, store):
    rows = gn_ref.shape[0]
    tt = tt_ref[first : first + rows, :]
    step = 512
    for n in range(gpool_ref.shape[1] // step):
        cols = slice(n * step, (n + 1) * step)
        live = jnp.concatenate([m[:, cols] for m in messages], axis=0).astype(F32) > 0
        gn_ref[:, cols] = jnp.where(live, dot(tt, gpool_ref[:, cols]), 0.0).astype(BF16)
    gn = gn_ref[...]
    for n in range(q_ref.shape[0] // step):
        cols = slice(n * step, (n + 1) * step)
        store(cols, dot(gn, q_ref[cols, :], 1, 1))


def back_far_kernel(block, place_ref, lists_ref, tt_ref, gpool_ref, msg_ref, q_ref, _, *refs):
    outs, gn_ref = refs[:-1], refs[-1]
    width = q_ref.shape[0]

    def store(cols, part):
        for i, out in enumerate(outs):
            out[:, cols] = part[i * block : (i + 1) * block].astype(BF16)

    for d, out in enumerate(outs, 2):
        mark_block(place_ref, lists_ref, d, out, width)
    back_dot((2 + LINE) * block, tt_ref, gpool_ref, [msg_ref[block:, :]], q_ref, gn_ref, store)


def back_own_kernel(block, lists_ref, tt_ref, gpool_ref, msg_ref, q_ref, _, same_ref, below_ref, gn_ref):
    same_ref[...] = jnp.zeros_like(same_ref)
    at = at_block(lists_ref[0, 1], block)

    def store(cols, part):
        same_ref[at, cols] = part[:block].astype(BF16)
        below_ref[:, cols] = part[block:].astype(BF16)

    back_dot(0, tt_ref, gpool_ref, [msg_ref[: 2 * block, :]], q_ref, gn_ref, store)


def own_rows_kernel(live_ref, g_ref, sw_ref, pre_ref, _, gself_ref, emb_ref):
    rows, width = pre_ref.shape
    step = 512
    for n in range(width // step):
        cols = slice(n * step, (n + 1) * step)
        gself_ref[:, cols] = dot(g_ref[...], sw_ref[cols, :], 1, 1)
    act = jnp.maximum(pre_ref[...], 0.0)
    inv = lax.rsqrt(jnp.mean(act * act, axis=1, keepdims=True) + EPS)
    keep = lax.broadcasted_iota(jnp.int32, (rows, 1), 0) < live_ref[0]
    emb_ref[...] = jnp.where(keep, act * inv, 0.0).astype(BF16)


def sum_near_kernel(block, place_ref, lists_ref, m1, m2, m3, own_ref, d1, d2, d3, out_ref, total):
    total[...] = jnp.zeros_like(total)
    total[at_block(lists_ref[LINE, 1], block), :] = own_ref[...].astype(F32)
    for d, (meta, part) in enumerate(zip((m1, m2, m3), (d1, d2, d3)), 1):
        p = lax.rem(place_ref[0] + d, LINE)
        total[at_block(meta[0, near(p, d)], block), :] += part[...].astype(F32)
    out_ref[...] = total[...].astype(BF16)


def join_kernel(place_ref, mine_ref, sent_ref, out_ref):
    @pl.when(place_ref[0] == 0)
    def _():
        out_ref[...] = sent_ref[...]

    @pl.when(place_ref[0] > 0)
    def _():
        out_ref[...] = mine_ref[...]


def place_kernel(gself_ref, c1, c2, c3, total_ref):
    block, width = c1.shape[0], gself_ref.shape[1]
    first, second = gself_ref[:block, :], gself_ref[block:, :]
    for part in (c1, c2, c3):
        grad = part[:, :width].astype(F32)
        late = part[:, width : width + 1].astype(F32) > 0.5
        first += jnp.where(late, 0.0, grad)
        second += jnp.where(late, grad, 0.0)
    total_ref[:block, :] = first
    total_ref[block:, :] = second


def finish_kernel(live_ref, total_ref, same_ref, below_ref, out_ref):
    total = total_ref[...] + same_ref[...].astype(F32) + below_ref[...].astype(F32)
    keep = lax.broadcasted_iota(jnp.int32, (total.shape[0], 1), 0) < live_ref[0]
    out_ref[...] = jnp.where(keep, total, 0.0).astype(BF16)


def local(x, live, listed, counts, cotangent, q, qb, sw, nb, ob):
    x, lists, counts, up = x[0], listed[0, 0], counts[0], cotangent[0]
    live = live.reshape(1)
    rows, width = x.shape
    hidden = q.shape[1]
    reach, block_count = lists.shape
    block = rows // block_count
    qb, ob = qb[None], ob[None]
    place = (lax.axis_index("dom") % LINE).astype(jnp.int32).reshape(1)
    keep = lax.broadcasted_iota(jnp.int32, (rows, 1), 0) < live[0]
    marked = jnp.where(keep, x, jnp.asarray(DEAD, BF16))
    row = jnp.pad(lists[:, 1], (0, 128 - reach))[None]
    steps = range(1, LINE)
    one, two = ((block, width), BF16), ((rows, width), BF16)

    below = swap_rows(marked, LINE)
    same = swap_rows(marked, 0)
    metas = [along(row, -d) for d in steps]
    later, *metas = lax.optimization_barrier((marked, *metas))
    below2 = swap_rows(later, 2 * LINE)
    scalars = [SMEM] * (1 + len(steps))
    tiles, tiles_t, self_pre = call(
        lambda *r: tiles_kernel(block, *r),
        [((rows, reach * block), BF16), ((reach * block, rows), BF16), ((rows, width), F32)],
        (place, lists, counts, x, sw),
        [SMEM] * 2 + [VMEM] * 3,
        flops=2 * rows * width * width,
    )
    sent = call(
        lambda *r: pick_near_kernel(block, *r),
        [one] * len(steps),
        (place, *metas, below, tiles),
        scalars + [VMEM, HELD],
    )
    got_near = [along(b, d) for d, b in zip(steps, sent)]
    sent = call(
        lambda *r: pick_far_kernel(block, *r),
        [one] * len(steps),
        (place, *metas, same, below2),
        scalars + [VMEM] * 2,
    )
    got_far = [along(b, d) for d, b in zip(steps, sent)]
    split = 1 + LINE

    def message(first, last, ins, specs):
        size = last - first
        return call(
            lambda *r: message_kernel(block, first, last, *r),
            [((size * block, hidden), BF16), ((rows, hidden), F32), ((rows, 128), F32)],
            ins,
            specs,
            flops=2 * size * block * hidden * (width + rows),
        )

    msg_a, acc, deg = message(
        0, split, (lists, same, below, *got_near, q, qb, tiles), [SMEM] + [VMEM] * 8
    )
    g, gpool, pre, msg_b, *near_back, far_first = call(
        lambda *r: layer_kernel(block, *r),
        [two, ((rows, hidden), BF16), ((rows, width), F32), ((3 * block, hidden), BF16)] + [one] * 3 + [((block, width + 128), BF16)],
        (live, place, lists, *got_far, q, qb, tiles, acc, deg, self_pre, up, nb, ob, tiles_t, msg_a),
        [SMEM] * 3 + [VMEM] * 14,
        scratch=[pltpu.VMEM((rows, hidden), BF16), pltpu.VMEM((4 * block, hidden), BF16)],
        flops=8 * MICROSECOND,
    )
    back_near = [along(b, -d) for d, b in zip(steps, near_back)]
    far_back = call(
        lambda *r: back_far_kernel(block, *r),
        [((block, width + 128), BF16)] * 2,
        (place, lists, tiles_t, gpool, msg_b, q, near_back[0]),
        [SMEM] * 2 + [VMEM] * 4 + [HELD],
        scratch=[pltpu.VMEM((2 * block, hidden), BF16)],
        flops=2 * MICROSECOND,
    )
    (joined,) = call(
        join_kernel,
        [((block, width + 128), BF16)],
        (place, far_first, two_back(far_first)),
        [SMEM] + [VMEM] * 2,
    )
    back_far = [turn(joined)]
    back_far += [straight_back(b, d) for d, b in zip(steps[1:], far_back)]
    own_same, own_below = call(
        lambda *r: back_own_kernel(block, *r),
        [two, one],
        (lists, tiles_t, gpool, msg_a, q, far_back[0]),
        [SMEM] + [VMEM] * 4 + [HELD],
        scratch=[pltpu.VMEM((2 * block, hidden), BF16)],
        flops=2 * MICROSECOND,
    )
    g_same = swap_rows(own_same, 0)
    total = pltpu.VMEM((rows, width), F32)
    (sum_below,) = call(
        lambda *r: sum_near_kernel(block, *r),
        [two],
        (place, lists, *metas, own_below, *back_near),
        [SMEM] * 5 + [VMEM] * 4,
        scratch=[total],
        flops=20 * MICROSECOND,
    )
    g_below = swap_rows(sum_below, -LINE)
    gself, emb = call(
        own_rows_kernel,
        [((rows, width), F32), two],
        (live, g, sw, pre, sum_below),
        [SMEM] + [VMEM] * 3 + [HELD],
        flops=2 * MICROSECOND,
    )
    (placed,) = call(
        place_kernel,
        [((rows, width), F32)],
        (gself, *back_far),
        [VMEM] * 4,
        flops=20 * MICROSECOND,
    )
    (grad,) = call(finish_kernel, [two], (live, placed, g_same, g_below), [SMEM] + [VMEM] * 3)
    return emb[None], grad[None]


def solution(mesh):
    data = P("side", "dom", None)
    return jax.shard_map(
        local,
        mesh=mesh,
        in_specs=(
            data,
            P("side", "dom"),
            P("side", "dom", None, None),
            data,
            data,
            P(),
            P(),
            P(),
            P(),
            P(),
        ),
        out_specs=(data, data),
        check_vma=False,
    )
```

```python
import jax
import jax.numpy as jnp
from jax import lax
from jax.experimental import pallas as pl
from jax.experimental.pallas import tpu as pltpu
from jax.sharding import PartitionSpec as P

EPS = 1e-06
DEAD = 16384.0
LIMIT = 8192.0
MICROSECOND = 10**9
LINE = 4
F32 = jnp.float32
BF16 = jnp.bfloat16
VMEM = pl.BlockSpec(memory_space=pltpu.VMEM)
HELD = pl.BlockSpec(memory_space=pl.ANY)
SMEM = pl.BlockSpec(memory_space=pltpu.SMEM)


def dot(a, b, ca=1, cb=0):
    return lax.dot_general(a, b, (((ca,), (cb,)), ((), ())), preferred_element_type=F32)


def call(kernel, outs, ins, in_specs=None, scratch=(), limit=24, flops=0):
    return pl.pallas_call(
        kernel,
        out_shape=[jax.ShapeDtypeStruct(s, d) for s, d in outs],
        in_specs=in_specs or [VMEM] * len(ins),
        out_specs=[VMEM] * len(outs),
        scratch_shapes=list(scratch),
        compiler_params=pltpu.CompilerParams(vmem_limit_bytes=limit << 20),
        cost_estimate=pl.CostEstimate(flops=flops, bytes_accessed=1 << 20, transcendentals=0),
    )(*ins)


def swap_rows(x, shift):
    count = lax.axis_size("dom")
    pairs = [
        (s * count + j, (1 - s) * count + (j + shift) % count)
        for s in range(2)
        for j in range(count)
    ]
    return lax.ppermute(x, ("side", "dom"), pairs)


def along(x, d):
    count = lax.axis_size("dom")
    pairs = [(j, j // LINE * LINE + (j + d) % LINE) for j in range(count)]
    return lax.ppermute(x, "dom", pairs)


def straight_back(x, d):
    count = lax.axis_size("dom")
    pairs = []
    for s in range(2):
        for j in range(count):
            to = j + d if j % LINE + d < LINE else j + d + LINE
            pairs.append(((1 - s) * count + to % count, s * count + j))
    return lax.ppermute(x, ("side", "dom"), pairs)


def two_back(x):
    count = lax.axis_size("dom")
    pairs = [
        (s * count + j, (1 - s) * count + (j - 2 * LINE) % count)
        for s in range(2)
        for j in range(0, count, LINE)
    ]
    return lax.ppermute(x, ("side", "dom"), pairs)


def turn(x):
    count = lax.axis_size("dom")
    pairs = []
    for s in range(2):
        for j in range(count):
            to = (1 - s) * count + j - 1 if j % LINE else s * count + j + LINE - 1
            pairs.append((s * count + j, to))
    return lax.ppermute(x, ("side", "dom"), pairs)


def near(p, d):
    return jnp.where(p >= d, d + LINE, d)


def far(p, d):
    return jnp.where(p >= d, d, d + LINE)


def at_block(index, block):
    return pl.ds(pl.multiple_of(index * block, block), block)


def pick_near_kernel(block, place_ref, m1, m2, m3, rows_ref, _, *outs):
    for d, (meta, out) in enumerate(zip((m1, m2, m3), outs), 1):
        p = lax.rem(place_ref[0] + d, LINE)
        out[...] = rows_ref[at_block(meta[0, near(p, d)], block), :]


def pick_far_kernel(block, place_ref, m1, m2, m3, same_ref, below_ref, *outs):
    for d, (meta, out) in enumerate(zip((m1, m2, m3), outs), 1):
        p = lax.rem(place_ref[0] + d, LINE)
        at = at_block(meta[0, far(p, d)], block)

        @pl.when(p >= d)
        def _():
            out[...] = same_ref[at, :]

        @pl.when(p < d)
        def _():
            out[...] = below_ref[at, :]


def slots(p):
    return [0, LINE] + [near(p, d) for d in range(1, LINE)] + [far(p, d) for d in range(1, LINE)]


def tiles_kernel(block, place_ref, lists_ref, counts_ref, x_ref, sw_ref, tiles_ref, tiles_t_ref, self_ref):
    for i, o in enumerate(slots(place_ref[0])):
        first, second = lists_ref[o, 0], lists_ref[o, 1]
        at = pl.ds(pl.multiple_of((o * 2 + second) * block, block), block)
        tile = (counts_ref[:, at] * (first + second)).astype(F32)
        tiles_ref[:, i * block : (i + 1) * block] = tile.astype(BF16)
        tiles_t_ref[i * block : (i + 1) * block, :] = tile.T.astype(BF16)
    self_ref[...] = dot(x_ref[...], sw_ref[...])


def message_kernel(block, first, last, *refs):
    size = last - first
    if first == 0:
        lists_ref, same_ref, below_ref = refs[:3]
        held = [same_ref[at_block(lists_ref[0, 1], block), :]]
        held += [below_ref[at_block(lists_ref[LINE, 1], block), :]]
        refs = refs[3:]
        held += [b[...] for b in refs[: size - 2]]
        refs = refs[size - 2 :]
    else:
        held = [b[...] for b in refs[:size]]
        refs = refs[size:]
    q_ref, qb_ref, tiles_ref = refs[:3]
    acc_in, deg_in = refs[3:5] if first else (None, None)
    msg_ref, acc_ref, deg_ref = refs[-3:]
    x = jnp.concatenate(held, axis=0)
    keep = x[:, :128].astype(F32) < LIMIT
    tiles = tiles_ref[:, first * block : last * block]
    deg = dot(tiles, jnp.where(keep, 1.0, 0.0).astype(BF16))
    deg_ref[...] = deg + deg_in[...] if first else deg
    keep = keep[:, :1]
    hidden = q_ref.shape[1]
    step = 1024
    for n in range(hidden // step):
        cols = slice(n * step, (n + 1) * step)
        pre = dot(x, q_ref[:, cols]) + qb_ref[:, cols]
        msg = jnp.where(keep, jnp.maximum(pre, 0.0), 0.0).astype(BF16)
        msg_ref[:, cols] = msg
        acc = dot(tiles, msg)
        acc_ref[:, cols] = acc + acc_in[:, cols] if first else acc


def layer_kernel(
    block, live_ref, place_ref, lists_ref, got_a, got_b, got_c, q_ref, qb_ref, tiles_ref, acc_ref, deg_ref, self_ref, up_ref, nb_ref, ob_ref, tt_ref,
    msg_ref, g_ref, gpool_ref, pre_ref, last_ref, near1, near2, near3, far1, pooled_ref, gn_ref,
):
    rows, width = self_ref.shape
    hidden = nb_ref.shape[0]
    step = 1024
    x = jnp.concatenate([got_a[...], got_b[...], got_c[...]], axis=0)
    keep = x[:, :128].astype(F32) < LIMIT
    tiles = tiles_ref[:, -3 * block :]
    deg = deg_ref[...] + dot(tiles, jnp.where(keep, 1.0, 0.0).astype(BF16))
    inv_deg = 1.0 / (1.0 + deg[:, :1])
    keep = keep[:, :1]
    for n in range(hidden // step):
        cols = slice(n * step, (n + 1) * step)
        pre = dot(x, q_ref[:, cols]) + qb_ref[:, cols]
        msg = jnp.where(keep, jnp.maximum(pre, 0.0), 0.0).astype(BF16)
        last_ref[:, cols] = msg
        pooled_ref[:, cols] = ((acc_ref[:, cols] + dot(tiles, msg)) * inv_deg).astype(BF16)
    pooled = pooled_ref[...]
    for n in range(width // step):
        cols = slice(n * step, (n + 1) * step)
        pre_ref[:, cols] = self_ref[:, cols] + dot(pooled, nb_ref[:, cols]) + ob_ref[:, cols]
    pre = pre_ref[...]
    act = jnp.maximum(pre, 0.0)
    inv = lax.rsqrt(jnp.mean(act * act, axis=1, keepdims=True) + EPS)
    keep = lax.broadcasted_iota(jnp.int32, (rows, 1), 0) < live_ref[0]
    up = jnp.where(keep, up_ref[...].astype(F32), 0.0)
    inner = jnp.sum(up * act, axis=1, keepdims=True) / width
    g = inv * up - act * (inv * inv * inv * inner)
    g = jnp.where(pre > 0, g, 0.0).astype(BF16)
    g_ref[...] = g
    for n in range(hidden // step):
        cols = slice(n * step, (n + 1) * step)
        gpool_ref[:, cols] = (dot(g, nb_ref[cols, :], 1, 1) * inv_deg).astype(BF16)

    def store(cols, part):
        for i, out in enumerate((near1, near2, near3, far1)):
            out[:, cols] = part[i * block : (i + 1) * block].astype(BF16)

    mark_block(place_ref, lists_ref, 1, far1, width)
    messages = [msg_ref[2 * block :, :], last_ref[:block, :]]
    back_dot(2 * block, tt_ref, gpool_ref, messages, q_ref, gn_ref, store)


def mark_block(place_ref, lists_ref, d, out, width):
    which = lists_ref[far(place_ref[0], d), 1].astype(F32)
    out[:, width:] = jnp.full((out.shape[0], out.shape[1] - width), which, F32).astype(BF16)


def back_dot(first, tt_ref, gpool_ref, messages, q_ref, gn_ref, store):
    rows = gn_ref.shape[0]
    tt = tt_ref[first : first + rows, :]
    step = 1024
    for n in range(gpool_ref.shape[1] // step):
        cols = slice(n * step, (n + 1) * step)
        live = jnp.concatenate([m[:, cols] for m in messages], axis=0).astype(F32) > 0
        gn_ref[:, cols] = jnp.where(live, dot(tt, gpool_ref[:, cols]), 0.0).astype(BF16)
    gn = gn_ref[...]
    for n in range(q_ref.shape[0] // step):
        cols = slice(n * step, (n + 1) * step)
        store(cols, dot(gn, q_ref[cols, :], 1, 1))


def back_far_kernel(block, place_ref, lists_ref, tt_ref, gpool_ref, msg_ref, q_ref, _, *refs):
    outs, gn_ref = refs[:-1], refs[-1]
    width = q_ref.shape[0]

    def store(cols, part):
        for i, out in enumerate(outs):
            out[:, cols] = part[i * block : (i + 1) * block].astype(BF16)

    for d, out in enumerate(outs, 2):
        mark_block(place_ref, lists_ref, d, out, width)
    back_dot((2 + LINE) * block, tt_ref, gpool_ref, [msg_ref[block:, :]], q_ref, gn_ref, store)


def back_own_kernel(block, lists_ref, tt_ref, gpool_ref, msg_ref, q_ref, _, same_ref, below_ref, gn_ref):
    same_ref[...] = jnp.zeros_like(same_ref)
    at = at_block(lists_ref[0, 1], block)

    def store(cols, part):
        same_ref[at, cols] = part[:block].astype(BF16)
        below_ref[:, cols] = part[block:].astype(BF16)

    back_dot(0, tt_ref, gpool_ref, [msg_ref[: 2 * block, :]], q_ref, gn_ref, store)


def own_rows_kernel(live_ref, g_ref, sw_ref, pre_ref, _, gself_ref, emb_ref):
    rows, width = pre_ref.shape
    step = 1024
    for n in range(width // step):
        cols = slice(n * step, (n + 1) * step)
        gself_ref[:, cols] = dot(g_ref[...], sw_ref[cols, :], 1, 1)
    act = jnp.maximum(pre_ref[...], 0.0)
    inv = lax.rsqrt(jnp.mean(act * act, axis=1, keepdims=True) + EPS)
    keep = lax.broadcasted_iota(jnp.int32, (rows, 1), 0) < live_ref[0]
    emb_ref[...] = jnp.where(keep, act * inv, 0.0).astype(BF16)


def sum_near_kernel(block, place_ref, lists_ref, m1, m2, m3, own_ref, d1, d2, d3, out_ref, total):
    total[...] = jnp.zeros_like(total)
    total[at_block(lists_ref[LINE, 1], block), :] = own_ref[...].astype(F32)
    for d, (meta, part) in enumerate(zip((m1, m2, m3), (d1, d2, d3)), 1):
        p = lax.rem(place_ref[0] + d, LINE)
        total[at_block(meta[0, near(p, d)], block), :] += part[...].astype(F32)
    out_ref[...] = total[...].astype(BF16)


def join_kernel(place_ref, mine_ref, sent_ref, out_ref):
    @pl.when(place_ref[0] == 0)
    def _():
        out_ref[...] = sent_ref[...]

    @pl.when(place_ref[0] > 0)
    def _():
        out_ref[...] = mine_ref[...]


def place_kernel(gself_ref, c1, c2, c3, total_ref):
    block, width = c1.shape[0], gself_ref.shape[1]
    first, second = gself_ref[:block, :], gself_ref[block:, :]
    for part in (c1, c2, c3):
        grad = part[:, :width].astype(F32)
        late = part[:, width : width + 1].astype(F32) > 0.5
        first += jnp.where(late, 0.0, grad)
        second += jnp.where(late, grad, 0.0)
    total_ref[:block, :] = first
    total_ref[block:, :] = second


def finish_kernel(live_ref, total_ref, same_ref, below_ref, out_ref):
    total = total_ref[...] + same_ref[...].astype(F32) + below_ref[...].astype(F32)
    keep = lax.broadcasted_iota(jnp.int32, (total.shape[0], 1), 0) < live_ref[0]
    out_ref[...] = jnp.where(keep, total, 0.0).astype(BF16)


def local(x, live, listed, counts, cotangent, q, qb, sw, nb, ob):
    x, lists, counts, up = x[0], listed[0, 0], counts[0], cotangent[0]
    live = live.reshape(1)
    rows, width = x.shape
    hidden = q.shape[1]
    reach, block_count = lists.shape
    block = rows // block_count
    qb, ob = qb[None], ob[None]
    place = (lax.axis_index("dom") % LINE).astype(jnp.int32).reshape(1)
    keep = lax.broadcasted_iota(jnp.int32, (rows, 1), 0) < live[0]
    marked = jnp.where(keep, x, jnp.asarray(DEAD, BF16))
    row = jnp.pad(lists[:, 1], (0, 128 - reach))[None]
    steps = range(1, LINE)
    one, two = ((block, width), BF16), ((rows, width), BF16)

    below = swap_rows(marked, LINE)
    same = swap_rows(marked, 0)
    metas = [along(row, -d) for d in steps]
    later, *metas = lax.optimization_barrier((marked, *metas))
    below2 = swap_rows(later, 2 * LINE)
    scalars = [SMEM] * (1 + len(steps))
    tiles, tiles_t, self_pre = call(
        lambda *r: tiles_kernel(block, *r),
        [((rows, reach * block), BF16), ((reach * block, rows), BF16), ((rows, width), F32)],
        (place, lists, counts, x, sw),
        [SMEM] * 2 + [VMEM] * 3,
        flops=2 * rows * width * width,
    )
    sent = call(
        lambda *r: pick_near_kernel(block, *r),
        [one] * len(steps),
        (place, *metas, below, tiles),
        scalars + [VMEM, HELD],
    )
    got_near = [along(b, d) for d, b in zip(steps, sent)]
    sent = call(
        lambda *r: pick_far_kernel(block, *r),
        [one] * len(steps),
        (place, *metas, same, below2),
        scalars + [VMEM] * 2,
    )
    got_far = [along(b, d) for d, b in zip(steps, sent)]
    split = 1 + LINE

    def message(first, last, ins, specs):
        size = last - first
        return call(
            lambda *r: message_kernel(block, first, last, *r),
            [((size * block, hidden), BF16), ((rows, hidden), F32), ((rows, 128), F32)],
            ins,
            specs,
            flops=2 * size * block * hidden * (width + rows),
        )

    msg_a, acc, deg = message(
        0, split, (lists, same, below, *got_near, q, qb, tiles), [SMEM] + [VMEM] * 8
    )
    g, gpool, pre, msg_b, *near_back, far_first = call(
        lambda *r: layer_kernel(block, *r),
        [two, ((rows, hidden), BF16), ((rows, width), F32), ((3 * block, hidden), BF16)] + [one] * 3 + [((block, width + 128), BF16)],
        (live, place, lists, *got_far, q, qb, tiles, acc, deg, self_pre, up, nb, ob, tiles_t, msg_a),
        [SMEM] * 3 + [VMEM] * 14,
        scratch=[pltpu.VMEM((rows, hidden), BF16), pltpu.VMEM((4 * block, hidden), BF16)],
        flops=8 * MICROSECOND,
    )
    back_near = [along(b, -d) for d, b in zip(steps, near_back)]
    far_back = call(
        lambda *r: back_far_kernel(block, *r),
        [((block, width + 128), BF16)] * 2,
        (place, lists, tiles_t, gpool, msg_b, q, near_back[0]),
        [SMEM] * 2 + [VMEM] * 4 + [HELD],
        scratch=[pltpu.VMEM((2 * block, hidden), BF16)],
        flops=2 * MICROSECOND,
    )
    (joined,) = call(
        join_kernel,
        [((block, width + 128), BF16)],
        (place, far_first, two_back(far_first)),
        [SMEM] + [VMEM] * 2,
    )
    back_far = [turn(joined)]
    back_far += [straight_back(b, d) for d, b in zip(steps[1:], far_back)]
    own_same, own_below = call(
        lambda *r: back_own_kernel(block, *r),
        [two, one],
        (lists, tiles_t, gpool, msg_a, q, far_back[0]),
        [SMEM] + [VMEM] * 4 + [HELD],
        scratch=[pltpu.VMEM((2 * block, hidden), BF16)],
        flops=2 * MICROSECOND,
    )
    g_same = swap_rows(own_same, 0)
    total = pltpu.VMEM((rows, width), F32)
    (sum_below,) = call(
        lambda *r: sum_near_kernel(block, *r),
        [two],
        (place, lists, *metas, own_below, *back_near),
        [SMEM] * 5 + [VMEM] * 4,
        scratch=[total],
        flops=20 * MICROSECOND,
    )
    g_below = swap_rows(sum_below, -LINE)
    gself, emb = call(
        own_rows_kernel,
        [((rows, width), F32), two],
        (live, g, sw, pre, sum_below),
        [SMEM] + [VMEM] * 3 + [HELD],
        flops=2 * MICROSECOND,
    )
    (placed,) = call(
        place_kernel,
        [((rows, width), F32)],
        (gself, *back_far),
        [VMEM] * 4,
        flops=20 * MICROSECOND,
    )
    (grad,) = call(finish_kernel, [two], (live, placed, g_same, g_below), [SMEM] + [VMEM] * 3)
    return emb[None], grad[None]


def solution(mesh):
    data = P("side", "dom", None)
    return jax.shard_map(
        local,
        mesh=mesh,
        in_specs=(
            data,
            P("side", "dom"),
            P("side", "dom", None, None),
            data,
            data,
            P(),
            P(),
            P(),
            P(),
            P(),
        ),
        out_specs=(data, data),
        check_vma=False,
    )
```
